32 devices in a mesh: batch: 8 (over z, y), head: 4 (over x, core).
Axes of the slice: x: 2, y: 2, z: 4, core: 2. Of those that a mesh axis runs over, the one named last changes fastest.
Arguments:
- inputs: bfloat16 [65536, 512], P(('batch', 'head')), may hold values from -6 to 6
- attn_gain: float32 [512], replicated, may hold values from 0.5 to 1.5
- query_weight: bfloat16 [512, 512], P(None, 'head'), may hold values from -0.25 to 0.25
- key_weight: bfloat16 [512, 512], P(None, 'head'), may hold values from -0.25 to 0.25
- value_weight: bfloat16 [512, 512], P(None, 'head'), may hold values from -0.25 to 0.25
- output_weight: bfloat16 [512, 512], P('head'), may hold values from -1 to 1
- ffn_gain: float32 [512], replicated, may hold values from 0.5 to 1.5
- controller: bfloat16 [512, 2], replicated, may hold values from -0.1875 to 0.1875
- expert_in: bfloat16 [2, 512, 2048], replicated, may hold values from -0.25 to 0.25
- expert_out: bfloat16 [2, 2048, 512], replicated, may hold values from -9 to 9
- group_ids: int32 [65536], P(('batch', 'head')), may hold values from 0 to 255, as said below
- live_mask: int32 [65536], P(('batch', 'head')), may hold values from 0 to 1, as said below
- cotangent: bfloat16 [65536, 512], P(('batch', 'head')), may hold values from -6 to 6
Outputs:
- layer_out: bfloat16 [65536, 512], P(('batch', 'head'))
- input_grad: float32 [65536, 512], P(('batch', 'head'))
- attn_gain_grad: float32 [512], replicated
- query_grad: float32 [512, 512], P(None, 'head')
- key_grad: float32 [512, 512], P(None, 'head')
- value_grad: float32 [512, 512], P(None, 'head')
- output_grad: float32 [512, 512], P('head')
- ffn_gain_grad: float32 [512], replicated
- controller_grad: float32 [512, 2], replicated
- expert_in_grad: float32 [2, 512, 2048], replicated
- expert_out_grad: float32 [2, 2048, 512], replicated
The draws below stay inside these ranges and needn't reach their ends.
Inputs may be any that keep to these rules, and one draw needn't show every extreme that they name: `group_ids`: within each aligned block of 2048 tokens (the tokens of one device) the ids count up from 0 by steps of 0 or 1; each group holds 8 to 64 tokens except the last of a block, which may hold fewer. `live_mask`: 1 except for a tail of the last group of each block; the first token of every group is 1.
All inputs are finite; a program needn't handle non-finite values.
Results may differ from the reference program's by a relative error of at most 0.017.
Values may be sent and summed in bfloat16 or wider, within the bound.
No kernel may reach another device: no remote copies, remote signals or barrier semaphores. Data moves between devices by JAX's collectives and lax.ppermute only.
A program may use at most 192 MiB of HBM per device.

```python
import jax
import jax.numpy as jnp
from jax import lax

D = 512
HEADS = 8
HD = 64
FF = 2048
EXPERTS = 2
LENGTH = 1024
SEQ_DEV = 8
TOK_DEV = 2048
TOKENS = 65536
N_HEAD = 4


def group_layout(key):
    blocks = TOKENS // TOK_DEV
    slots = TOK_DEV // 8
    size_key, wide_key, even_key, tail_key = jax.random.split(key, 4)
    sizes = jax.random.randint(size_key, (blocks, slots), 8, 65)
    widest = jax.random.randint(wide_key, (blocks, 1), 0, max(slots // 8, 1))
    column = jnp.arange(slots, dtype=jnp.int32)[None, :]
    sizes = jnp.where(column == widest, 64, sizes)
    even_block = jax.random.randint(even_key, (), 0, blocks)
    block_index = jnp.arange(blocks, dtype=jnp.int32)[:, None]
    sizes = jnp.where(block_index == even_block, 8, sizes)
    bounds = jnp.cumsum(sizes, axis=1)
    places = jnp.arange(TOK_DEV, dtype=jnp.int32)
    group_ids = jnp.sum((bounds[:, None, :] <= places[None, :, None]).astype(jnp.int32), axis=2)
    final_group = group_ids[:, -1:]
    first_final = jnp.sum((group_ids < final_group).astype(jnp.int32), axis=1, keepdims=True)
    final_size = TOK_DEV - first_final
    keeping = jax.random.randint(tail_key, (blocks, 1), 1, final_size + 1)
    live = (group_ids < final_group) | (places[None, :] - first_final < keeping)
    return (group_ids.reshape(TOKENS), live.astype(jnp.int32).reshape(TOKENS))


def draw_group_ids(key, part):
    layout = group_layout(key)
    return layout[0]


def draw_live_mask(key, part):
    layout = group_layout(key)
    return layout[1]


def levels(key, extent, pieces, least, high):
    level = 1.0
    for axis_at, blocks in pieces:
        steps = jax.random.uniform(jax.random.fold_in(jax.random.fold_in(key, 6), axis_at), (blocks,), jnp.float32, least / len(pieces), high / len(pieces))
        level = level * jnp.repeat(jnp.exp(steps), extent[axis_at] // blocks).reshape((-1,) + (1,) * (len(extent) - 1 - axis_at))
    return level


def scatter_about(stream_key, dims, deviation, reach, shards=(), kind=jnp.bfloat16):
    drawn = deviation * jax.random.normal(stream_key, dims, jnp.float32)
    if shards:
        drawn = drawn * levels(stream_key, dims, shards, -0.22, 0.18)
    return jnp.clip(drawn, -reach, reach).astype(kind)


def setup_inputs(seed: int = 0) -> dict:
    key_of = jax.random.split(jax.random.key(seed), 14)
    return {
        "inputs": scatter_about(key_of[0], (TOKENS, D), 1.0, 6.0, ((0, 32),)),
        "attn_gain": jnp.clip(1.0 + 0.1 * jax.random.normal(key_of[1], (D,), jnp.float32), 0.5, 1.5),
        "query_weight": scatter_about(key_of[2], (D, HEADS * HD), D ** -0.5, 0.25, ((1, 4),)),
        "key_weight": scatter_about(key_of[3], (D, HEADS * HD), D ** -0.5, 0.25, ((1, 4),)),
        "value_weight": scatter_about(key_of[4], (D, HEADS * HD), D ** -0.5, 0.25, ((1, 4),)),
        "output_weight": scatter_about(key_of[5], (HEADS * HD, D), (HEADS * HD // 16) ** -0.5, 1.0, ((0, 4),)),
        "ffn_gain": jnp.clip(1.0 + 0.1 * jax.random.normal(key_of[6], (D,), jnp.float32), 0.5, 1.5),
        "controller": scatter_about(key_of[7], (D, EXPERTS), (2 * D) ** -0.5, 0.1875),
        "expert_in": scatter_about(key_of[8], (EXPERTS, D, FF), D ** -0.5, 0.25),
        "expert_out": scatter_about(key_of[9], (EXPERTS, FF, D), 1.5, 9.0),
        "group_ids": draw_group_ids(jax.random.fold_in(key_of[13], 71), 0),
        "live_mask": draw_live_mask(jax.random.fold_in(key_of[13], 71), 0),
        "cotangent": scatter_about(key_of[12], (TOKENS, D), 1.0, 6.0, ((0, 32),)),
    }


@jax.custom_vjp
def low(v):
    return lax.optimization_barrier(v.astype(jnp.bfloat16)).astype(jnp.float32)

@jax.custom_vjp
def low_back(v):
    return v

def low_keep(v):
    return (low(v), None)

def low_pass(kept, grad):
    return (grad,)

def back_keep(v):
    return (v, None)

def back_low(kept, grad):
    return (low(grad),)
low.defvjp(low_keep, low_pass)
low_back.defvjp(back_keep, back_low)
highest = lax.Precision.HIGHEST
eps = 1e-06

def hdot(left, right):
    return jnp.dot(left, right, precision=highest, preferred_element_type=jnp.float32)

def rms_norm(vector, gain):
    return vector * lax.rsqrt(lax.optimization_barrier(jnp.mean(vector * vector, axis=-1, keepdims=True)) + eps) * gain

def attend_head(query, keys, values):
    scores = jnp.einsum('sqd,skd->sqk', query, keys, precision=highest) * HD ** (-0.5)
    scores = low_back(scores)
    places = jnp.arange(LENGTH, dtype=jnp.int32)
    causal = places[None, :] <= places[:, None]
    scores = jnp.where(causal[None], scores, -1e+30)
    probs = low(jax.nn.softmax(scores, axis=-1))
    return jnp.einsum('sqk,skd->sqd', probs, values, precision=highest)

def mix_block(normed_blk, logit_blk, ids_blk, live_blk, expert_in, expert_out):
    slots = TOK_DEV // 8
    live_float = live_blk.astype(jnp.float32)
    onehot = (ids_blk[:, None] == jnp.arange(slots, dtype=jnp.int32)[None, :]).astype(jnp.float32) * live_float[:, None]
    expo = jnp.exp(logit_blk) * live_float[:, None]
    totals = hdot(onehot.T, expo)
    per_token = hdot(onehot, totals) + (1.0 - live_float)[:, None]
    weights = low(expo / per_token)
    assign = onehot[None, :, :] * weights.T[:, :, None]
    mixed = low_back(low(jnp.einsum('etg,td->egd', assign, normed_blk, precision=highest)))
    before = low_back(jnp.einsum('egd,edf->egf', mixed, expert_in, precision=highest))
    active = low(jax.nn.gelu(before, approximate=True))
    result = low_back(low(jnp.einsum('egf,efd->egd', active, expert_out, precision=highest)))
    return jnp.einsum('etg,egd->td', assign, result, precision=highest)

def layer(rows_in, attn_gain, query_weight, key_weight, value_weight, output_weight, ffn_gain, controller, expert_in, expert_out, ids_rows, live_rows):
    normed = low(rms_norm(rows_in, attn_gain))

    def project(weight):
        flat = low_back(low(hdot(normed, weight)))
        return flat.reshape(SEQ_DEV, LENGTH, HEADS, HD).transpose(2, 0, 1, 3)
    checked = jax.checkpoint(attend_head)
    heads_out = lax.map(lambda bundle: checked(bundle[0], bundle[1], bundle[2]), (project(query_weight), project(key_weight), project(value_weight)))
    context = heads_out.transpose(1, 2, 0, 3).reshape(SEQ_DEV * LENGTH, HEADS * HD)
    context = low_back(low(context))
    middle = rows_in + low_back(hdot(context, output_weight))
    normed2 = low(rms_norm(middle, ffn_gain))
    logits = hdot(normed2, controller)
    mixture = jax.vmap(mix_block, in_axes=(0, 0, 0, 0, None, None))(normed2.reshape(N_HEAD, TOK_DEV, D), logits.reshape(N_HEAD, TOK_DEV, EXPERTS), ids_rows.reshape(N_HEAD, TOK_DEV), live_rows.reshape(N_HEAD, TOK_DEV), expert_in, expert_out)
    return middle + mixture.reshape(SEQ_DEV * LENGTH, D)

def reference(inputs, attn_gain, query_weight, key_weight, value_weight, output_weight, ffn_gain, controller, expert_in, expert_out, group_ids, live_mask, cotangent):
    params = tuple((item.astype(jnp.float32) for item in (attn_gain, query_weight, key_weight, value_weight, output_weight, ffn_gain, controller, expert_in, expert_out)))
    stretch = SEQ_DEV * LENGTH
    groups_count = inputs.shape[0] // stretch
    rows_all = inputs.astype(jnp.float32).reshape(groups_count, stretch, D)
    cot_all = cotangent.astype(jnp.float32).reshape(groups_count, stretch, D)
    ids_all = group_ids.reshape(groups_count, stretch)
    live_all = live_mask.reshape(groups_count, stretch)

    def advance(totals, bundle):
        rows_in, ids_rows, live_rows, cot_rows = bundle

        def forward(rows_arg, *weights):
            return layer(rows_arg, *weights, ids_rows, live_rows)
        produced, pull = jax.vjp(forward, rows_in, *params)
        grads = pull(cot_rows)
        totals = tuple((first + second for first, second in zip(totals, grads[1:])))
        return (totals, (produced.astype(jnp.bfloat16), grads[0]))
    zeros = tuple((jnp.zeros(item.shape, jnp.float32) for item in params))
    totals, (outputs, input_grads) = lax.scan(advance, zeros, (rows_all, ids_all, live_all, cot_all))
    return (outputs.reshape(-1, D), input_grads.reshape(-1, D), totals[0], totals[1], totals[2], totals[3], totals[4], totals[5], totals[6], totals[7], totals[8])
```

```python
import functools

import jax
import jax.numpy as jnp
from jax import lax
from jax.experimental import pallas as pl
from jax.experimental.pallas import tpu as pltpu
from jax.sharding import PartitionSpec as P

HD = 64
LENGTH = 1024
WIDTH = 128
BF = jnp.bfloat16
F32 = jnp.float32
LOG2E = 1.4426950408889634
LN2 = 0.6931471805599453
VMEM = 56 * 2**20

eps = 1e-06
highest = lax.Precision.HIGHEST
last_dims = (((1,), (1,)), ((), ()))
first_dims = (((0,), (0,)), ((), ()))


def dot(left, right):
    return jnp.dot(left, right, preferred_element_type=F32)


def dot_last(left, right):
    return lax.dot_general(left, right, last_dims, preferred_element_type=F32)


def dot_first(left, right):
    return lax.dot_general(left, right, first_dims, preferred_element_type=F32)


def split3(value):
    high = value.astype(BF)
    rest = value - high.astype(F32)
    mid = rest.astype(BF)
    low = (rest - mid.astype(F32)).astype(BF)
    return high, mid, low


def call(body, name, grid, in_specs, out_specs, out_shape, flops, moved, exps=0, **extra):
    return pl.pallas_call(
        body,
        grid=grid,
        in_specs=in_specs,
        out_specs=out_specs,
        out_shape=out_shape,
        compiler_params=pltpu.CompilerParams(vmem_limit_bytes=VMEM),
        cost_estimate=pl.CostEstimate(
            flops=int(flops), bytes_accessed=int(moved), transcendentals=int(exps)
        ),
        name=name,
        **extra,
    )


def row_block(columns):
    return pl.BlockSpec((LENGTH, columns), lambda s: (s, 0))


def whole(*shape):
    return pl.BlockSpec(shape, lambda s: (0,) * len(shape))


def head_lanes(rows, head):
    lane = lax.broadcasted_iota(jnp.int32, (rows, WIDTH), 1)
    mine = (lane < HD) if head == 0 else (lane >= HD)
    return lane, mine, HD if head == 0 else 0


def with_extra(mine, lane, other, values, extra):
    high, mid, low = split3(extra)
    filler = jnp.zeros_like(values)
    for place, part in ((2, low), (1, mid), (0, high)):
        filler = jnp.where(lane == other + place, part, filler)
    return jnp.where(mine, values, filler)


def attend_slot(normed, weight, slot, qa_ref, k_ref, v_ref, ctx_ref):
    block = 256
    qkv = dot(normed, weight)
    q = (qkv[:, :WIDTH] * (HD**-0.5 * LOG2E)).astype(BF)
    k = qkv[:, WIDTH : 2 * WIDTH].astype(BF)
    v = qkv[:, 2 * WIDTH :].astype(BF)
    k_ref[slot] = k
    v_ref[slot] = v
    for head in range(2):
        lane, mine, other = head_lanes(LENGTH, head)
        qh = jnp.where(mine, q, jnp.zeros_like(q))
        vh = jnp.where(mine, v, (lane == other).astype(F32).astype(BF))
        q_long = qh.astype(F32)
        k_long = jnp.where(mine, k, jnp.zeros_like(k)).astype(F32)
        bound = jnp.max(jnp.sum(q_long * q_long, axis=1, keepdims=True)) * jnp.max(
            jnp.sum(k_long * k_long, axis=1, keepdims=True)
        )

        def rows_of(small):
            lane_b, mine_b, _ = head_lanes(block, head)
            for start in range(0, LENGTH, block):
                here = slice(start, start + block)
                queries = qh[here]
                scores = []
                for at in range(0, start + block, block):
                    part = dot_last(queries, k[at : at + block])
                    if at == start:
                        r = lax.broadcasted_iota(jnp.int32, (block, block), 0)
                        c = lax.broadcasted_iota(jnp.int32, (block, block), 1)
                        part = jnp.where(c <= r, part, -1e30)
                    scores.append(part)
                if not small:
                    peak = functools.reduce(
                        jnp.maximum, [jnp.max(part, axis=1, keepdims=True) for part in scores]
                    )
                    scores = [part - peak for part in scores]
                out = 0.0
                for index, part in enumerate(scores):
                    out = out + dot(
                        jnp.exp2(part).astype(BF), vh[index * block : (index + 1) * block]
                    )
                total = out[:, other : other + 1]
                logsum = jnp.log2(total)
                if not small:
                    logsum = logsum + peak
                context = (out * (1.0 / total)).astype(BF)
                qa_ref[slot, head, here] = with_extra(mine_b, lane_b, other, queries, logsum)
                if head == 1:
                    context = jnp.where(mine_b, context, ctx_ref[slot, here])
                ctx_ref[slot, here] = context

        small = bound < 1e4

        @pl.when(small)
        def _():
            rows_of(True)

        @pl.when(jnp.logical_not(small))
        def _():
            rows_of(False)


def norm_rows(rows):
    return rows * lax.rsqrt(jnp.mean(rows * rows, axis=-1, keepdims=True) + eps)


def forward_first(x_ref, gain_ref, *refs):
    slots = len(refs) - 5
    normed_ref, qa_ref, k_ref, v_ref, ctx_ref = refs[slots:]
    normed = (norm_rows(x_ref[...].astype(F32)) * gain_ref[...]).astype(BF)
    normed_ref[...] = normed
    for slot in range(slots):
        attend_slot(normed, refs[slot][...], slot, qa_ref, k_ref, v_ref, ctx_ref)


def forward_last(normed_ref, x_ref, ctx_in_ref, wo_ref, *refs):
    slots = len(refs) - 5
    qa_ref, k_ref, v_ref, ctx_ref, middle_ref = refs[slots:]
    normed = normed_ref[...]
    for slot in range(slots):
        attend_slot(normed, refs[slot][...], slot, qa_ref, k_ref, v_ref, ctx_ref)
    before = ctx_in_ref.shape[0]
    context = jnp.concatenate(
        [ctx_in_ref[i] for i in range(before)] + [ctx_ref[i] for i in range(slots)], axis=1
    )
    middle_ref[...] = x_ref[...].astype(F32) + dot(context, wo_ref[...])


def slot_outputs(slots, tokens):
    per = pl.BlockSpec((slots, LENGTH, WIDTH), lambda s: (0, s, 0))
    specs = [pl.BlockSpec((slots, 2, LENGTH, WIDTH), lambda s: (0, 0, s, 0)), per, per, per]
    flat = jax.ShapeDtypeStruct((slots, tokens, WIDTH), BF)
    shapes = [jax.ShapeDtypeStruct((slots, 2, tokens, WIDTH), BF), flat, flat, flat]
    return specs, shapes


def run_forward_first(x, gain, weights):
    tokens, width = x.shape
    specs, shapes = slot_outputs(len(weights), tokens)
    return call(
        forward_first,
        "attention_forward_first",
        (tokens // LENGTH,),
        [row_block(width), whole(1, width)] + [whole(width, 3 * WIDTH)] * len(weights),
        [row_block(width)] + specs,
        [jax.ShapeDtypeStruct((tokens, width), BF)] + shapes,
        1.5e10,
        1e7,
        1e7,
    )(x, gain, *weights)


def run_forward_last(normed, x, ctx, wo, weights):
    tokens, width = x.shape
    specs, shapes = slot_outputs(len(weights), tokens)
    ctx_spec = pl.BlockSpec((ctx.shape[0], LENGTH, WIDTH), lambda s: (0, s, 0))
    return call(
        forward_last,
        "attention_forward_last",
        (tokens // LENGTH,),
        [row_block(width), row_block(width), ctx_spec, whole(*wo.shape)]
        + [whole(width, 3 * WIDTH)] * len(weights),
        specs + [row_block(width)],
        shapes + [jax.ShapeDtypeStruct((tokens, width), F32)],
        1.5e10,
        1e7,
        1e7,
    )(normed, x, ctx, wo, *weights)


def backward_slot(
    qa_ref, k_ref, v_ref, ctx_ref, ml_ref, wo_ref, normed_ref, dqkv_ref, dw_ref, dwo_ref
):
    block = 512
    ml = ml_ref[...]
    ctx = ctx_ref[0]
    d_out = dot_last(ml, wo_ref[...]).astype(BF)
    product = d_out.astype(F32) * ctx.astype(F32)
    k = k_ref[0]
    v = v_ref[0]
    k_flip = k.T
    dks, dvs, dqs = [], [], []
    for head in range(2):
        lane, mine, other = head_lanes(LENGTH, head)
        minus = jnp.where((lane >= other) & (lane < other + 3), -1.0, 0.0).astype(BF)
        central = jnp.sum(jnp.where(mine, product, 0.0), axis=1, keepdims=True)
        d_all = with_extra(mine, lane, other, d_out, central)
        k_all = jnp.where(mine, k, minus)
        v_all = jnp.where(mine, v, minus)
        q_all = qa_ref[0, head]
        dq = [0.0] * (LENGTH // block)
        dk, dv = [], []
        for at in range(0, LENGTH, block):
            keys = k_all[at : at + block]
            values = v_all[at : at + block]
            flipped = k_flip[head * HD : (head + 1) * HD, at : at + block]
            dk_here = 0.0
            dv_here = 0.0
            for start in range(at, LENGTH, block):
                queries = q_all[start : start + block]
                d_rows = d_all[start : start + block]
                probs = jnp.exp2(dot_last(keys, queries))
                if start == at:
                    r = lax.broadcasted_iota(jnp.int32, (block, block), 0)
                    c = lax.broadcasted_iota(jnp.int32, (block, block), 1)
                    probs = jnp.where(r <= c, probs, 0.0)
                d_scores = (probs * dot_last(values, d_rows)).astype(BF)
                dv_here = dv_here + dot(probs.astype(BF), d_rows)
                dk_here = dk_here + dot(d_scores, queries)
                dq[start // block] = dq[start // block] + dot(flipped, d_scores)
            dk.append(dk_here)
            dv.append(dv_here)
        dks.append(jnp.concatenate(dk, axis=0))
        dvs.append(jnp.concatenate(dv, axis=0))
        dqs.append(jnp.concatenate(dq, axis=1))
    lane, mine, _ = head_lanes(LENGTH, 0)
    dk = (jnp.where(mine, dks[0], dks[1]) * LN2).astype(BF)
    dv = jnp.where(mine, dvs[0], dvs[1]).astype(BF)
    dq_flip = (jnp.concatenate(dqs, axis=0) * HD**-0.5).astype(BF)
    dqkv_ref[:, :WIDTH] = dq_flip.T
    dqkv_ref[:, WIDTH : 2 * WIDTH] = dk
    dqkv_ref[:, 2 * WIDTH :] = dv
    dw = dot(jnp.concatenate([dq_flip, dk.T, dv.T], axis=0), normed_ref[...])
    dwo = dot_first(ctx, ml)
    first = pl.program_id(0) == 0

    @pl.when(first)
    def _():
        dw_ref[...] = dw
        dwo_ref[...] = dwo

    @pl.when(jnp.logical_not(first))
    def _():
        dw_ref[...] += dw
        dwo_ref[...] += dwo


def run_backward(saved, index, ml, wo, normed):
    qa, k, v, ctx = saved
    tokens, width = ml.shape
    per = pl.BlockSpec((1, LENGTH, WIDTH), lambda s: (index, s, 0))
    return call(
        backward_slot,
        "attention_backward",
        (tokens // LENGTH,),
        [
            pl.BlockSpec((1, 2, LENGTH, WIDTH), lambda s: (index, 0, s, 0)),
            per,
            per,
            per,
            row_block(width),
            whole(WIDTH, width),
            row_block(width),
        ],
        [row_block(3 * WIDTH), whole(3 * WIDTH, width), whole(WIDTH, width)],
        [
            jax.ShapeDtypeStruct((tokens, 3 * WIDTH), BF),
            jax.ShapeDtypeStruct((3 * WIDTH, width), F32),
            jax.ShapeDtypeStruct((WIDTH, width), F32),
        ],
        1.5e10,
        1e7,
        1e7,
    )(qa, k, v, ctx, ml, wo, normed)


def rms_norm(vector, gain):
    return norm_rows(vector) * gain


def gelu_tanh(vector):
    return jax.nn.gelu(vector, approximate=True)


def build(mesh):
    n_head, n_batch = mesh.shape["head"], mesh.shape["batch"]
    head_bits = [1 << i for i in range(n_head.bit_length() - 1)]
    batch_bits = [1 << i for i in range(n_batch.bit_length() - 1)]

    def swap(value, axis, bit):
        size = mesh.shape[axis]
        return lax.ppermute(value, axis, [(i, i ^ bit) for i in range(size)])

    def bit_of(axis, bit):
        return (lax.axis_index(axis) // bit) % 2

    def halve(value, axis, bit):
        half = value.shape[0] // 2
        side = bit_of(axis, bit)
        sent = lax.dynamic_slice_in_dim(value, (1 - side) * half, half, 0)
        kept = lax.dynamic_slice_in_dim(value, side * half, half, 0)
        got = swap(sent, axis, bit)
        return (kept.astype(F32) + got.astype(F32)).astype(BF)

    def join(value, axis, bit):
        side = bit_of(axis, bit)
        got = swap(value, axis, bit)
        return jnp.where(
            side == 0,
            jnp.concatenate([value, got], axis=0),
            jnp.concatenate([got, value], axis=0),
        )

    def sum_everywhere(value, order):
        for axis, bit in order:
            value = halve(value, axis, bit)
        for axis, bit in order[::-1]:
            value = join(value, axis, bit)
        return value

    def sum_small(value, order):
        for axis, bit in order:
            value = value + swap(value, axis, bit)
        return value

    across = [("head", bit) for bit in head_bits[1:]] + [("batch", bit) for bit in batch_bits]
    everywhere = [("head", bit) for bit in head_bits] + [("batch", bit) for bit in batch_bits]

    def local(
        inputs,
        attn_gain,
        query_weight,
        key_weight,
        value_weight,
        output_weight,
        ffn_gain,
        controller,
        expert_in,
        expert_out,
        group_ids,
        live_mask,
        cotangent,
    ):
        tokens_here, width = inputs.shape
        pair = head_bits[0]
        w0 = jnp.concatenate([query_weight, key_weight, value_weight], axis=1)
        w1 = swap(w0, "head", 1)
        w2 = swap(w0, "head", 2)
        w3 = swap(w2, "head", 1)
        o0 = output_weight
        o1 = swap(o0, "head", 1)
        o2 = swap(o0, "head", 2)
        o3 = swap(o2, "head", 1)
        weights = [w0, w1, w2, w3]
        outs = [o0, o1, o2, o3]
        wo = jnp.concatenate(outs, axis=0)
        normed, *saved_a = run_forward_first(inputs, attn_gain[None], weights[:2])
        *saved_b, middle = run_forward_last(normed, inputs, saved_a[3], wo, weights[2:])

        normed2 = rms_norm(middle, ffn_gain).astype(BF)
        logits = jnp.dot(normed2, controller, preferred_element_type=F32)
        slots = tokens_here // 8
        live_float = live_mask.astype(F32)
        onehot = (group_ids[:, None] == lax.iota(jnp.int32, slots)[None, :]).astype(
            F32
        ) * live_float[:, None]

        def group_softmax(logit_rows):
            expo = jnp.exp(logit_rows) * live_float[:, None]
            totals = jnp.dot(onehot.T, expo, precision=highest)
            return expo / (
                jnp.dot(onehot, totals, precision=highest) + (1.0 - live_float)[:, None]
            )

        mixes, softmax_back = jax.vjp(group_softmax, logits)
        assign = onehot.astype(BF)[None, :, :] * mixes.astype(BF).T[:, :, None]
        mixed = jnp.einsum("etg,td->egd", assign, normed2, preferred_element_type=F32).astype(BF)
        result_grad = jnp.einsum(
            "etg,td->egd", assign, cotangent, preferred_element_type=F32
        ).astype(BF)

        mine = bit_of("head", pair)

        def trade(values):
            kept = lax.dynamic_index_in_dim(values, mine, 0, keepdims=False)
            sent = lax.dynamic_index_in_dim(values, 1 - mine, 0, keepdims=False)
            return jnp.concatenate([kept, swap(sent, "head", pair)], axis=0)

        def trade_back(values):
            kept, sent = values[:slots], values[slots:]
            got = swap(sent, "head", pair)
            return jnp.where(mine == 0, jnp.stack([kept, got]), jnp.stack([got, kept]))

        e_in = lax.dynamic_index_in_dim(expert_in, mine, 0, keepdims=False)
        e_out = lax.dynamic_index_in_dim(expert_out, mine, 0, keepdims=False)
        mixed_two = trade(mixed)
        result_grad_two = trade(result_grad)
        before = dot(mixed_two, e_in)
        active = gelu_tanh(before).astype(BF)
        result = trade_back(dot(active, e_out).astype(BF))
        expert_out_part = dot_first(active, result_grad_two).astype(BF)
        active_grad = dot_last(result_grad_two, e_out)
        before_grad = jax.vjp(gelu_tanh, before)[1](active_grad)[0].astype(BF)
        mixed_grad = trade_back(dot_last(before_grad, e_in).astype(BF))
        expert_in_part = dot_first(mixed_two, before_grad).astype(BF)

        mixture = jnp.einsum("etg,egd->td", assign, result, preferred_element_type=F32)
        layer_out = (middle + mixture).astype(BF)
        assign_grad = jnp.einsum("td,egd->etg", cotangent, result, preferred_element_type=F32)
        assign_grad = assign_grad + jnp.einsum(
            "td,egd->etg", normed2, mixed_grad, preferred_element_type=F32
        )
        normed2_grad = jnp.einsum("etg,egd->td", assign, mixed_grad, preferred_element_type=F32)
        weight_grad = jnp.sum(assign_grad * onehot[None, :, :], axis=-1).T
        logit_grad = softmax_back(weight_grad)[0]
        controller_grad = jnp.dot(normed2.astype(F32).T, logit_grad, precision=highest)
        normed2_grad = normed2_grad + jnp.dot(
            logit_grad, controller.astype(F32).T, precision=highest
        )
        middle_grad, ffn_gain_grad = jax.vjp(rms_norm, middle, ffn_gain)[1](normed2_grad)
        middle_grad = cotangent.astype(F32) + middle_grad
        middle_low = middle_grad.astype(BF)

        quarter = expert_in_part.shape[1] // 4
        payload = [
            jnp.concatenate(
                [expert_in_part[:, i * quarter : (i + 1) * quarter] for i in range(4)], axis=0
            ),
            expert_out_part,
        ]
        payload = jnp.concatenate(payload, axis=0)
        unit = payload.shape[0] // 16
        cuts = [0, 6 * unit, 11 * unit, 16 * unit]
        turned = [
            across,
            across[1:] + across[:1],
            across[2:3] + across[:2] + across[3:],
        ]
        summed = [
            sum_everywhere(payload[low:high], order)
            for low, high, order in zip(cuts[:-1], cuts[1:], turned)
        ]

        grads = [None] * 4
        flats = [None] * 4

        def backward(slot):
            saved, index = (saved_a, slot) if slot < 2 else (saved_b, slot - 2)
            flats[slot], dw, dwo = run_backward(saved, index, middle_low, outs[slot], normed)
            return jnp.concatenate([dw, dwo], axis=0)

        third = backward(3)
        third_got = swap(third.astype(BF), "head", 1)
        second = backward(2) + third_got.astype(F32)
        second_got = swap(second.astype(BF), "head", 2)
        first = backward(1)
        first_got = swap(first.astype(BF), "head", 1)
        own = backward(0) + second_got.astype(F32) + first_got.astype(F32)
        own = own.astype(BF)
        weight_sum = sum_everywhere(own, [("batch", bit) for bit in batch_bits]).astype(F32)
        query_grad = weight_sum[:WIDTH].T
        key_grad = weight_sum[WIDTH : 2 * WIDTH].T
        value_grad = weight_sum[2 * WIDTH : 3 * WIDTH].T
        output_grad = weight_sum[3 * WIDTH :]

        normed_grad = dot_last(
            jnp.concatenate(flats, axis=1), jnp.concatenate(weights, axis=1)
        )
        rows_in = inputs.astype(F32)
        rows_grad, attn_gain_grad = jax.vjp(rms_norm, rows_in, attn_gain)[1](normed_grad)
        input_grad = middle_grad + rows_grad

        small = jnp.concatenate([ffn_gain_grad[None], controller_grad.T], axis=0)
        small = sum_small(small, everywhere)
        attn_gain_grad = sum_small(attn_gain_grad[None], everywhere)[0]

        total = jnp.concatenate(summed, axis=0)
        other = swap(total, "head", pair)
        both = jnp.where(mine == 0, jnp.stack([total, other]), jnp.stack([other, total]))
        split = payload.shape[0] // 2
        expert_in_grad = (
            both[:, :split]
            .reshape(2, 4, width, quarter)
            .transpose(0, 2, 1, 3)
            .reshape(2, width, 4 * quarter)
            .astype(F32)
        )
        expert_out_grad = both[:, split:].astype(F32)
        return (
            layer_out,
            input_grad,
            attn_gain_grad,
            query_grad,
            key_grad,
            value_grad,
            output_grad,
            small[0],
            small[1:].T,
            expert_in_grad,
            expert_out_grad,
        )

    return local


def solution(mesh):
    in_specs = (
        P(("batch", "head"), None),
        P(),
        P(None, "head"),
        P(None, "head"),
        P(None, "head"),
        P("head", None),
        P(),
        P(),
        P(),
        P(),
        P(("batch", "head")),
        P(("batch", "head")),
        P(("batch", "head"), None),
    )
    out_specs = (
        P(("batch", "head"), None),
        P(("batch", "head"), None),
        P(),
        P(None, "head"),
        P(None, "head"),
        P(None, "head"),
        P("head", None),
        P(),
        P(),
        P(),
        P(),
    )
    return jax.shard_map(
        build(mesh), mesh=mesh, in_specs=in_specs, out_specs=out_specs, check_vma=False
    )
```

```python
import functools

import jax
import jax.numpy as jnp
from jax import lax
from jax.experimental import pallas as pl
from jax.experimental.pallas import tpu as pltpu
from jax.sharding import PartitionSpec as P

HD = 64
LENGTH = 1024
WIDTH = 128
BF = jnp.bfloat16
F32 = jnp.float32
LOG2E = 1.4426950408889634
LN2 = 0.6931471805599453
VMEM = 56 * 2**20

eps = 1e-06
last_dims = (((1,), (1,)), ((), ()))
first_dims = (((0,), (0,)), ((), ()))


def dot(left, right):
    return jnp.dot(left, right, preferred_element_type=F32)


def dot_last(left, right):
    return lax.dot_general(left, right, last_dims, preferred_element_type=F32)


def dot_first(left, right):
    return lax.dot_general(left, right, first_dims, preferred_element_type=F32)


def split3(value):
    high = value.astype(BF)
    rest = value - high.astype(F32)
    mid = rest.astype(BF)
    low = (rest - mid.astype(F32)).astype(BF)
    return high, mid, low


def call(body, name, grid, in_specs, out_specs, out_shape, flops, moved, exps=0, **extra):
    return pl.pallas_call(
        body,
        grid=grid,
        in_specs=in_specs,
        out_specs=out_specs,
        out_shape=out_shape,
        compiler_params=pltpu.CompilerParams(vmem_limit_bytes=VMEM),
        cost_estimate=pl.CostEstimate(
            flops=int(flops), bytes_accessed=int(moved), transcendentals=int(exps)
        ),
        name=name,
        **extra,
    )


def row_block(columns):
    return pl.BlockSpec((LENGTH, columns), lambda s: (s, 0))


def whole(*shape):
    return pl.BlockSpec(shape, lambda s: (0,) * len(shape))


def head_lanes(rows, head):
    lane = lax.broadcasted_iota(jnp.int32, (rows, WIDTH), 1)
    mine = (lane < HD) if head == 0 else (lane >= HD)
    return lane, mine, HD if head == 0 else 0


def with_extra(mine, lane, other, values, extra):
    high, mid, low = split3(extra)
    filler = jnp.zeros_like(values)
    for place, part in ((2, low), (1, mid), (0, high)):
        filler = jnp.where(lane == other + place, part, filler)
    return jnp.where(mine, values, filler)


def attend_slot(normed, weight, slot, qa_ref, k_ref, v_ref, ctx_ref):
    block = 256
    qkv = dot(normed, weight)
    q = (qkv[:, :WIDTH] * (HD**-0.5 * LOG2E)).astype(BF)
    k = qkv[:, WIDTH : 2 * WIDTH].astype(BF)
    v = qkv[:, 2 * WIDTH :].astype(BF)
    k_ref[slot] = k
    v_ref[slot] = v
    for head in range(2):
        lane, mine, other = head_lanes(LENGTH, head)
        qh = jnp.where(mine, q, jnp.zeros_like(q))
        vh = jnp.where(mine, v, (lane == other).astype(F32).astype(BF))
        q_long = qh.astype(F32)
        k_long = jnp.where(mine, k, jnp.zeros_like(k)).astype(F32)
        bound = jnp.max(jnp.sum(q_long * q_long, axis=1, keepdims=True)) * jnp.max(
            jnp.sum(k_long * k_long, axis=1, keepdims=True)
        )

        def rows_of(small):
            lane_b, mine_b, _ = head_lanes(block, head)
            for start in range(0, LENGTH, block):
                here = slice(start, start + block)
                queries = qh[here]
                scores = []
                for at in range(0, start + block, block):
                    part = dot_last(queries, k[at : at + block])
                    if at == start:
                        r = lax.broadcasted_iota(jnp.int32, (block, block), 0)
                        c = lax.broadcasted_iota(jnp.int32, (block, block), 1)
                        part = jnp.where(c <= r, part, -1e30)
                    scores.append(part)
                if not small:
                    peak = functools.reduce(
                        jnp.maximum, [jnp.max(part, axis=1, keepdims=True) for part in scores]
                    )
                    scores = [part - peak for part in scores]
                out = 0.0
                for index, part in enumerate(scores):
                    out = out + dot(
                        jnp.exp2(part).astype(BF), vh[index * block : (index + 1) * block]
                    )
                total = out[:, other : other + 1]
                logsum = jnp.log2(total)
                if not small:
                    logsum = logsum + peak
                context = (out * (1.0 / total)).astype(BF)
                qa_ref[slot, head, here] = with_extra(mine_b, lane_b, other, queries, logsum)
                if head == 1:
                    context = jnp.where(mine_b, context, ctx_ref[slot, here])
                ctx_ref[slot, here] = context

        small = bound < 1e4

        @pl.when(small)
        def _():
            rows_of(True)

        @pl.when(jnp.logical_not(small))
        def _():
            rows_of(False)


def norm_rows(rows):
    return rows * lax.rsqrt(jnp.mean(rows * rows, axis=-1, keepdims=True) + eps)


def pack_weights(q_ref, k_ref, v_ref, o_ref, packed_ref):
    for index, ref in enumerate((q_ref, k_ref, v_ref)):
        packed_ref[:, index * WIDTH : (index + 1) * WIDTH] = ref[...]
    packed_ref[:, 3 * WIDTH :] = o_ref[...].T


def run_pack(q, k, v, o):
    width = q.shape[0]
    return call(
        pack_weights,
        "pack_weights",
        (),
        [pl.BlockSpec(memory_space=pltpu.VMEM)] * 4,
        pl.BlockSpec(memory_space=pltpu.VMEM),
        jax.ShapeDtypeStruct((width, 4 * WIDTH), BF),
        1e6,
        2e6,
    )(q, k, v, o)


def forward_first(x_ref, gain_ref, *refs):
    slots = len(refs) - 5
    normed_ref, qa_ref, k_ref, v_ref, ctx_ref = refs[slots:]
    normed = (norm_rows(x_ref[...].astype(F32)) * gain_ref[...]).astype(BF)
    normed_ref[...] = normed
    for slot in range(slots):
        weight = refs[slot][:, : 3 * WIDTH]
        attend_slot(normed, weight, slot, qa_ref, k_ref, v_ref, ctx_ref)


def forward_last(normed_ref, x_ref, ctx_in_ref, ffn_gain_ref, control_ref, *refs):
    slots = len(refs) - 7
    weights = refs[:slots]
    qa_ref, k_ref, v_ref, ctx_ref, middle_ref, normed2_ref, logits_ref = refs[slots:]
    normed = normed_ref[...]
    before = ctx_in_ref.shape[0]
    for slot in range(slots - before):
        weight = weights[before + slot][:, : 3 * WIDTH]
        attend_slot(normed, weight, slot, qa_ref, k_ref, v_ref, ctx_ref)
    context = jnp.concatenate(
        [ctx_in_ref[i] for i in range(before)] + [ctx_ref[i] for i in range(slots - before)],
        axis=1,
    )
    flipped = jnp.concatenate([ref[:, 3 * WIDTH :] for ref in weights], axis=1)
    middle = x_ref[...].astype(F32) + dot_last(context, flipped)
    middle_ref[...] = middle
    normed2 = (norm_rows(middle) * ffn_gain_ref[...]).astype(BF)
    normed2_ref[...] = normed2
    logits_ref[...] = dot(normed2, control_ref[...])


def slot_outputs(slots, tokens):
    per = pl.BlockSpec((slots, LENGTH, WIDTH), lambda s: (0, s, 0))
    specs = [pl.BlockSpec((slots, 2, LENGTH, WIDTH), lambda s: (0, 0, s, 0)), per, per, per]
    flat = jax.ShapeDtypeStruct((slots, tokens, WIDTH), BF)
    shapes = [jax.ShapeDtypeStruct((slots, 2, tokens, WIDTH), BF), flat, flat, flat]
    return specs, shapes


def run_forward_first(x, gain, weights):
    tokens, width = x.shape
    specs, shapes = slot_outputs(len(weights), tokens)
    return call(
        forward_first,
        "attention_forward_first",
        (tokens // LENGTH,),
        [row_block(width), whole(1, width)] + [whole(width, 4 * WIDTH)] * len(weights),
        [row_block(width)] + specs,
        [jax.ShapeDtypeStruct((tokens, width), BF)] + shapes,
        1.5e10,
        1e7,
        1e7,
    )(x, gain, *weights)


def run_forward_last(normed, x, ctx, ffn_gain, control, weights):
    tokens, width = x.shape
    specs, shapes = slot_outputs(len(weights) - ctx.shape[0], tokens)
    ctx_spec = pl.BlockSpec((ctx.shape[0], LENGTH, WIDTH), lambda s: (0, s, 0))
    return call(
        forward_last,
        "attention_forward_last",
        (tokens // LENGTH,),
        [row_block(width), row_block(width), ctx_spec, whole(1, width), whole(width, WIDTH)]
        + [whole(width, 4 * WIDTH)] * len(weights),
        specs + [row_block(width), row_block(width), row_block(WIDTH)],
        shapes
        + [
            jax.ShapeDtypeStruct((tokens, width), F32),
            jax.ShapeDtypeStruct((tokens, width), BF),
            jax.ShapeDtypeStruct((tokens, WIDTH), F32),
        ],
        1.5e10,
        1e7,
        1e7,
    )(normed, x, ctx, ffn_gain, control, *weights)


def backward_slot(
    qa_ref, k_ref, v_ref, ctx_ref, ml_ref, wo_ref, normed_ref, *refs
):
    dqkv_ref, dw_ref = refs[-2:]
    block = 512
    ml = ml_ref[...]
    ctx = ctx_ref[0]
    d_out = dot(ml, wo_ref[...]).astype(BF)
    product = d_out.astype(F32) * ctx.astype(F32)
    k = k_ref[0]
    v = v_ref[0]
    k_flip = k.T
    dks, dvs, dqs = [], [], []
    for head in range(2):
        lane, mine, other = head_lanes(LENGTH, head)
        minus = jnp.where((lane >= other) & (lane < other + 3), -1.0, 0.0).astype(BF)
        central = jnp.sum(jnp.where(mine, product, 0.0), axis=1, keepdims=True)
        d_all = with_extra(mine, lane, other, d_out, central)
        k_all = jnp.where(mine, k, minus)
        v_all = jnp.where(mine, v, minus)
        q_all = qa_ref[0, head]
        dq = [0.0] * (LENGTH // block)
        dk, dv = [], []
        for at in range(0, LENGTH, block):
            keys = k_all[at : at + block]
            values = v_all[at : at + block]
            flipped = k_flip[head * HD : (head + 1) * HD, at : at + block]
            dk_here = 0.0
            dv_here = 0.0
            for start in range(at, LENGTH, block):
                queries = q_all[start : start + block]
                d_rows = d_all[start : start + block]
                probs = jnp.exp2(dot_last(keys, queries))
                if start == at:
                    r = lax.broadcasted_iota(jnp.int32, (block, block), 0)
                    c = lax.broadcasted_iota(jnp.int32, (block, block), 1)
                    probs = jnp.where(r <= c, probs, 0.0)
                d_scores = (probs * dot_last(values, d_rows)).astype(BF)
                dv_here = dv_here + dot(probs.astype(BF), d_rows)
                dk_here = dk_here + dot(d_scores, queries)
                dq[start // block] = dq[start // block] + dot(flipped, d_scores)
            dk.append(dk_here)
            dv.append(dv_here)
        dks.append(jnp.concatenate(dk, axis=0))
        dvs.append(jnp.concatenate(dv, axis=0))
        dqs.append(jnp.concatenate(dq, axis=1))
    lane, mine, _ = head_lanes(LENGTH, 0)
    dk = (jnp.where(mine, dks[0], dks[1]) * LN2).astype(BF)
    dv = jnp.where(mine, dvs[0], dvs[1]).astype(BF)
    dq_flip = (jnp.concatenate(dqs, axis=0) * HD**-0.5).astype(BF)
    dqkv_ref[:, :WIDTH] = dq_flip.T
    dqkv_ref[:, WIDTH : 2 * WIDTH] = dk
    dqkv_ref[:, 2 * WIDTH :] = dv
    dw = dot(jnp.concatenate([dq_flip, dk.T, dv.T], axis=0), normed_ref[...])
    dwo = dot_first(ctx, ml)
    parts = [dw[:WIDTH], dw[WIDTH : 2 * WIDTH], dw[2 * WIDTH :], dwo]
    first = pl.program_id(0) == 0

    @pl.when(first)
    def _():
        for index, part in enumerate(parts):
            dw_ref[index] = part if len(refs) == 2 else refs[1][index] + part

    @pl.when(jnp.logical_not(first))
    def _():
        for index, part in enumerate(parts):
            dw_ref[index] += part


def run_backward(saved, index, ml, weight, normed, first, count, earlier=None):
    qa, k, v, ctx = saved
    tokens, width = ml.shape
    per = pl.BlockSpec((1, LENGTH, WIDTH), lambda s: (index, s + first, 0))
    rows = lambda columns: pl.BlockSpec((LENGTH, columns), lambda s: (s + first, 0))
    sums = (4, WIDTH, width)
    args = [qa, k, v, ctx, ml, weight, normed]
    in_specs = [
        pl.BlockSpec((1, 2, LENGTH, WIDTH), lambda s: (index, 0, s + first, 0)),
        per,
        per,
        per,
        rows(width),
        pl.BlockSpec((width, WIDTH), lambda s: (0, 3)),
        rows(width),
    ]
    aliases = {}
    if earlier is not None:
        args += list(earlier)
        in_specs += [pl.BlockSpec(memory_space=pl.ANY), whole(*sums)]
        aliases = {len(args) - 2: 0}
    return call(
        backward_slot,
        "attention_backward",
        (count,),
        in_specs,
        [rows(3 * WIDTH), whole(*sums)],
        [jax.ShapeDtypeStruct((tokens, 3 * WIDTH), BF), jax.ShapeDtypeStruct(sums, F32)],
        0.75e10 * count,
        4e6 * count,
        4e6 * count,
        input_output_aliases=aliases,
    )(*args)


def group_marks(tags, groups):
    id_row, live_row = tags[2:3], tags[3:4]
    slot = lax.broadcasted_iota(jnp.int32, (groups, tags.shape[1]), 0).astype(F32)
    return jnp.where((slot == id_row) & (live_row > 0), 1.0, 0.0).astype(BF)


def token_marks(columns, groups):
    slot = lax.broadcasted_iota(jnp.int32, (columns.shape[0], groups), 1).astype(F32)
    return jnp.where((slot == columns[:, 2:3]) & (columns[:, 3:4] > 0), 1.0, 0.0).astype(BF)


def dot_exact(marks, values):
    return functools.reduce(jnp.add, [dot(marks, part) for part in split3(values)])


def gather_groups(ids_ref, logits_ref, normed2_ref, cot_ref, tags_ref, columns_ref, keep_ref, send_ref):
    tokens = normed2_ref.shape[0]
    groups = keep_ref.shape[1]
    tags = tags_ref[...]
    blank = jnp.zeros((WIDTH - tags.shape[0], tokens), F32)
    turned = jnp.concatenate([tags, blank], axis=0).T
    marks = group_marks(tags, groups)
    token_side = token_marks(turned, groups)
    live = turned[:, 3:4]
    expo = jnp.exp(logits_ref[...]) * live
    totals = dot_exact(marks, expo)
    weights = expo / (dot_exact(token_side, totals) + (1.0 - live))
    lane = lax.broadcasted_iota(jnp.int32, weights.shape, 1)
    columns_ref[...] = jnp.where(lane < 2, weights, turned)
    rows = weights.T[:8].astype(BF)
    own = ids_ref[0] == 0
    normed2 = normed2_ref[...]
    cot = cot_ref[...]
    for ref, pick in ((keep_ref, own), (send_ref, jnp.logical_not(own))):
        assign = marks * jnp.where(pick, rows[0:1].astype(F32), rows[1:2].astype(F32)).astype(BF)
        ref[0] = dot(assign, normed2).astype(BF)
        ref[1] = dot(assign, cot).astype(BF)


def run_gather(ids, logits, normed2, cot, tags):
    tokens, width = normed2.shape
    groups = tokens // 8
    vmem = pl.BlockSpec(memory_space=pltpu.VMEM)
    sums = jax.ShapeDtypeStruct((2, groups, width), BF)
    return call(
        gather_groups,
        "gather_groups",
        (),
        [pl.BlockSpec(memory_space=pltpu.SMEM)] + [vmem] * 4,
        [vmem] * 3,
        [jax.ShapeDtypeStruct((tokens, WIDTH), F32), sums, sums],
        4e9,
        8e6,
    )(ids, logits, normed2, cot, tags)


def gelu_both(x):
    inner = 0.7978845608028654
    cubic = 0.044715
    square = x * x
    bent = jnp.tanh(inner * x * (1.0 + cubic * square))
    half = 0.5 * (1.0 + bent)
    slope = half + 0.5 * x * (1.0 - bent * bent) * (inner * (1.0 + 3.0 * cubic * square))
    return x * half, slope


SPLIT = (176, 176, 160)


def expert_step(
    ids_ref, keep_ref, got_ref, in_ref, out_ref, a_ref, b_ref, c_ref, home_ref, away_ref,
    mixed_flip, result, mixed_grad,
):
    step = pl.program_id(0)
    groups = keep_ref.shape[1]
    mixed = jnp.concatenate([keep_ref[0], got_ref[0]], axis=0)
    d_result = jnp.concatenate([keep_ref[1], got_ref[1]], axis=0)

    @pl.when(step == 0)
    def _():
        mixed_flip[...] = mixed.T
        result[...] = jnp.zeros_like(result)
        mixed_grad[...] = jnp.zeros_like(mixed_grad)

    w_in = in_ref[0]
    w_out = out_ref[0]
    active, slope = gelu_both(dot(mixed, w_in))
    active = active.astype(BF)
    d_before = (dot_last(d_result, w_out) * slope).astype(BF)
    result[...] += dot(active, w_out)
    mixed_grad[...] += dot_last(d_before, w_in)
    d_out = dot_first(active, d_result).astype(BF)
    d_in = dot(mixed_flip[...], d_before).astype(BF)
    half = d_in.shape[0] // 2
    block = jnp.concatenate(
        [d_out, jnp.concatenate([d_in[:half], d_in[half:]], axis=1)], axis=0
    )
    low, high = SPLIT[0], SPLIT[0] + SPLIT[1]
    a_ref[0] = block[:low]
    b_ref[0] = block[low:high]
    c_ref[0] = block[high:]

    @pl.when(step == pl.num_programs(0) - 1)
    def _():
        home_ref[0] = result[:groups].astype(BF)
        home_ref[1] = mixed_grad[:groups].astype(BF)
        away_ref[0] = result[groups:].astype(BF)
        away_ref[1] = mixed_grad[groups:].astype(BF)


def run_experts(ids, keep, got, expert_in, expert_out):
    _, width, hidden = expert_in.shape
    steps = 8
    wide = hidden // steps
    groups = keep.shape[1]
    sums = jax.ShapeDtypeStruct(keep.shape, BF)
    fixed = lambda f, ids: (0, 0, 0)

    def place(index):
        return lambda f, ids: (jnp.bitwise_xor(f, ids[index]), 0, 0)

    return pl.pallas_call(
        expert_step,
        grid_spec=pltpu.PrefetchScalarGridSpec(
            num_scalar_prefetch=1,
            grid=(steps,),
            in_specs=[
                pl.BlockSpec(keep.shape, fixed),
                pl.BlockSpec(keep.shape, fixed),
                pl.BlockSpec((1, width, wide), lambda f, ids: (ids[0], 0, f)),
                pl.BlockSpec((1, wide, width), lambda f, ids: (ids[0], f, 0)),
            ],
            out_specs=[
                pl.BlockSpec((1, SPLIT[i], width), place(i + 1)) for i in range(3)
            ]
            + [pl.BlockSpec(keep.shape, fixed)] * 2,
            scratch_shapes=[
                pltpu.VMEM((width, 2 * groups), BF),
                pltpu.VMEM((2 * groups, width), F32),
                pltpu.VMEM((2 * groups, width), F32),
            ],
        ),
        out_shape=[jax.ShapeDtypeStruct((steps, SPLIT[i], width), BF) for i in range(3)]
        + [sums, sums],
        compiler_params=pltpu.CompilerParams(vmem_limit_bytes=VMEM),
        cost_estimate=pl.CostEstimate(
            flops=int(1e10), bytes_accessed=int(1.2e7), transcendentals=int(1e6)
        ),
        name="experts",
    )(ids, keep, got, expert_in, expert_out)


def spread_groups(
    ids_ref, middle_ref, normed2_ref, cot_ref, columns_ref, tags_ref, home_ref, got_ref,
    gain_ref, control_ref, out_ref, grad_ref, low_ref, small_ref,
    table, mixed_part, weight_grads, group_sums,
):
    phase, index = pl.program_id(0), pl.program_id(1)
    rows, width = middle_ref.shape
    groups = home_ref.shape[1]
    here = pl.ds(pl.multiple_of(index * rows, rows), rows)
    columns = columns_ref[...]
    lane = lax.broadcasted_iota(jnp.int32, columns.shape, 1)
    token_side = token_marks(columns, groups)
    cot = cot_ref[...].astype(F32)
    normed2 = normed2_ref[...].astype(F32)
    middle = middle_ref[...]

    @pl.when((phase == 0) & (index == 0))
    def _():
        group_sums[...] = jnp.zeros_like(group_sums)
        small_ref[...] = jnp.zeros_like(small_ref)
        own = ids_ref[0] == 0
        for kind in range(2):
            home, got = home_ref[kind], got_ref[kind]
            at = 2 * kind * width
            table[:, at : at + width] = jnp.where(own, home, got)
            table[:, at + width : at + 2 * width] = jnp.where(own, got, home)

    @pl.when(phase == 0)
    def _():
        spread = dot(token_side, table[...])
        low = columns.astype(BF).astype(F32)
        first, second = low[:, 0:1], low[:, 1:2]
        result = [spread[:, i * width : (i + 1) * width] for i in range(4)]
        out_ref[...] = (middle + first * result[0] + second * result[1]).astype(BF)
        mixed_part[here] = first * result[2] + second * result[3]
        grads = [
            jnp.sum(cot * result[i] + normed2 * result[2 + i], axis=1, keepdims=True)
            for i in range(2)
        ]
        grads = jnp.where(lane == 0, grads[0], jnp.where(lane == 1, grads[1], 0.0))
        weight_grads[here] = grads
        marks = group_marks(tags_ref[...], groups)
        group_sums[...] += dot_exact(marks, jnp.where(lane < 2, columns * grads, 0.0))

    @pl.when(phase == 1)
    def _():
        central = dot_exact(token_side, group_sums[...])
        logit_grads = jnp.where(lane < 2, columns * (weight_grads[here] - central), 0.0)
        first, second = logit_grads[:, 0:1], logit_grads[:, 1:2]
        control = control_ref[...].astype(F32)
        grad = mixed_part[here] + first * control[0:1] + second * control[1:2]
        scale = lax.rsqrt(jnp.mean(middle * middle, axis=-1, keepdims=True) + eps)
        unit = middle * scale
        pulled = grad * gain_ref[...]
        pulled = scale * (pulled - unit * jnp.mean(pulled * unit, axis=-1, keepdims=True))
        total = cot + pulled
        grad_ref[...] = total
        low_ref[...] = total.astype(BF)
        small_ref[0:1] += jnp.sum(grad * unit, axis=0, keepdims=True)
        small_ref[1:2] += jnp.sum(first * normed2, axis=0, keepdims=True)
        small_ref[2:3] += jnp.sum(second * normed2, axis=0, keepdims=True)


def run_spread(ids, middle, normed2, cot, columns, tags, home, got, gain, control):
    tokens, width = middle.shape
    groups = home.shape[1]
    rows = 512
    steps = tokens // rows
    by_block = lambda n: pl.BlockSpec((rows, n), lambda p, b: (b, 0))
    fixed = lambda *shape: pl.BlockSpec(shape, lambda p, b: (0,) * len(shape))
    second = lambda n: pl.BlockSpec((rows, n), lambda p, b: (b * p, 0))
    return call(
        spread_groups,
        "spread_groups",
        (2, steps),
        [
            pl.BlockSpec(memory_space=pltpu.SMEM),
            by_block(width),
            by_block(width),
            by_block(width),
            by_block(WIDTH),
            pl.BlockSpec((8, rows), lambda p, b: (0, b)),
            fixed(*home.shape),
            fixed(*home.shape),
            fixed(1, width),
            fixed(8, width),
        ],
        [
            pl.BlockSpec((rows, width), lambda p, b: (b * (1 - p) + (steps - 1) * p, 0)),
            second(width),
            second(width),
            fixed(8, width),
        ],
        [
            jax.ShapeDtypeStruct((tokens, width), BF),
            jax.ShapeDtypeStruct((tokens, width), F32),
            jax.ShapeDtypeStruct((tokens, width), BF),
            jax.ShapeDtypeStruct((8, width), F32),
        ],
        8e9,
        2.4e7,
        scratch_shapes=[
            pltpu.VMEM((groups, 4 * width), BF),
            pltpu.VMEM((tokens, width), F32),
            pltpu.VMEM((tokens, WIDTH), F32),
            pltpu.VMEM((groups, WIDTH), F32),
        ],
    )(ids, middle, normed2, cot, columns, tags, home, got, gain, control)


def input_rows(x_ref, gain_ref, grad_ref, small_ref, *refs):
    slots = (len(refs) - 2) // 2
    flats, weights = refs[:slots], refs[slots : 2 * slots]
    out_ref, sums_ref = refs[2 * slots :]
    rows = x_ref[...].astype(F32)
    grad = 0.0
    for flat, weight in zip(flats, weights):
        grad = grad + dot_last(flat[...], weight[:, : 3 * WIDTH])
    scale = lax.rsqrt(jnp.mean(rows * rows, axis=-1, keepdims=True) + eps)
    unit = rows * scale
    pulled = grad * gain_ref[...]
    pulled = scale * (pulled - unit * jnp.mean(pulled * unit, axis=-1, keepdims=True))
    out_ref[...] = grad_ref[...] + pulled

    @pl.when(pl.program_id(0) == 0)
    def _():
        sums_ref[...] = small_ref[...]

    sums_ref[3:4] += jnp.sum(grad * unit, axis=0, keepdims=True)


def run_input(x, gain, grad, small, flats, weights):
    tokens, width = x.shape
    rows = 256
    by_block = lambda n: pl.BlockSpec((rows, n), lambda s: (s, 0))
    return call(
        input_rows,
        "input_rows",
        (tokens // rows,),
        [by_block(width), whole(1, width), by_block(width), whole(8, width)]
        + [by_block(3 * WIDTH)] * len(flats)
        + [whole(width, 4 * WIDTH)] * len(weights),
        [by_block(width), whole(8, width)],
        [jax.ShapeDtypeStruct((tokens, width), F32), jax.ShapeDtypeStruct((8, width), F32)],
        5e9,
        1.6e7,
    )(x, gain, grad, small, *flats, *weights)


def join_own(ids_ref, own_ref, one_ref, two_ref, out_ref):
    out_ref[...] = (
        own_ref[...] + one_ref[...].astype(F32) + two_ref[...].astype(F32)
    ).astype(BF)


def run_join(ids, own, one, two):
    n, rows, width = own.shape
    source = pl.BlockSpec((1, rows, width), lambda r, ids: (jnp.bitwise_xor(r, ids[4]), 0, 0))
    return pl.pallas_call(
        join_own,
        grid_spec=pltpu.PrefetchScalarGridSpec(
            num_scalar_prefetch=1,
            grid=(n,),
            in_specs=[source] * 3,
            out_specs=pl.BlockSpec((1, rows, width), lambda r, ids: (r, 0, 0)),
        ),
        out_shape=jax.ShapeDtypeStruct(own.shape, BF),
        name="join_own",
    )(ids, own, one, two)


def open_own(ids_ref, low_ref, high_ref, q_ref, k_ref, v_ref, o_ref):
    half = low_ref.shape[0]
    for index, ref in enumerate((q_ref, k_ref, v_ref, o_ref)):
        place = jnp.bitwise_xor(index, ids_ref[4])
        near = low_ref[lax.rem(place, half)].astype(F32)
        far = high_ref[lax.rem(place, half)].astype(F32)
        value = jnp.where(place < half, near, far)
        ref[...] = value if index == 3 else value.T


def run_open(ids, low, high):
    _, rows, width = low.shape
    vmem = pl.BlockSpec(memory_space=pltpu.VMEM)
    return call(
        open_own,
        "open_own",
        (),
        [pl.BlockSpec(memory_space=pltpu.SMEM), vmem, vmem],
        [vmem] * 4,
        [jax.ShapeDtypeStruct((width, rows), F32)] * 3
        + [jax.ShapeDtypeStruct((rows, width), F32)],
        1e6,
        2e6,
    )(ids, low, high)


def open_experts(ids_ref, *refs):
    in_ref, out_ref = refs[-2:]
    step = pl.program_id(1)
    own = pl.program_id(0) == ids_ref[0]
    pieces = []
    for index in range(3):
        low, high, low_far, high_far = refs[4 * index : 4 * index + 4]
        near = jnp.bitwise_xor(step, ids_ref[index + 1]) < 4
        mine = jnp.where(near, low[0], high[0])
        other = jnp.where(near, low_far[0], high_far[0])
        pieces.append(jnp.where(own, mine, other))
    block = jnp.concatenate(pieces, axis=0).astype(F32)
    rows = block.shape[0] // 2
    out_ref[0] = block[:rows]
    in_ref[0, :rows] = block[rows:, :rows]
    in_ref[0, rows:] = block[rows:, rows:]


def run_open_experts(ids, parts, shape_in, shape_out):
    experts, width, hidden = shape_in
    steps = 8
    wide = hidden // steps

    def place(index, high):
        def at(e, f, ids):
            spot = jnp.bitwise_xor(f, ids[index + 1])
            return (lax.rem(spot, 4), 0, 0)

        return pl.BlockSpec((1, SPLIT[index], width), at)

    args, specs = [], []
    for index, part in enumerate(parts):
        args += part
        specs += [place(index, False)] * 4
    return pl.pallas_call(
        open_experts,
        grid_spec=pltpu.PrefetchScalarGridSpec(
            num_scalar_prefetch=1,
            grid=(experts, steps),
            in_specs=specs,
            out_specs=[
                pl.BlockSpec((1, width, wide), lambda e, f, ids: (e, 0, f)),
                pl.BlockSpec((1, wide, width), lambda e, f, ids: (e, f, 0)),
            ],
        ),
        out_shape=[jax.ShapeDtypeStruct(shape_in, F32), jax.ShapeDtypeStruct(shape_out, F32)],
        compiler_params=pltpu.CompilerParams(vmem_limit_bytes=VMEM),
        cost_estimate=pl.CostEstimate(flops=10**6, bytes_accessed=3 * 10**7, transcendentals=0),
        name="open_experts",
    )(ids, *args)


def tie(*values):
    return lax.optimization_barrier(values)


def build(mesh):
    n_head, n_batch = mesh.shape["head"], mesh.shape["batch"]
    head_bits = [("head", 1 << i) for i in range(n_head.bit_length() - 1)]
    batch_bits = [("batch", 1 << i) for i in range(n_batch.bit_length() - 1)]
    pair, across = head_bits
    first_batch, second_batch, *last_batch = batch_bits
    orders = [
        (across, first_batch, second_batch),
        (first_batch, second_batch, across),
        (second_batch, across, first_batch),
    ]

    def swap(value, step):
        axis, bit = step
        return lax.ppermute(value, axis, [(i, i ^ bit) for i in range(mesh.shape[axis])])

    def bit_of(step):
        axis, bit = step
        return (lax.axis_index(axis) // bit) % 2

    def number(steps):
        return functools.reduce(lambda value, step: 2 * value + bit_of(step), steps, 0)

    def add(kept, got):
        return (kept.astype(F32) + got.astype(F32)).astype(BF)

    def local(
        inputs,
        attn_gain,
        query_weight,
        key_weight,
        value_weight,
        output_weight,
        ffn_gain,
        controller,
        expert_in,
        expert_out,
        group_ids,
        live_mask,
        cotangent,
    ):
        tokens_here, width = inputs.shape
        sequences = tokens_here // LENGTH
        ids = jnp.stack(
            [bit_of(pair)]
            + [number(order) for order in orders]
            + [number((first_batch, second_batch))]
        ).astype(jnp.int32)
        w0 = run_pack(query_weight, key_weight, value_weight, output_weight)
        w2 = swap(w0, across)
        w1 = swap(w0, pair)
        normed, *saved_a = run_forward_first(inputs, attn_gain[None], [w0, w1])
        w3 = swap(w2, pair)
        weights = [w0, w1, w2, w3]
        control = jnp.pad(controller, ((0, 0), (0, WIDTH - controller.shape[1])))
        *saved_b, middle, normed2, logits = run_forward_last(
            normed, inputs, saved_a[3], ffn_gain[None], control, weights
        )

        blank = jnp.zeros((1, tokens_here), F32)
        tags = jnp.concatenate(
            [blank, blank, group_ids.astype(F32)[None], live_mask.astype(F32)[None]] + [blank] * 4,
            axis=0,
        )
        columns, keep, send = run_gather(ids, logits, normed2, cotangent, tags)
        *parts, home, away = run_experts(ids, keep, swap(send, pair), expert_in, expert_out)
        home_got = swap(away, pair)

        def send_half(blocks, step):
            half = blocks.shape[0] // 2
            return blocks[:half], swap(blocks[half:], step)

        kept, got = zip(*[send_half(part, order[0]) for part, order in zip(parts, orders)])
        layer_out, middle_grad, middle_low, small = run_spread(
            ids,
            middle,
            normed2,
            cotangent,
            columns,
            tags,
            home,
            home_got,
            ffn_gain[None],
            jnp.pad(controller.T, ((0, 8 - controller.shape[1]), (0, 0))),
        )

        flats = [None] * 4
        sums = [None] * 4

        def backward(slot, low, first=0, count=sequences):
            saved, index = (saved_a, slot) if slot < 2 else (saved_b, slot - 2)
            earlier = None if first == 0 else (flats[slot], sums[slot])
            flats[slot], sums[slot] = run_backward(
                saved, index, low, weights[slot], normed, first, count, earlier
            )

        half = sequences // 2

        def next_stage(kept, got, low, mark, stage):
            *got, mark = tie(*got, mark)
            blocks = [add(a, b) for a, b in zip(kept, got)]
            if stage < 3:
                kept = [block[: block.shape[0] // 2] for block in blocks]
                sent = [block[block.shape[0] // 2 :] for block in blocks]
            else:
                kept = sent = blocks
            *sent, low = tie(*sent, low)
            steps = [order[stage] if stage < 3 else last_batch[stage - 3] for order in orders]
            return kept, [swap(block, step) for block, step in zip(sent, steps)], low

        low = middle_low
        backward(3, low, 0, half)
        kept, got, low = next_stage(kept, got, low, sums[3], 1)
        backward(3, low, half, sequences - half)
        third_got = swap(sums[3].astype(BF), pair)
        backward(2, low, 0, half)
        kept, got, low = next_stage(kept, got, low, sums[2], 2)
        backward(2, low, half, sequences - half)
        second = sums[2] + third_got.astype(F32)
        second_got = swap(second.astype(BF), across)
        kept, got, low = next_stage(kept, got, low, sums[2], 3)
        backward(1, low)
        first_got = swap(sums[1].astype(BF), pair)
        backward(0, low)
        mark = sums[0]
        for stage in range(4, 3 + len(last_batch)):
            kept, got, low = next_stage(kept, got, low, mark, stage)
        own = run_join(ids, sums[0], second_got, first_got)

        *got, own = tie(*got, own)
        blocks = [add(a, b) for a, b in zip(kept, got)]
        for stage in (2, 1):
            blocks = [
                jnp.concatenate([block, swap(block, order[stage])], axis=0)
                for block, order in zip(blocks, orders)
            ]
        far = [swap(block, order[0]) for block, order in zip(blocks, orders)]
        blocks_other = [swap(block, pair) for block in blocks]
        far_other = [swap(block, pair) for block in far]
        expert_in_grad, expert_out_grad = run_open_experts(
            ids,
            [list(group) for group in zip(blocks, far, blocks_other, far_other)],
            expert_in.shape,
            expert_out.shape,
        )

        kept, got = send_half(own, first_batch)
        kept, got = send_half(add(kept, got), second_batch)
        total = add(kept, got)
        for step in last_batch:
            total = add(total, swap(total, step))
        total = jnp.concatenate([total, swap(total, second_batch)], axis=0)
        query_grad, key_grad, value_grad, output_grad = run_open(
            ids, total, swap(total, first_batch)
        )

        input_grad, small = run_input(inputs, attn_gain[None], middle_grad, small, flats, weights)
        for step in head_bits + batch_bits:
            small = small + swap(small, step)
        return (
            layer_out,
            input_grad,
            small[3],
            query_grad,
            key_grad,
            value_grad,
            output_grad,
            small[0],
            small[1:3].T,
            expert_in_grad,
            expert_out_grad,
        )

    return local


def solution(mesh):
    in_specs = (
        P(("batch", "head"), None),
        P(),
        P(None, "head"),
        P(None, "head"),
        P(None, "head"),
        P("head", None),
        P(),
        P(),
        P(),
        P(),
        P(("batch", "head")),
        P(("batch", "head")),
        P(("batch", "head"), None),
    )
    out_specs = (
        P(("batch", "head"), None),
        P(("batch", "head"), None),
        P(),
        P(None, "head"),
        P(None, "head"),
        P(None, "head"),
        P("head", None),
        P(),
        P(),
        P(),
        P(),
    )
    return jax.shard_map(
        build(mesh), mesh=mesh, in_specs=in_specs, out_specs=out_specs, check_vma=False
    )
```

```python
import functools

import jax
import jax.numpy as jnp
from jax import lax
from jax.experimental import pallas as pl
from jax.experimental.pallas import tpu as pltpu
from jax.sharding import PartitionSpec as P

HD = 64
LENGTH = 1024
WIDTH = 128
BF = jnp.bfloat16
F32 = jnp.float32
LOG2E = 1.4426950408889634
LN2 = 0.6931471805599453
VMEM = 20 * 2**20
FULL_VMEM = 56 * 2**20

eps = 1e-06
last_dims = (((1,), (1,)), ((), ()))
first_dims = (((0,), (0,)), ((), ()))


def dot(left, right):
    return jnp.dot(left, right, preferred_element_type=F32)


def dot_last(left, right):
    return lax.dot_general(left, right, last_dims, preferred_element_type=F32)


def dot_first(left, right):
    return lax.dot_general(left, right, first_dims, preferred_element_type=F32)


def split3(value):
    high = value.astype(BF)
    rest = value - high.astype(F32)
    mid = rest.astype(BF)
    low = (rest - mid.astype(F32)).astype(BF)
    return high, mid, low


def call(
    body, name, grid, in_specs, out_specs, out_shape, flops, moved, exps=0, vmem=VMEM, **extra
):
    return pl.pallas_call(
        body,
        grid=grid,
        in_specs=in_specs,
        out_specs=out_specs,
        out_shape=out_shape,
        compiler_params=pltpu.CompilerParams(vmem_limit_bytes=vmem),
        cost_estimate=pl.CostEstimate(
            flops=int(flops), bytes_accessed=int(moved), transcendentals=int(exps)
        ),
        name=name,
        **extra,
    )


def row_block(columns):
    return pl.BlockSpec((LENGTH, columns), lambda s: (s, 0))


def whole(*shape):
    return pl.BlockSpec(shape, lambda s: (0,) * len(shape))


def head_lanes(rows, head):
    lane = lax.broadcasted_iota(jnp.int32, (rows, WIDTH), 1)
    mine = (lane < HD) if head == 0 else (lane >= HD)
    return lane, mine, HD if head == 0 else 0


def with_extra(mine, lane, other, values, extra):
    high, mid, low = split3(extra)
    filler = jnp.zeros_like(values)
    for place, part in ((2, low), (1, mid), (0, high)):
        filler = jnp.where(lane == other + place, part, filler)
    return jnp.where(mine, values, filler)


def attend_slot(normed, weight, slot, qa_ref, k_ref, v_ref, ctx_ref):
    block = 256
    qkv = dot(normed, weight)
    q = (qkv[:, :WIDTH] * (HD**-0.5 * LOG2E)).astype(BF)
    k = qkv[:, WIDTH : 2 * WIDTH].astype(BF)
    v = qkv[:, 2 * WIDTH :].astype(BF)
    k_ref[slot] = k
    v_ref[slot] = v
    for head in range(2):
        lane, mine, other = head_lanes(LENGTH, head)
        qh = jnp.where(mine, q, jnp.zeros_like(q))
        vh = jnp.where(mine, v, (lane == other).astype(F32).astype(BF))
        q_long = qh.astype(F32)
        k_long = jnp.where(mine, k, jnp.zeros_like(k)).astype(F32)
        bound = jnp.max(jnp.sum(q_long * q_long, axis=1, keepdims=True)) * jnp.max(
            jnp.sum(k_long * k_long, axis=1, keepdims=True)
        )

        def rows_of(small):
            lane_b, mine_b, _ = head_lanes(block, head)
            for start in range(0, LENGTH, block):
                here = slice(start, start + block)
                queries = qh[here]
                scores = []
                for at in range(0, start + block, block):
                    part = dot_last(queries, k[at : at + block])
                    if at == start:
                        r = lax.broadcasted_iota(jnp.int32, (block, block), 0)
                        c = lax.broadcasted_iota(jnp.int32, (block, block), 1)
                        part = jnp.where(c <= r, part, -1e30)
                    scores.append(part)
                if not small:
                    peak = functools.reduce(
                        jnp.maximum, [jnp.max(part, axis=1, keepdims=True) for part in scores]
                    )
                    scores = [part - peak for part in scores]
                out = 0.0
                for index, part in enumerate(scores):
                    out = out + dot(
                        jnp.exp2(part).astype(BF), vh[index * block : (index + 1) * block]
                    )
                total = out[:, other : other + 1]
                logsum = jnp.log2(total)
                if not small:
                    logsum = logsum + peak
                context = (out * (1.0 / total)).astype(BF)
                qa_ref[slot, head, here] = with_extra(mine_b, lane_b, other, queries, logsum)
                if head == 1:
                    context = jnp.where(mine_b, context, ctx_ref[slot, here])
                ctx_ref[slot, here] = context

        small = bound < 1e4

        @pl.when(small)
        def _():
            rows_of(True)

        @pl.when(jnp.logical_not(small))
        def _():
            rows_of(False)


def norm_rows(rows):
    return rows * lax.rsqrt(jnp.mean(rows * rows, axis=-1, keepdims=True) + eps)


def pack_weights(q_ref, k_ref, v_ref, o_ref, packed_ref):
    for index, ref in enumerate((q_ref, k_ref, v_ref)):
        packed_ref[:, index * WIDTH : (index + 1) * WIDTH] = ref[...]
    packed_ref[:, 3 * WIDTH :] = o_ref[...].T


def run_pack(q, k, v, o):
    width = q.shape[0]
    return call(
        pack_weights,
        "pack_weights",
        (),
        [pl.BlockSpec(memory_space=pltpu.VMEM)] * 4,
        pl.BlockSpec(memory_space=pltpu.VMEM),
        jax.ShapeDtypeStruct((width, 4 * WIDTH), BF),
        1e6,
        2e6,
        vmem=FULL_VMEM,
    )(q, k, v, o)


def forward_first(x_ref, gain_ref, *refs):
    slots = len(refs) - 5
    normed_ref, qa_ref, k_ref, v_ref, ctx_ref = refs[slots:]
    normed = (norm_rows(x_ref[...].astype(F32)) * gain_ref[...]).astype(BF)
    normed_ref[...] = normed
    for slot in range(slots):
        weight = refs[slot][:, : 3 * WIDTH]
        attend_slot(normed, weight, slot, qa_ref, k_ref, v_ref, ctx_ref)


def forward_last(normed_ref, x_ref, ctx_in_ref, ffn_gain_ref, control_ref, *refs):
    slots = len(refs) - 7
    weights = refs[:slots]
    qa_ref, k_ref, v_ref, ctx_ref, middle_ref, normed2_ref, logits_ref = refs[slots:]
    normed = normed_ref[...]
    before = ctx_in_ref.shape[0]
    for slot in range(slots - before):
        weight = weights[before + slot][:, : 3 * WIDTH]
        attend_slot(normed, weight, slot, qa_ref, k_ref, v_ref, ctx_ref)
    context = jnp.concatenate(
        [ctx_in_ref[i] for i in range(before)] + [ctx_ref[i] for i in range(slots - before)],
        axis=1,
    )
    flipped = jnp.concatenate([ref[:, 3 * WIDTH :] for ref in weights], axis=1)
    middle = x_ref[...].astype(F32) + dot_last(context, flipped)
    middle_ref[...] = middle
    normed2 = (norm_rows(middle) * ffn_gain_ref[...]).astype(BF)
    normed2_ref[...] = normed2
    logits_ref[...] = dot(normed2, control_ref[...])


def slot_outputs(slots, tokens):
    per = pl.BlockSpec((slots, LENGTH, WIDTH), lambda s: (0, s, 0))
    specs = [pl.BlockSpec((slots, 2, LENGTH, WIDTH), lambda s: (0, 0, s, 0)), per, per, per]
    flat = jax.ShapeDtypeStruct((slots, tokens, WIDTH), BF)
    shapes = [jax.ShapeDtypeStruct((slots, 2, tokens, WIDTH), BF), flat, flat, flat]
    return specs, shapes


def run_forward_first(x, gain, weights):
    tokens, width = x.shape
    specs, shapes = slot_outputs(len(weights), tokens)
    return call(
        forward_first,
        "attention_forward_first",
        (tokens // LENGTH,),
        [row_block(width), whole(1, width)] + [whole(width, 4 * WIDTH)] * len(weights),
        [row_block(width)] + specs,
        [jax.ShapeDtypeStruct((tokens, width), BF)] + shapes,
        1.5e10,
        1e7,
        1e7,
    )(x, gain, *weights)


def run_forward_last(normed, x, ctx, ffn_gain, control, weights):
    tokens, width = x.shape
    specs, shapes = slot_outputs(len(weights) - ctx.shape[0], tokens)
    ctx_spec = pl.BlockSpec((ctx.shape[0], LENGTH, WIDTH), lambda s: (0, s, 0))
    return call(
        forward_last,
        "attention_forward_last",
        (tokens // LENGTH,),
        [row_block(width), row_block(width), ctx_spec, whole(1, width), whole(width, WIDTH)]
        + [whole(width, 4 * WIDTH)] * len(weights),
        specs + [row_block(width), row_block(width), row_block(WIDTH)],
        shapes
        + [
            jax.ShapeDtypeStruct((tokens, width), F32),
            jax.ShapeDtypeStruct((tokens, width), BF),
            jax.ShapeDtypeStruct((tokens, WIDTH), F32),
        ],
        1.5e10,
        1e7,
        1e7,
    )(normed, x, ctx, ffn_gain, control, *weights)


def backward_slot(slots, qa_ref, k_ref, v_ref, ctx_ref, ml_ref, normed_ref, *refs):
    dqkv_ref, dw_ref = refs[-2:]
    slot, sequence = pl.program_id(0), pl.program_id(1)
    weight = refs[0][...]
    for index in range(1, slots):
        weight = jnp.where(slot == index, refs[index][...], weight)
    block = 512
    ml = ml_ref[...]
    ctx = ctx_ref[0]
    d_out = dot(ml, weight).astype(BF)
    product = d_out.astype(F32) * ctx.astype(F32)
    k = k_ref[0]
    v = v_ref[0]
    k_flip = k.T
    dks, dvs, dqs = [], [], []
    for head in range(2):
        lane, mine, other = head_lanes(LENGTH, head)
        minus = jnp.where((lane >= other) & (lane < other + 3), -1.0, 0.0).astype(BF)
        central = jnp.sum(jnp.where(mine, product, 0.0), axis=1, keepdims=True)
        d_all = with_extra(mine, lane, other, d_out, central)
        k_all = jnp.where(mine, k, minus)
        v_all = jnp.where(mine, v, minus)
        q_all = qa_ref[0, head]
        dq = [0.0] * (LENGTH // block)
        dk, dv = [], []
        for at in range(0, LENGTH, block):
            keys = k_all[at : at + block]
            values = v_all[at : at + block]
            flipped = k_flip[head * HD : (head + 1) * HD, at : at + block]
            dk_here = 0.0
            dv_here = 0.0
            for start in range(at, LENGTH, block):
                queries = q_all[start : start + block]
                d_rows = d_all[start : start + block]
                probs = jnp.exp2(dot_last(keys, queries))
                if start == at:
                    r = lax.broadcasted_iota(jnp.int32, (block, block), 0)
                    c = lax.broadcasted_iota(jnp.int32, (block, block), 1)
                    probs = jnp.where(r <= c, probs, 0.0)
                d_scores = (probs * dot_last(values, d_rows)).astype(BF)
                dv_here = dv_here + dot(probs.astype(BF), d_rows)
                dk_here = dk_here + dot(d_scores, queries)
                dq[start // block] = dq[start // block] + dot(flipped, d_scores)
            dk.append(dk_here)
            dv.append(dv_here)
        dks.append(jnp.concatenate(dk, axis=0))
        dvs.append(jnp.concatenate(dv, axis=0))
        dqs.append(jnp.concatenate(dq, axis=1))
    lane, mine, _ = head_lanes(LENGTH, 0)
    dk = (jnp.where(mine, dks[0], dks[1]) * LN2).astype(BF)
    dv = jnp.where(mine, dvs[0], dvs[1]).astype(BF)
    dq_flip = (jnp.concatenate(dqs, axis=0) * HD**-0.5).astype(BF)
    dqkv_ref[0, :, :WIDTH] = dq_flip.T
    dqkv_ref[0, :, WIDTH : 2 * WIDTH] = dk
    dqkv_ref[0, :, 2 * WIDTH :] = dv
    dw = dot(jnp.concatenate([dq_flip, dk.T, dv.T], axis=0), normed_ref[...])
    dwo = dot_first(ctx, ml)
    parts = [dw[:WIDTH], dw[WIDTH : 2 * WIDTH], dw[2 * WIDTH :], dwo]
    earlier = refs[slots + 1] if len(refs) > slots + 2 else None

    @pl.when(sequence == 0)
    def _():
        for index, part in enumerate(parts):
            dw_ref[0, index] = part if earlier is None else earlier[0, index] + part

    @pl.when(sequence > 0)
    def _():
        for index, part in enumerate(parts):
            dw_ref[0, index] += part


def run_backward(saved, index, ml, weights, normed, first, count, earlier=None):
    qa, k, v, ctx = saved
    tokens, width = ml.shape
    slots = len(weights)
    per = pl.BlockSpec((1, LENGTH, WIDTH), lambda j, s: (index - j, s + first, 0))
    rows = pl.BlockSpec((LENGTH, width), lambda j, s: (s + first, 0))
    sums = pl.BlockSpec((1, 4, WIDTH, width), lambda j, s: (j, 0, 0, 0))
    args = [qa, k, v, ctx, ml, normed, *weights]
    in_specs = [
        pl.BlockSpec((1, 2, LENGTH, WIDTH), lambda j, s: (index - j, 0, s + first, 0)),
        per,
        per,
        per,
        rows,
        rows,
    ] + [pl.BlockSpec((width, WIDTH), lambda j, s: (0, 3))] * slots
    aliases = {}
    if earlier is not None:
        args += list(earlier)
        in_specs += [pl.BlockSpec(memory_space=pl.ANY), sums]
        aliases = {len(args) - 2: 0}
    return call(
        functools.partial(backward_slot, slots),
        "attention_backward",
        (slots, count),
        in_specs,
        [pl.BlockSpec((1, LENGTH, 3 * WIDTH), lambda j, s: (j, s + first, 0)), sums],
        [
            jax.ShapeDtypeStruct((slots, tokens, 3 * WIDTH), BF),
            jax.ShapeDtypeStruct((slots, 4, WIDTH, width), F32),
        ],
        0.75e10 * count * slots,
        4e6 * count,
        4e6 * count,
        input_output_aliases=aliases,
    )(*args)


def group_marks(tags, groups):
    id_row, live_row = tags[2:3], tags[3:4]
    slot = lax.broadcasted_iota(jnp.int32, (groups, tags.shape[1]), 0).astype(F32)
    return jnp.where((slot == id_row) & (live_row > 0), 1.0, 0.0).astype(BF)


def token_marks(columns, groups):
    slot = lax.broadcasted_iota(jnp.int32, (columns.shape[0], groups), 1).astype(F32)
    return jnp.where((slot == columns[:, 2:3]) & (columns[:, 3:4] > 0), 1.0, 0.0).astype(BF)


def dot_exact(marks, values):
    return functools.reduce(jnp.add, [dot(marks, part) for part in split3(values)])


def gather_groups(ids_ref, logits_ref, normed2_ref, cot_ref, tags_ref, columns_ref, keep_ref, send_ref):
    tokens = normed2_ref.shape[0]
    groups = keep_ref.shape[1]
    tags = tags_ref[...]
    blank = jnp.zeros((WIDTH - tags.shape[0], tokens), F32)
    turned = jnp.concatenate([tags, blank], axis=0).T
    marks = group_marks(tags, groups)
    token_side = token_marks(turned, groups)
    live = turned[:, 3:4]
    expo = jnp.exp(logits_ref[...]) * live
    totals = dot_exact(marks, expo)
    weights = expo / (dot_exact(token_side, totals) + (1.0 - live))
    lane = lax.broadcasted_iota(jnp.int32, weights.shape, 1)
    columns_ref[...] = jnp.where(lane < 2, weights, turned)
    rows = weights.T[:8].astype(BF)
    own = ids_ref[0] == 0
    normed2 = normed2_ref[...]
    cot = cot_ref[...]
    for ref, pick in ((keep_ref, own), (send_ref, jnp.logical_not(own))):
        assign = marks * jnp.where(pick, rows[0:1].astype(F32), rows[1:2].astype(F32)).astype(BF)
        ref[0] = dot(assign, normed2).astype(BF)
        ref[1] = dot(assign, cot).astype(BF)


def run_gather(ids, logits, normed2, cot, tags):
    tokens, width = normed2.shape
    groups = tokens // 8
    vmem = pl.BlockSpec(memory_space=pltpu.VMEM)
    sums = jax.ShapeDtypeStruct((2, groups, width), BF)
    return call(
        gather_groups,
        "gather_groups",
        (),
        [pl.BlockSpec(memory_space=pltpu.SMEM)] + [vmem] * 4,
        [vmem] * 3,
        [jax.ShapeDtypeStruct((tokens, WIDTH), F32), sums, sums],
        4e9,
        8e6,
    )(ids, logits, normed2, cot, tags)


def gelu_both(x):
    inner = 0.7978845608028654
    cubic = 0.044715
    square = x * x
    bent = jnp.tanh(inner * x * (1.0 + cubic * square))
    half = 0.5 * (1.0 + bent)
    slope = half + 0.5 * x * (1.0 - bent * bent) * (inner * (1.0 + 3.0 * cubic * square))
    return x * half, slope


SPLIT = (176, 176, 160)


def expert_step(
    ids_ref, keep_ref, got_ref, in_ref, out_ref, *refs
):
    kept_refs, sent_refs = refs[:3], refs[3:6]
    home_ref, away_ref, mixed_flip, result, mixed_grad = refs[6:]
    step = pl.program_id(0)
    groups = keep_ref.shape[1]
    mixed = jnp.concatenate([keep_ref[0], got_ref[0]], axis=0)
    d_result = jnp.concatenate([keep_ref[1], got_ref[1]], axis=0)

    @pl.when(step == 0)
    def _():
        mixed_flip[...] = mixed.T
        result[...] = jnp.zeros_like(result)
        mixed_grad[...] = jnp.zeros_like(mixed_grad)

    w_in = in_ref[0]
    w_out = out_ref[0]
    active, slope = gelu_both(dot(mixed, w_in))
    active = active.astype(BF)
    d_before = (dot_last(d_result, w_out) * slope).astype(BF)
    result[...] += dot(active, w_out)
    mixed_grad[...] += dot_last(d_before, w_in)
    d_out = dot_first(active, d_result).astype(BF)
    d_in = dot(mixed_flip[...], d_before).astype(BF)
    half = d_in.shape[0] // 2
    block = jnp.concatenate(
        [d_out, jnp.concatenate([d_in[:half], d_in[half:]], axis=1)], axis=0
    )
    at = 0
    for index, rows in enumerate(SPLIT):
        place = jnp.bitwise_xor(step, ids_ref[index + 1])
        piece = block[at : at + rows]
        at += rows

        @pl.when(place < 4)
        def _():
            kept_refs[index][place] = piece

        @pl.when(place >= 4)
        def _():
            sent_refs[index][place - 4] = piece

    @pl.when(step == pl.num_programs(0) - 1)
    def _():
        home_ref[0] = result[:groups].astype(BF)
        home_ref[1] = mixed_grad[:groups].astype(BF)
        away_ref[0] = result[groups:].astype(BF)
        away_ref[1] = mixed_grad[groups:].astype(BF)


def run_experts(ids, keep, got, expert_in, expert_out):
    _, width, hidden = expert_in.shape
    steps = 8
    wide = hidden // steps
    groups = keep.shape[1]
    sums = jax.ShapeDtypeStruct(keep.shape, BF)
    fixed = lambda f, ids: (0, 0, 0)

    halves = [(steps // 2, rows, width) for rows in SPLIT] * 2
    return pl.pallas_call(
        expert_step,
        grid_spec=pltpu.PrefetchScalarGridSpec(
            num_scalar_prefetch=1,
            grid=(steps,),
            in_specs=[
                pl.BlockSpec(keep.shape, fixed),
                pl.BlockSpec(keep.shape, fixed),
                pl.BlockSpec((1, width, wide), lambda f, ids: (ids[0], 0, f)),
                pl.BlockSpec((1, wide, width), lambda f, ids: (ids[0], f, 0)),
            ],
            out_specs=[pl.BlockSpec(shape, fixed) for shape in halves + [keep.shape] * 2],
            scratch_shapes=[
                pltpu.VMEM((width, 2 * groups), BF),
                pltpu.VMEM((2 * groups, width), F32),
                pltpu.VMEM((2 * groups, width), F32),
            ],
        ),
        out_shape=[jax.ShapeDtypeStruct(shape, BF) for shape in halves] + [sums, sums],
        compiler_params=pltpu.CompilerParams(vmem_limit_bytes=VMEM),
        cost_estimate=pl.CostEstimate(
            flops=int(1e10), bytes_accessed=int(1.2e7), transcendentals=int(1e6)
        ),
        name="experts",
    )(ids, keep, got, expert_in, expert_out)


def spread_groups(
    ids_ref, middle_ref, normed2_ref, cot_ref, columns_ref, tags_ref, home_ref, got_ref,
    gain_ref, control_ref, out_ref, low_ref, small_ref,
    table, mixed_part, weight_grads, group_sums,
):
    phase, index = pl.program_id(0), pl.program_id(1)
    rows, width = middle_ref.shape
    groups = home_ref.shape[1]
    here = pl.ds(pl.multiple_of(index * rows, rows), rows)

    @pl.when((phase == 0) & (index == 0))
    def _():
        group_sums[...] = jnp.zeros_like(group_sums)
        small_ref[...] = jnp.zeros_like(small_ref)
        own = ids_ref[0] == 0
        for kind in range(2):
            home, got = home_ref[kind], got_ref[kind]
            at = 2 * kind * width
            table[:, at : at + width] = jnp.where(own, home, got)
            table[:, at + width : at + 2 * width] = jnp.where(own, got, home)

    @pl.when(phase == 0)
    def _():
        columns = columns_ref[...]
        lane = lax.broadcasted_iota(jnp.int32, columns.shape, 1)
        token_side = token_marks(columns, groups)
        spread = dot(token_side, table[...])
        cot = cot_ref[...]
        normed2 = normed2_ref[...]
        middle = middle_ref[...]
        cot = cot.astype(F32)
        normed2 = normed2.astype(F32)
        low = columns.astype(BF).astype(F32)
        first, second = low[:, 0:1], low[:, 1:2]
        result = [spread[:, i * width : (i + 1) * width] for i in range(4)]
        out_ref[...] = (middle + first * result[0] + second * result[1]).astype(BF)
        mixed_part[here] = first * result[2] + second * result[3]
        grads = [
            jnp.sum(cot * result[i] + normed2 * result[2 + i], axis=1, keepdims=True)
            for i in range(2)
        ]
        grads = jnp.where(lane == 0, grads[0], jnp.where(lane == 1, grads[1], 0.0))
        pulls = jnp.where(lane < 2, columns * grads, 0.0)
        weight_grads[here] = pulls
        group_sums[...] += dot_exact(group_marks(tags_ref[...], groups), pulls)

    @pl.when(phase == 1)
    def _():
        columns = columns_ref[...]
        central = dot_exact(token_marks(columns, groups), group_sums[...])
        logit_grads = weight_grads[here] - columns * central
        first, second = logit_grads[:, 0:1], logit_grads[:, 1:2]
        control = control_ref[...].astype(F32)
        cot = cot_ref[...].astype(F32)
        normed2 = normed2_ref[...].astype(F32)
        middle = middle_ref[...]
        grad = mixed_part[here] + first * control[0:1] + second * control[1:2]
        scale = lax.rsqrt(jnp.mean(middle * middle, axis=-1, keepdims=True) + eps)
        unit = middle * scale
        pulled = grad * gain_ref[...]
        pulled = scale * (pulled - unit * jnp.mean(pulled * unit, axis=-1, keepdims=True))
        low_ref[...] = (cot + pulled).astype(BF)
        small_ref[0:1] += jnp.sum(grad * unit, axis=0, keepdims=True)
        small_ref[1:2] += jnp.sum(first * normed2, axis=0, keepdims=True)
        small_ref[2:3] += jnp.sum(second * normed2, axis=0, keepdims=True)


def run_spread(ids, middle, normed2, cot, columns, tags, home, got, gain, control):
    tokens, width = middle.shape
    groups = home.shape[1]
    rows = 512
    steps = tokens // rows
    by_block = lambda n: pl.BlockSpec((rows, n), lambda p, b: (b, 0))
    fixed = lambda *shape: pl.BlockSpec(shape, lambda p, b: (0,) * len(shape))
    return call(
        spread_groups,
        "spread_groups",
        (2, steps),
        [
            pl.BlockSpec(memory_space=pltpu.SMEM),
            by_block(width),
            by_block(width),
            by_block(width),
            by_block(WIDTH),
            pl.BlockSpec((8, rows), lambda p, b: (0, b)),
            fixed(*home.shape),
            fixed(*home.shape),
            fixed(1, width),
            fixed(8, width),
        ],
        [
            pl.BlockSpec((rows, width), lambda p, b: (b * (1 - p) + (steps - 1) * p, 0)),
            pl.BlockSpec((rows, width), lambda p, b: (b * p, 0)),
            fixed(8, width),
        ],
        [
            jax.ShapeDtypeStruct((tokens, width), BF),
            jax.ShapeDtypeStruct((tokens, width), BF),
            jax.ShapeDtypeStruct((8, width), F32),
        ],
        8e9,
        2e7,
        scratch_shapes=[
            pltpu.VMEM((groups, 4 * width), BF),
            pltpu.VMEM((tokens, width), F32),
            pltpu.VMEM((tokens, WIDTH), F32),
            pltpu.VMEM((groups, WIDTH), F32),
        ],
    )(ids, middle, normed2, cot, columns, tags, home, got, gain, control)


def input_rows(x_ref, gain_ref, grad_ref, small_ref, *refs):
    slots = 4
    flats, weights = refs[: -slots - 2], refs[-slots - 2 : -2]
    out_ref, sums_ref = refs[-2:]
    rows = x_ref[...].astype(F32)
    grad = dot_last(
        jnp.concatenate([flat[i] for flat in flats for i in range(flat.shape[0])], axis=1),
        jnp.concatenate([weight[:, : 3 * WIDTH] for weight in weights], axis=1),
    )
    scale = lax.rsqrt(jnp.mean(rows * rows, axis=-1, keepdims=True) + eps)
    unit = rows * scale
    pulled = grad * gain_ref[...]
    pulled = scale * (pulled - unit * jnp.mean(pulled * unit, axis=-1, keepdims=True))
    out_ref[...] = grad_ref[...].astype(F32) + pulled

    @pl.when(pl.program_id(0) == 0)
    def _():
        sums_ref[...] = small_ref[...]

    sums_ref[3:4] += jnp.sum(grad * unit, axis=0, keepdims=True)


def run_input(x, gain, grad, small, flats, weights):
    tokens, width = x.shape
    rows = 512
    by_block = lambda n: pl.BlockSpec((rows, n), lambda s: (s, 0))
    return call(
        input_rows,
        "input_rows",
        (tokens // rows,),
        [by_block(width), whole(1, width), by_block(width), whole(8, width)]
        + [
            pl.BlockSpec((flat.shape[0], rows, 3 * WIDTH), lambda s: (0, s, 0)) for flat in flats
        ]
        + [whole(width, 4 * WIDTH)] * len(weights),
        [by_block(width), whole(8, width)],
        [jax.ShapeDtypeStruct((tokens, width), F32), jax.ShapeDtypeStruct((8, width), F32)],
        1,
        1,
        vmem=FULL_VMEM,
    )(x, gain, grad, small, *flats, *weights)


def join_own(ids_ref, own_ref, one_ref, two_ref, kept_ref, sent_ref):
    half = kept_ref.shape[0]
    for index in range(2 * half):
        place = jnp.bitwise_xor(index, ids_ref[4])
        total = own_ref[0, place] + one_ref[place].astype(F32) + two_ref[place].astype(F32)
        ref = kept_ref if index < half else sent_ref
        ref[index % half] = total.astype(BF)


def run_join(ids, own, one, two):
    _, n, rows, width = own.shape
    vmem = pl.BlockSpec(memory_space=pltpu.VMEM)
    return call(
        join_own,
        "join_own",
        (),
        [pl.BlockSpec(memory_space=pltpu.SMEM)] + [vmem] * 3,
        [vmem] * 2,
        [jax.ShapeDtypeStruct((n // 2, rows, width), BF)] * 2,
        1,
        1,
    )(ids, own, one, two)


def open_own(ids_ref, low_ref, high_ref, q_ref, k_ref, v_ref, o_ref):
    half = low_ref.shape[0]
    for index, ref in enumerate((q_ref, k_ref, v_ref, o_ref)):
        place = jnp.bitwise_xor(index, ids_ref[4])
        near = low_ref[lax.rem(place, half)].astype(F32)
        far = high_ref[lax.rem(place, half)].astype(F32)
        value = jnp.where(place < half, near, far)
        ref[...] = value if index == 3 else value.T


def run_open(ids, low, high):
    _, rows, width = low.shape
    vmem = pl.BlockSpec(memory_space=pltpu.VMEM)
    return call(
        open_own,
        "open_own",
        (),
        [pl.BlockSpec(memory_space=pltpu.SMEM), vmem, vmem],
        [vmem] * 4,
        [jax.ShapeDtypeStruct((width, rows), F32)] * 3
        + [jax.ShapeDtypeStruct((rows, width), F32)],
        1e6,
        2e6,
    )(ids, low, high)


def open_experts(ids_ref, *refs):
    in_ref, out_ref = refs[-2:]
    step = pl.program_id(1)
    own = pl.program_id(0) == ids_ref[0]
    rows = out_ref.shape[1]

    def store(index, piece):
        at = sum(SPLIT[:index])
        piece = piece.astype(F32)
        for low, high in ((0, rows), (rows, 2 * rows)):
            start, stop = max(at, low), min(at + piece.shape[0], high)
            if start >= stop:
                continue
            part = piece[start - at : stop - at]
            if low == 0:
                out_ref[0, start:stop] = part
            else:
                in_ref[0, start - low : stop - low] = part[:, :rows]
                in_ref[0, start - low + rows : stop - low + rows] = part[:, rows:]

    for index in range(3):
        place = jnp.bitwise_xor(step, ids_ref[index + 1])
        near = place < 4
        spot = lax.rem(place, 4)
        for which, ref in enumerate(refs[4 * index : 4 * index + 4]):
            fits = near if which % 2 == 0 else jnp.logical_not(near)
            side = own if which < 2 else jnp.logical_not(own)

            @pl.when(fits & side)
            def _():
                store(index, ref[spot])


def run_open_experts(ids, parts, shape_in, shape_out):
    experts, width, hidden = shape_in
    steps = 8
    wide = hidden // steps
    args = [array for part in parts for array in part]
    return pl.pallas_call(
        open_experts,
        grid_spec=pltpu.PrefetchScalarGridSpec(
            num_scalar_prefetch=1,
            grid=(experts, steps),
            in_specs=[pl.BlockSpec(array.shape, lambda e, f, ids: (0, 0, 0)) for array in args],
            out_specs=[
                pl.BlockSpec((1, width, wide), lambda e, f, ids: (e, 0, f)),
                pl.BlockSpec((1, wide, width), lambda e, f, ids: (e, f, 0)),
            ],
        ),
        out_shape=[jax.ShapeDtypeStruct(shape_in, F32), jax.ShapeDtypeStruct(shape_out, F32)],
        compiler_params=pltpu.CompilerParams(vmem_limit_bytes=VMEM),
        cost_estimate=pl.CostEstimate(flops=10**6, bytes_accessed=3 * 10**7, transcendentals=0),
        name="open_experts",
    )(ids, *args)


def tie(*values):
    return lax.optimization_barrier(values)


def build(mesh):
    n_head, n_batch = mesh.shape["head"], mesh.shape["batch"]
    head_bits = [("head", 1 << i) for i in range(n_head.bit_length() - 1)]
    batch_bits = [("batch", 1 << i) for i in range(n_batch.bit_length() - 1)]
    pair, across = head_bits
    first_batch, second_batch, *last_batch = batch_bits
    orders = [
        (across, first_batch, second_batch),
        (first_batch, second_batch, across),
        (second_batch, across, first_batch),
    ]

    def swap(value, step):
        axis, bit = step
        return lax.ppermute(value, axis, [(i, i ^ bit) for i in range(mesh.shape[axis])])

    def bit_of(step):
        axis, bit = step
        return (lax.axis_index(axis) // bit) % 2

    def number(steps):
        return functools.reduce(lambda value, step: 2 * value + bit_of(step), steps, 0)

    def add(kept, got):
        return (kept.astype(F32) + got.astype(F32)).astype(BF)

    def local(
        inputs,
        attn_gain,
        query_weight,
        key_weight,
        value_weight,
        output_weight,
        ffn_gain,
        controller,
        expert_in,
        expert_out,
        group_ids,
        live_mask,
        cotangent,
    ):
        tokens_here, width = inputs.shape
        sequences = tokens_here // LENGTH
        ids = jnp.stack(
            [bit_of(pair)]
            + [number(order) for order in orders]
            + [number((first_batch, second_batch))]
        ).astype(jnp.int32)
        w0 = run_pack(query_weight, key_weight, value_weight, output_weight)
        w2 = swap(w0, across)
        w1 = swap(w0, pair)
        normed, *saved_a = run_forward_first(inputs, attn_gain[None], [w0, w1])
        w2, normed = tie(w2, normed)
        w3 = swap(w2, pair)
        weights = [w0, w1, w2, w3]
        control = jnp.pad(controller, ((0, 0), (0, WIDTH - controller.shape[1])))
        *saved_b, middle, normed2, logits = run_forward_last(
            normed, inputs, saved_a[3], ffn_gain[None], control, weights
        )

        blank = jnp.zeros((1, tokens_here), F32)
        tags = jnp.concatenate(
            [blank, blank, group_ids.astype(F32)[None], live_mask.astype(F32)[None]] + [blank] * 4,
            axis=0,
        )
        columns, keep, send = run_gather(ids, logits, normed2, cotangent, tags)
        *parts, home, away = run_experts(ids, keep, swap(send, pair), expert_in, expert_out)
        home_got = swap(away, pair)
        kept, sent = parts[:3], parts[3:]
        got = [swap(part, order[0]) for part, order in zip(sent, orders)]

        def send_half(blocks, step):
            half = blocks.shape[0] // 2
            return blocks[:half], swap(blocks[half:], step)

        layer_out, middle_low, small = run_spread(
            ids,
            middle,
            normed2,
            cotangent,
            columns,
            tags,
            home,
            home_got,
            ffn_gain[None],
            jnp.pad(controller.T, ((0, 8 - controller.shape[1]), (0, 0))),
        )

        def backward(slots, low, first=0, count=sequences, earlier=None):
            saved, index = (saved_a, slots[0]) if slots[0] < 2 else (saved_b, slots[0] - 2)
            return run_backward(
                saved, index, low, [weights[i] for i in slots], normed, first, count, earlier
            )

        half = sequences // 2

        def next_stage(kept, got, low, mark, stage):
            *got, mark = tie(*got, mark)
            blocks = [add(a, b) for a, b in zip(kept, got)]
            if stage < 3:
                kept = [block[: block.shape[0] // 2] for block in blocks]
                sent = [block[block.shape[0] // 2 :] for block in blocks]
            else:
                kept = sent = blocks
            *sent, low = tie(*sent, low)
            steps = [order[stage] if stage < 3 else last_batch[stage - 3] for order in orders]
            return kept, [swap(block, step) for block, step in zip(sent, steps)], low, mark

        low = middle_low
        flat3, sum3 = backward([3], low, 0, half)
        kept, got, low, sum3 = next_stage(kept, got, low, sum3, 1)
        flat3, sum3 = backward([3], low, half, sequences - half, (flat3, sum3))
        third_got = swap(sum3.astype(BF), pair)
        flat2, sum2 = backward([2], low, 0, half)
        kept, got, low, sum2 = next_stage(kept, got, low, sum2, 2)
        flat2, sum2 = backward([2], low, half, sequences - half, (flat2, sum2))
        kept, got, low, sum2 = next_stage(kept, got, low, sum2, 3)
        for stage in range(4, 3 + len(last_batch)):
            kept, got, low, sum2 = next_stage(kept, got, low, sum2, stage)
        second = (sum2[0] + third_got[0].astype(F32)).astype(BF)
        second, low = tie(second, low)
        second_got = swap(second, across)
        flat10, sum10 = backward([1, 0], low)

        *got, second_got, sum10, low = tie(*got, second_got, sum10, low)
        first_got = swap(sum10[0].astype(BF), pair)
        blocks = [add(a, b) for a, b in zip(kept, got)]
        *blocks, low = tie(*blocks, low)
        got = [swap(block, order[2]) for block, order in zip(blocks, orders)]
        own_kept, own_sent = run_join(ids, sum10[1:], second_got, first_got)
        own_sent, low = tie(own_sent, low)
        own_got = swap(own_sent, first_batch)
        input_grad, small = run_input(
            inputs, attn_gain[None], low, small, [flat10, flat2, flat3], [w1, w0, w2, w3]
        )
        *got, own_got, small = tie(*got, own_got, small)
        own = add(own_kept, own_got)
        own_kept, own_sent = own[: own.shape[0] // 2], own[own.shape[0] // 2 :]

        def widen(blocks, stage):
            return [swap(block, order[stage]) for block, order in zip(blocks, orders)]

        def join(blocks, got):
            return [jnp.concatenate(pair_of, axis=0) for pair_of in zip(blocks, got)]

        small_steps = head_bits + batch_bits

        def small_stage(small, got, index):
            if index >= len(small_steps):
                return small, None
            small = small if got is None else small + got
            return small, swap(small, small_steps[index])

        blocks = join(blocks, got)
        got = widen(blocks, 1)
        own_got = swap(own_sent, second_batch)
        small, small_got = small_stage(small, None, 0)
        own_got, small_got = tie(own_got, small_got)
        own = add(own_kept, own_got)
        own_got = swap(own, last_batch[0]) if last_batch else jnp.zeros_like(own)
        small, small_got = small_stage(small, small_got, 1)
        *got, own_got, small_got = tie(*got, own_got, small_got)

        blocks = join(blocks, got)
        far = widen(blocks, 0)
        own = add(own, own_got)
        for step in last_batch[1:]:
            own = add(own, swap(own, step))
        own_got = swap(own, second_batch)
        small, small_got = small_stage(small, small_got, 2)
        blocks_other = [swap(block, pair) for block in blocks]
        own_got, small_got, *blocks_other = tie(own_got, small_got, *blocks_other)

        own = jnp.concatenate([own, own_got], axis=0)
        own_got = swap(own, first_batch)
        for index in range(3, len(small_steps)):
            small, small_got = small_stage(small, small_got, index)
        small = small + small_got
        *far, own_got, small = tie(*far, own_got, small)

        far_other = [swap(block, pair) for block in far]
        query_grad, key_grad, value_grad, output_grad = run_open(ids, own, own_got)
        expert_in_grad, expert_out_grad = run_open_experts(
            ids,
            [list(group) for group in zip(blocks, far, blocks_other, far_other)],
            expert_in.shape,
            expert_out.shape,
        )
        return (
            layer_out,
            input_grad,
            small[3],
            query_grad,
            key_grad,
            value_grad,
            output_grad,
            small[0],
            small[1:3].T,
            expert_in_grad,
            expert_out_grad,
        )

    return local


def solution(mesh):
    in_specs = (
        P(("batch", "head"), None),
        P(),
        P(None, "head"),
        P(None, "head"),
        P(None, "head"),
        P("head", None),
        P(),
        P(),
        P(),
        P(),
        P(("batch", "head")),
        P(("batch", "head")),
        P(("batch", "head"), None),
    )
    out_specs = (
        P(("batch", "head"), None),
        P(("batch", "head"), None),
        P(),
        P(None, "head"),
        P(None, "head"),
        P(None, "head"),
        P("head", None),
        P(),
        P(),
        P(),
        P(),
    )
    return jax.shard_map(
        build(mesh), mesh=mesh, in_specs=in_specs, out_specs=out_specs, check_vma=False
    )
```

```python
import functools

import jax
import jax.numpy as jnp
from jax import lax
from jax.experimental import pallas as pl
from jax.experimental.pallas import tpu as pltpu
from jax.sharding import PartitionSpec as P

HD = 64
LENGTH = 1024
WIDTH = 128
BF = jnp.bfloat16
F32 = jnp.float32
LOG2E = 1.4426950408889634
LN2 = 0.6931471805599453
VMEM = 20 * 2**20
FULL_VMEM = 56 * 2**20

eps = 1e-06
last_dims = (((1,), (1,)), ((), ()))
first_dims = (((0,), (0,)), ((), ()))


def dot(left, right):
    return jnp.dot(left, right, preferred_element_type=F32)


def dot_last(left, right):
    return lax.dot_general(left, right, last_dims, preferred_element_type=F32)


def dot_first(left, right):
    return lax.dot_general(left, right, first_dims, preferred_element_type=F32)


def split3(value):
    high = value.astype(BF)
    rest = value - high.astype(F32)
    mid = rest.astype(BF)
    low = (rest - mid.astype(F32)).astype(BF)
    return high, mid, low


def call(
    body, name, grid, in_specs, out_specs, out_shape, flops, moved, exps=0, vmem=VMEM, **extra
):
    return pl.pallas_call(
        body,
        grid=grid,
        in_specs=in_specs,
        out_specs=out_specs,
        out_shape=out_shape,
        compiler_params=pltpu.CompilerParams(vmem_limit_bytes=vmem),
        cost_estimate=pl.CostEstimate(
            flops=int(flops), bytes_accessed=int(moved), transcendentals=int(exps)
        ),
        name=name,
        **extra,
    )


def row_block(columns):
    return pl.BlockSpec((LENGTH, columns), lambda s: (s, 0))


def whole(*shape):
    return pl.BlockSpec(shape, lambda s: (0,) * len(shape))


def head_lanes(rows, head):
    lane = lax.broadcasted_iota(jnp.int32, (rows, WIDTH), 1)
    mine = (lane < HD) if head == 0 else (lane >= HD)
    return lane, mine, HD if head == 0 else 0


def with_extra(mine, lane, other, values, extra):
    high, mid, low = split3(extra)
    filler = jnp.zeros_like(values)
    for place, part in ((2, low), (1, mid), (0, high)):
        filler = jnp.where(lane == other + place, part, filler)
    return jnp.where(mine, values, filler)


def twice(mine, values):
    return jnp.where(mine, values, jnp.roll(values, HD, axis=1))


def scaled_queries(mine, q):
    long = q.astype(F32) * (HD**-0.5 * LOG2E)
    high = long.astype(BF)
    low = (long - high.astype(F32)).astype(BF)
    return jnp.where(mine, high, jnp.roll(low, HD, axis=1))


def attend(normed, weights, q_ref, k_ref, v_ref, logsum_ref, ctx_ref):
    block = 256
    r = lax.broadcasted_iota(jnp.int32, (WIDTH, WIDTH), 0)
    c = lax.broadcasted_iota(jnp.int32, (WIDTH, WIDTH), 1)
    same_head = jnp.where((r < HD) == (c < HD), 1.0, 0.0).astype(BF)

    def most(values):
        long = values.astype(F32)
        return jnp.max(dot((long * long).astype(BF), same_head), axis=0, keepdims=True)

    bounds = []
    for slot, weight in enumerate(weights):
        qkv = dot(normed, weight)
        q = qkv[:, :WIDTH].astype(BF)
        k = qkv[:, WIDTH : 2 * WIDTH].astype(BF)
        q_ref[slot] = q
        k_ref[slot] = k
        v_ref[slot] = qkv[:, 2 * WIDTH :].astype(BF)
        bounds.append(most(q) * most(k))
    bound = jnp.max(functools.reduce(jnp.maximum, bounds))

    def finish(slot, head, here, out, peak):
        lane_b, mine_b, other = head_lanes(block, head)
        total = out[:, other : other + 1]
        logsum = jnp.log2(total) + peak
        context = (out * (1.0 / total)).astype(BF)
        marks = with_extra(jnp.full_like(mine_b, False), lane_b, head * HD, context, logsum)
        if head == 1:
            context = jnp.where(mine_b, context, ctx_ref[slot, here])
            marks = jnp.where(mine_b, marks, logsum_ref[slot, here])
        ctx_ref[slot, here] = context
        logsum_ref[slot, here] = marks

    def head_keys(slot, head):
        lane, mine, other = head_lanes(LENGTH, head)
        vh = jnp.where(mine, v_ref[slot], (lane == other).astype(F32).astype(BF))
        return twice(mine, k_ref[slot]), vh

    def rows_small(slot, head):
        kh, vh = head_keys(slot, head)
        qh = scaled_queries(head_lanes(LENGTH, head)[1], q_ref[slot])
        for start in range(0, LENGTH, block):
            here = slice(start, start + block)
            queries = qh[here]
            scores = []
            for at in range(0, start + block, block):
                part = dot_last(queries, kh[at : at + block])
                if at == start:
                    r = lax.broadcasted_iota(jnp.int32, (block, block), 0)
                    c = lax.broadcasted_iota(jnp.int32, (block, block), 1)
                    part = jnp.where(c <= r, part, -1e30)
                scores.append(part)
            out = 0.0
            for index, part in enumerate(scores):
                out = out + dot(
                    jnp.exp2(part).astype(BF), vh[index * block : (index + 1) * block]
                )
            finish(slot, head, here, out, 0.0)

    def rows_large(slot, head):
        @pl.loop(0, LENGTH // block)
        def _(index):
            kh, vh = head_keys(slot, head)
            here = pl.ds(pl.multiple_of(index * block, block), block)
            queries = scaled_queries(head_lanes(block, head)[1], q_ref[slot, here])
            scores = dot_last(queries, kh)
            r = lax.broadcasted_iota(jnp.int32, scores.shape, 0) + index * block
            c = lax.broadcasted_iota(jnp.int32, scores.shape, 1)
            scores = jnp.where(c <= r, scores, -1e30)
            peak = jnp.max(scores, axis=1, keepdims=True)
            finish(slot, head, here, dot(jnp.exp2(scores - peak).astype(BF), vh), peak)

    small = bound * (HD**-0.5 * LOG2E) ** 2 * 1.1 < 1e4

    @pl.when(small)
    def _():
        for slot in range(len(weights)):
            for head in range(2):
                rows_small(slot, head)

    @pl.when(jnp.logical_not(small))
    def _():
        for head in range(2):

            @pl.loop(0, len(weights))
            def _(slot):
                rows_large(slot, head)


def norm_rows(rows):
    return rows * lax.rsqrt(jnp.mean(rows * rows, axis=-1, keepdims=True) + eps)


def pack_weights(q_ref, k_ref, v_ref, o_ref, packed_ref):
    for index, ref in enumerate((q_ref, k_ref, v_ref)):
        packed_ref[:, index * WIDTH : (index + 1) * WIDTH] = ref[...]
    packed_ref[:, 3 * WIDTH :] = o_ref[...].T


def run_pack(q, k, v, o):
    width = q.shape[0]
    return call(
        pack_weights,
        "pack_weights",
        (),
        [pl.BlockSpec(memory_space=pltpu.VMEM)] * 4,
        pl.BlockSpec(memory_space=pltpu.VMEM),
        jax.ShapeDtypeStruct((width, 4 * WIDTH), BF),
        1e6,
        2e6,
        vmem=FULL_VMEM,
    )(q, k, v, o)


def forward_first(x_ref, gain_ref, *refs):
    slots = len(refs) - 6
    normed_ref, *saved = refs[slots:]
    normed = (norm_rows(x_ref[...].astype(F32)) * gain_ref[...]).astype(BF)
    normed_ref[...] = normed
    attend(normed, [ref[:, : 3 * WIDTH] for ref in refs[:slots]], *saved)


def forward_last(normed_ref, x_ref, ctx_in_ref, ffn_gain_ref, control_ref, *refs):
    slots = len(refs) - 8
    weights = refs[:slots]
    *saved, middle_ref, normed2_ref, logits_ref = refs[slots:]
    ctx_ref = saved[-1]
    normed = normed_ref[...]
    before = ctx_in_ref.shape[0]
    attend(normed, [ref[:, : 3 * WIDTH] for ref in weights[before:]], *saved)
    context = jnp.concatenate(
        [ctx_in_ref[i] for i in range(before)] + [ctx_ref[i] for i in range(slots - before)],
        axis=1,
    )
    flipped = jnp.concatenate([ref[:, 3 * WIDTH :] for ref in weights], axis=1)
    middle = x_ref[...].astype(F32) + dot_last(context, flipped)
    middle_ref[...] = middle
    normed2 = (norm_rows(middle) * ffn_gain_ref[...]).astype(BF)
    normed2_ref[...] = normed2
    logits_ref[...] = dot(normed2, control_ref[...])


def slot_outputs(slots, tokens):
    per = pl.BlockSpec((slots, LENGTH, WIDTH), lambda s: (0, s, 0))
    return [per] * 5, [jax.ShapeDtypeStruct((slots, tokens, WIDTH), BF)] * 5


def run_forward_first(x, gain, weights):
    tokens, width = x.shape
    specs, shapes = slot_outputs(len(weights), tokens)
    return call(
        forward_first,
        "attention_forward_first",
        (tokens // LENGTH,),
        [row_block(width), whole(1, width)] + [whole(width, 4 * WIDTH)] * len(weights),
        [row_block(width)] + specs,
        [jax.ShapeDtypeStruct((tokens, width), BF)] + shapes,
        1.5e10,
        1e7,
        1e7,
        vmem=FULL_VMEM,
    )(x, gain, *weights)


def run_forward_last(normed, x, ctx, ffn_gain, control, weights):
    tokens, width = x.shape
    specs, shapes = slot_outputs(len(weights) - ctx.shape[0], tokens)
    ctx_spec = pl.BlockSpec((ctx.shape[0], LENGTH, WIDTH), lambda s: (0, s, 0))
    return call(
        forward_last,
        "attention_forward_last",
        (tokens // LENGTH,),
        [row_block(width), row_block(width), ctx_spec, whole(1, width), whole(width, WIDTH)]
        + [whole(width, 4 * WIDTH)] * len(weights),
        specs + [row_block(width), row_block(width), row_block(WIDTH)],
        shapes
        + [
            jax.ShapeDtypeStruct((tokens, width), F32),
            jax.ShapeDtypeStruct((tokens, width), BF),
            jax.ShapeDtypeStruct((tokens, WIDTH), F32),
        ],
        1.5e10,
        1e7,
        1e7,
        vmem=FULL_VMEM,
    )(normed, x, ctx, ffn_gain, control, *weights)


def backward_items(
    slots, items_ref, q_ref, k_ref, v_ref, logsum_ref, ctx_ref, ml_ref, normed_ref, *refs
):
    dqkv_ref, dw_ref = refs[-2:]
    item = pl.program_id(0)
    weight = refs[0][...]
    for index in range(1, slots):
        weight = jnp.where(items_ref[0, item] == index, refs[index][...], weight)
    block = 256
    ml = ml_ref[...]
    ctx = ctx_ref[0]
    d_out = dot(ml, weight).astype(BF)
    product = d_out.astype(F32) * ctx.astype(F32)
    q = q_ref[0]
    k = k_ref[0]
    v = v_ref[0]
    logsum = logsum_ref[0]
    k_flip = k.T
    dks, dvs, dqs = [], [], []
    for head in range(2):
        lane, mine, other = head_lanes(LENGTH, head)
        minus = jnp.where((lane >= other) & (lane < other + 3), -1.0, 0.0).astype(BF)
        minus_own = jnp.where((lane >= HD - other) & (lane < HD - other + 3), -1.0, 0.0).astype(BF)
        central = jnp.sum(jnp.where(mine, product, 0.0), axis=1, keepdims=True)
        d_all = with_extra(mine, lane, other, d_out, central)
        v_all = jnp.where(mine, v, minus)
        k_all = jnp.concatenate([twice(mine, k), minus_own], axis=1)
        q_scaled = scaled_queries(mine, q)
        q_all = jnp.concatenate([q_scaled, logsum], axis=1)
        dq = [0.0] * (LENGTH // block)
        dk, dv = [], []
        for at in range(0, LENGTH, block):
            keys = k_all[at : at + block]
            values = v_all[at : at + block]
            flipped = k_flip[head * HD : (head + 1) * HD, at : at + block]
            probs = jnp.exp2(dot_last(keys, q_all[at:]))
            r = lax.broadcasted_iota(jnp.int32, (block, block), 0)
            c = lax.broadcasted_iota(jnp.int32, (block, block), 1)
            corner = jnp.where(r <= c, probs[:, :block], 0.0)
            probs = corner if at + block == LENGTH else jnp.concatenate([corner, probs[:, block:]], axis=1)
            d_scores = (probs * dot_last(values, d_all[at:])).astype(BF)
            dv.append(dot(probs.astype(BF), d_all[at:]))
            dk.append(dot(d_scores, q_scaled[at:]))
            part = dot(flipped, d_scores)
            for start in range(at, LENGTH, block):
                dq[start // block] = dq[start // block] + part[:, start - at : start - at + block]
        dk = jnp.concatenate(dk, axis=0)
        dks.append(dk + jnp.roll(dk, HD, axis=1))
        dvs.append(jnp.concatenate(dv, axis=0))
        dqs.append(jnp.concatenate(dq, axis=1))
    lane, mine, _ = head_lanes(LENGTH, 0)
    dk = (jnp.where(mine, dks[0], dks[1]) * LN2).astype(BF)
    dv = jnp.where(mine, dvs[0], dvs[1]).astype(BF)
    dq_flip = (jnp.concatenate(dqs, axis=0) * HD**-0.5).astype(BF)
    dqkv_ref[0, :, :WIDTH] = dq_flip.T
    dqkv_ref[0, :, WIDTH : 2 * WIDTH] = dk
    dqkv_ref[0, :, 2 * WIDTH :] = dv
    dw = dot(jnp.concatenate([dq_flip, dk.T, dv.T], axis=0), normed_ref[...])
    dwo = dot_first(ctx, ml)
    parts = [dw[:WIDTH], dw[WIDTH : 2 * WIDTH], dw[2 * WIDTH :], dwo]
    adds = items_ref[2, item]
    earlier = refs[slots + 1] if len(refs) > slots + 2 else None

    @pl.when(adds == 0)
    def _():
        for index, part in enumerate(parts):
            dw_ref[0, index] = part

    @pl.when(adds == 1)
    def _():
        for index, part in enumerate(parts):
            dw_ref[0, index] += part

    if earlier is not None:

        @pl.when(adds == 2)
        def _():
            for index, part in enumerate(parts):
                dw_ref[0, index] = earlier[0, index] + part


def run_backward(saved, ml, weights, normed, items, done=(), earlier=None, flops=6e9):
    tokens, width = ml.shape
    slots = len(weights)
    table = [[], [], []]
    for index, (slot, sequence) in enumerate(items):
        seen = [one for one in items[:index] if one[0] == slot]
        before = [one for one in done if one[0] == slot]
        table[0].append(slot)
        table[1].append(sequence)
        table[2].append(1 if seen else 2 if before else 0)
    table = jnp.array(table, jnp.int32)
    per = pl.BlockSpec((1, LENGTH, WIDTH), lambda i, t: (t[0, i], t[1, i], 0))
    rows = pl.BlockSpec((LENGTH, width), lambda i, t: (t[1, i], 0))
    sums = pl.BlockSpec((1, 4, WIDTH, width), lambda i, t: (t[0, i], 0, 0, 0))
    args = [table, *saved, ml, normed, *weights]
    in_specs = [*([per] * 5), rows, rows]
    in_specs += [pl.BlockSpec((width, WIDTH), lambda i, t: (0, 3))] * slots
    aliases = {}
    if earlier is not None:
        aliases = {len(args): 0, len(args) + 1: 1}
        args += list(earlier)
        in_specs += [pl.BlockSpec(memory_space=pl.ANY), sums]
    return pl.pallas_call(
        functools.partial(backward_items, slots),
        grid_spec=pltpu.PrefetchScalarGridSpec(
            num_scalar_prefetch=1,
            grid=(len(items),),
            in_specs=in_specs,
            out_specs=[pl.BlockSpec((1, LENGTH, 3 * WIDTH), lambda i, t: (t[0, i], t[1, i], 0)), sums],
        ),
        out_shape=[
            jax.ShapeDtypeStruct((slots, tokens, 3 * WIDTH), BF),
            jax.ShapeDtypeStruct((slots, 4, WIDTH, width), F32),
        ],
        input_output_aliases=aliases,
        compiler_params=pltpu.CompilerParams(vmem_limit_bytes=VMEM),
        cost_estimate=pl.CostEstimate(
            flops=int(flops * len(items)), bytes_accessed=1, transcendentals=0
        ),
        name="attention_backward",
    )(*args)


def group_marks(tags, groups):
    id_row, live_row = tags[2:3], tags[3:4]
    slot = lax.broadcasted_iota(jnp.int32, (groups, tags.shape[1]), 0).astype(F32)
    return jnp.where((slot == id_row) & (live_row > 0), 1.0, 0.0).astype(BF)


def token_marks(columns, groups):
    slot = lax.broadcasted_iota(jnp.int32, (columns.shape[0], groups), 1).astype(F32)
    return jnp.where((slot == columns[:, 2:3]) & (columns[:, 3:4] > 0), 1.0, 0.0).astype(BF)


def dot_exact(marks, values):
    return functools.reduce(jnp.add, [dot(marks, part) for part in split3(values)])


def gather_groups(ids_ref, logits_ref, normed2_ref, cot_ref, tags_ref, columns_ref, keep_ref, send_ref):
    tokens = normed2_ref.shape[0]
    groups = keep_ref.shape[1]
    tags = tags_ref[...]
    blank = jnp.zeros((WIDTH - tags.shape[0], tokens), F32)
    turned = jnp.concatenate([tags, blank], axis=0).T
    marks = group_marks(tags, groups)
    token_side = token_marks(turned, groups)
    live = turned[:, 3:4]
    expo = jnp.exp(logits_ref[...]) * live
    totals = dot_exact(marks, expo)
    weights = expo / (dot_exact(token_side, totals) + (1.0 - live))
    lane = lax.broadcasted_iota(jnp.int32, weights.shape, 1)
    columns_ref[...] = jnp.where(lane < 2, weights, turned)
    rows = weights.T[:8].astype(BF)
    own = ids_ref[0] == 0
    normed2 = normed2_ref[...]
    cot = cot_ref[...]
    for ref, pick in ((keep_ref, own), (send_ref, jnp.logical_not(own))):
        assign = marks * jnp.where(pick, rows[0:1].astype(F32), rows[1:2].astype(F32)).astype(BF)
        ref[0] = dot(assign, normed2).astype(BF)
        ref[1] = dot(assign, cot).astype(BF)


def run_gather(ids, logits, normed2, cot, tags):
    tokens, width = normed2.shape
    groups = tokens // 8
    vmem = pl.BlockSpec(memory_space=pltpu.VMEM)
    sums = jax.ShapeDtypeStruct((2, groups, width), BF)
    return call(
        gather_groups,
        "gather_groups",
        (),
        [pl.BlockSpec(memory_space=pltpu.SMEM)] + [vmem] * 4,
        [vmem] * 3,
        [jax.ShapeDtypeStruct((tokens, WIDTH), F32), sums, sums],
        4e9,
        8e6,
    )(ids, logits, normed2, cot, tags)


def gelu_both(x):
    inner = 0.7978845608028654
    cubic = 0.044715
    square = x * x
    bent = jnp.tanh(inner * x * (1.0 + cubic * square))
    half = 0.5 * (1.0 + bent)
    slope = half + 0.5 * x * (1.0 - bent * bent) * (inner * (1.0 + 3.0 * cubic * square))
    return x * half, slope


SPLIT = (176, 176, 160)


def expert_step(
    ids_ref, keep_ref, got_ref, in_ref, out_ref, *refs
):
    kept_refs, sent_refs = refs[:3], refs[3:6]
    home_ref, away_ref, mixed_flip, result, mixed_grad = refs[6:]
    step = pl.program_id(0)
    groups = keep_ref.shape[1]
    mixed = jnp.concatenate([keep_ref[0], got_ref[0]], axis=0)
    d_result = jnp.concatenate([keep_ref[1], got_ref[1]], axis=0)

    @pl.when(step == 0)
    def _():
        mixed_flip[...] = mixed.T
        result[...] = jnp.zeros_like(result)
        mixed_grad[...] = jnp.zeros_like(mixed_grad)

    w_in = in_ref[0]
    w_out = out_ref[0]
    active, slope = gelu_both(dot(mixed, w_in))
    active = active.astype(BF)
    d_before = (dot_last(d_result, w_out) * slope).astype(BF)
    result[...] += dot(active, w_out)
    mixed_grad[...] += dot_last(d_before, w_in)
    d_out = dot_first(active, d_result).astype(BF)
    d_in = dot(mixed_flip[...], d_before).astype(BF)
    half = d_in.shape[0] // 2
    block = jnp.concatenate(
        [d_out, jnp.concatenate([d_in[:half], d_in[half:]], axis=1)], axis=0
    )
    at = 0
    for index, rows in enumerate(SPLIT):
        place = jnp.bitwise_xor(step, ids_ref[index + 1])
        piece = block[at : at + rows]
        at += rows

        @pl.when(place < 4)
        def _():
            kept_refs[index][place] = piece

        @pl.when(place >= 4)
        def _():
            sent_refs[index][place - 4] = piece

    @pl.when(step == pl.num_programs(0) - 1)
    def _():
        home_ref[0] = result[:groups].astype(BF)
        home_ref[1] = mixed_grad[:groups].astype(BF)
        away_ref[0] = result[groups:].astype(BF)
        away_ref[1] = mixed_grad[groups:].astype(BF)


def run_experts(ids, keep, got, expert_in, expert_out):
    _, width, hidden = expert_in.shape
    steps = 8
    wide = hidden // steps
    groups = keep.shape[1]
    sums = jax.ShapeDtypeStruct(keep.shape, BF)
    fixed = lambda f, ids: (0, 0, 0)

    halves = [(steps // 2, rows, width) for rows in SPLIT] * 2
    return pl.pallas_call(
        expert_step,
        grid_spec=pltpu.PrefetchScalarGridSpec(
            num_scalar_prefetch=1,
            grid=(steps,),
            in_specs=[
                pl.BlockSpec(keep.shape, fixed),
                pl.BlockSpec(keep.shape, fixed),
                pl.BlockSpec((1, width, wide), lambda f, ids: (ids[0], 0, f)),
                pl.BlockSpec((1, wide, width), lambda f, ids: (ids[0], f, 0)),
            ],
            out_specs=[pl.BlockSpec(shape, fixed) for shape in halves + [keep.shape] * 2],
            scratch_shapes=[
                pltpu.VMEM((width, 2 * groups), BF),
                pltpu.VMEM((2 * groups, width), F32),
                pltpu.VMEM((2 * groups, width), F32),
            ],
        ),
        out_shape=[jax.ShapeDtypeStruct(shape, BF) for shape in halves] + [sums, sums],
        compiler_params=pltpu.CompilerParams(vmem_limit_bytes=VMEM),
        cost_estimate=pl.CostEstimate(
            flops=int(1e10), bytes_accessed=int(1.2e7), transcendentals=int(1e6)
        ),
        name="experts",
    )(ids, keep, got, expert_in, expert_out)


def spread_groups(
    ids_ref, middle_ref, normed2_ref, cot_ref, columns_ref, tags_ref, home_ref, got_ref,
    gain_ref, control_ref, out_ref, low_ref, small_ref,
    table, mixed_part, weight_grads, group_sums,
):
    phase, index = pl.program_id(0), pl.program_id(1)
    rows, width = middle_ref.shape
    groups = home_ref.shape[1]
    here = pl.ds(pl.multiple_of(index * rows, rows), rows)

    @pl.when((phase == 0) & (index == 0))
    def _():
        group_sums[...] = jnp.zeros_like(group_sums)
        small_ref[...] = jnp.zeros_like(small_ref)
        own = ids_ref[0] == 0
        for kind in range(2):
            home, got = home_ref[kind], got_ref[kind]
            at = 2 * kind * width
            table[:, at : at + width] = jnp.where(own, home, got)
            table[:, at + width : at + 2 * width] = jnp.where(own, got, home)

    @pl.when(phase == 0)
    def _():
        columns = columns_ref[...]
        lane = lax.broadcasted_iota(jnp.int32, columns.shape, 1)
        token_side = token_marks(columns, groups)
        spread = dot(token_side, table[...])
        cot = cot_ref[...]
        normed2 = normed2_ref[...]
        middle = middle_ref[...]
        cot = cot.astype(F32)
        normed2 = normed2.astype(F32)
        low = columns.astype(BF).astype(F32)
        first, second = low[:, 0:1], low[:, 1:2]
        result = [spread[:, i * width : (i + 1) * width] for i in range(4)]
        out_ref[...] = (middle + first * result[0] + second * result[1]).astype(BF)
        mixed_part[here] = first * result[2] + second * result[3]
        grads = [
            jnp.sum(cot * result[i] + normed2 * result[2 + i], axis=1, keepdims=True)
            for i in range(2)
        ]
        grads = jnp.where(lane == 0, grads[0], jnp.where(lane == 1, grads[1], 0.0))
        pulls = jnp.where(lane < 2, columns * grads, 0.0)
        weight_grads[here] = pulls
        group_sums[...] += dot_exact(group_marks(tags_ref[...], groups), pulls)

    @pl.when(phase == 1)
    def _():
        columns = columns_ref[...]
        central = dot_exact(token_marks(columns, groups), group_sums[...])
        logit_grads = weight_grads[here] - columns * central
        first, second = logit_grads[:, 0:1], logit_grads[:, 1:2]
        control = control_ref[...].astype(F32)
        cot = cot_ref[...].astype(F32)
        normed2 = normed2_ref[...].astype(F32)
        middle = middle_ref[...]
        grad = mixed_part[here] + first * control[0:1] + second * control[1:2]
        scale = lax.rsqrt(jnp.mean(middle * middle, axis=-1, keepdims=True) + eps)
        unit = middle * scale
        pulled = grad * gain_ref[...]
        pulled = scale * (pulled - unit * jnp.mean(pulled * unit, axis=-1, keepdims=True))
        low_ref[...] = (cot + pulled).astype(BF)
        small_ref[0:1] += jnp.sum(grad * unit, axis=0, keepdims=True)
        small_ref[1:2] += jnp.sum(first * normed2, axis=0, keepdims=True)
        small_ref[2:3] += jnp.sum(second * normed2, axis=0, keepdims=True)


def run_spread(ids, middle, normed2, cot, columns, tags, home, got, gain, control):
    tokens, width = middle.shape
    groups = home.shape[1]
    rows = 512
    steps = tokens // rows
    by_block = lambda n: pl.BlockSpec((rows, n), lambda p, b: (b, 0))
    fixed = lambda *shape: pl.BlockSpec(shape, lambda p, b: (0,) * len(shape))
    return call(
        spread_groups,
        "spread_groups",
        (2, steps),
        [
            pl.BlockSpec(memory_space=pltpu.SMEM),
            by_block(width),
            by_block(width),
            by_block(width),
            by_block(WIDTH),
            pl.BlockSpec((8, rows), lambda p, b: (0, b)),
            fixed(*home.shape),
            fixed(*home.shape),
            fixed(1, width),
            fixed(8, width),
        ],
        [
            pl.BlockSpec((rows, width), lambda p, b: (b * (1 - p) + (steps - 1) * p, 0)),
            pl.BlockSpec((rows, width), lambda p, b: (b * p, 0)),
            fixed(8, width),
        ],
        [
            jax.ShapeDtypeStruct((tokens, width), BF),
            jax.ShapeDtypeStruct((tokens, width), BF),
            jax.ShapeDtypeStruct((8, width), F32),
        ],
        8e9,
        2e7,
        scratch_shapes=[
            pltpu.VMEM((groups, 4 * width), BF),
            pltpu.VMEM((tokens, width), F32),
            pltpu.VMEM((tokens, WIDTH), F32),
            pltpu.VMEM((groups, WIDTH), F32),
        ],
    )(ids, middle, normed2, cot, columns, tags, home, got, gain, control)


def input_rows(x_ref, gain_ref, grad_ref, small_ref, *refs):
    slots = 4
    flats, weights = refs[: -slots - 2], refs[-slots - 2 : -2]
    out_ref, sums_ref = refs[-2:]
    rows = x_ref[...].astype(F32)
    grad = dot_last(
        jnp.concatenate([flat[i] for flat in flats for i in range(flat.shape[0])], axis=1),
        jnp.concatenate([weight[:, : 3 * WIDTH] for weight in weights], axis=1),
    )
    scale = lax.rsqrt(jnp.mean(rows * rows, axis=-1, keepdims=True) + eps)
    unit = rows * scale
    pulled = grad * gain_ref[...]
    pulled = scale * (pulled - unit * jnp.mean(pulled * unit, axis=-1, keepdims=True))
    out_ref[...] = grad_ref[...].astype(F32) + pulled

    @pl.when(pl.program_id(0) == 0)
    def _():
        sums_ref[...] = small_ref[...]

    sums_ref[3:4] += jnp.sum(grad * unit, axis=0, keepdims=True)


def run_input(x, gain, grad, small, flats, weights):
    tokens, width = x.shape
    rows = 512
    by_block = lambda n: pl.BlockSpec((rows, n), lambda s: (s, 0))
    return call(
        input_rows,
        "input_rows",
        (tokens // rows,),
        [by_block(width), whole(1, width), by_block(width), whole(8, width)]
        + [
            pl.BlockSpec((flat.shape[0], rows, 3 * WIDTH), lambda s: (0, s, 0)) for flat in flats
        ]
        + [whole(width, 4 * WIDTH)] * len(weights),
        [by_block(width), whole(8, width)],
        [jax.ShapeDtypeStruct((tokens, width), F32), jax.ShapeDtypeStruct((8, width), F32)],
        1,
        1,
        vmem=FULL_VMEM,
    )(x, gain, grad, small, *flats, *weights)


def join_own(ids_ref, own_ref, one_ref, two_ref, kept_ref, sent_ref):
    half = kept_ref.shape[0]
    for index in range(2 * half):
        place = jnp.bitwise_xor(index, ids_ref[4])
        total = own_ref[0, place] + one_ref[place].astype(F32) + two_ref[place].astype(F32)
        ref = kept_ref if index < half else sent_ref
        ref[index % half] = total.astype(BF)


def run_join(ids, own, one, two):
    _, n, rows, width = own.shape
    vmem = pl.BlockSpec(memory_space=pltpu.VMEM)
    return call(
        join_own,
        "join_own",
        (),
        [pl.BlockSpec(memory_space=pltpu.SMEM)] + [vmem] * 3,
        [vmem] * 2,
        [jax.ShapeDtypeStruct((n // 2, rows, width), BF)] * 2,
        1,
        1,
    )(ids, own, one, two)


def open_own(ids_ref, low_ref, high_ref, q_ref, k_ref, v_ref, o_ref):
    half = low_ref.shape[0]
    for index, ref in enumerate((q_ref, k_ref, v_ref, o_ref)):
        place = jnp.bitwise_xor(index, ids_ref[4])
        near = low_ref[lax.rem(place, half)].astype(F32)
        far = high_ref[lax.rem(place, half)].astype(F32)
        value = jnp.where(place < half, near, far)
        ref[...] = value if index == 3 else value.T


def run_open(ids, low, high):
    _, rows, width = low.shape
    vmem = pl.BlockSpec(memory_space=pltpu.VMEM)
    return call(
        open_own,
        "open_own",
        (),
        [pl.BlockSpec(memory_space=pltpu.SMEM), vmem, vmem],
        [vmem] * 4,
        [jax.ShapeDtypeStruct((width, rows), F32)] * 3
        + [jax.ShapeDtypeStruct((rows, width), F32)],
        1e6,
        2e6,
    )(ids, low, high)


def part_regions(index, half):
    start = sum(SPLIT[:index])
    regions = []
    for low, high, output in ((0, half, 1), (half, 2 * half, 0)):
        first, last = max(start, low), min(start + SPLIT[index], high)
        if first < last:
            regions.append((first - start, last - first, output, first - low))
    return regions


def open_experts(base, ids_ref, *refs):
    sources, (in_ref, out_ref, stage, sems) = refs[:6], refs[-4:]
    half = stage.shape[2] // 2
    copies = []
    for side in range(2):
        expert = ids_ref[0] if side == 0 else 1 - ids_ref[0]
        for index in range(3):
            rows = SPLIT[index]
            for spot in range(4):
                slot = (side * 3 + index) * 4 + spot
                place = jnp.bitwise_xor(base + spot, ids_ref[index + 1])
                columns = pl.ds(pl.multiple_of(place * half, half), half)
                stage[slot, :rows] = sources[2 * index + side][spot].astype(F32)
                for start, count, output, at in part_regions(index, half):
                    if output == 1:
                        copies.append(
                            pltpu.make_async_copy(
                                stage.at[slot, pl.ds(start, count)],
                                out_ref.at[expert, pl.ds(place * half + at, count)],
                                sems.at[len(copies)],
                            )
                        )
                        copies[-1].start()
                        continue
                    for part in range(2):
                        copies.append(
                            pltpu.make_async_copy(
                                stage.at[slot, pl.ds(start, count), pl.ds(part * half, half)],
                                in_ref.at[expert, pl.ds(part * half + at, count), columns],
                                sems.at[len(copies)],
                            )
                        )
                        copies[-1].start()
    for copy in copies:
        copy.wait()


def run_open_experts(ids, base, parts, shape_in, shape_out, begun=()):
    args = [array for part in parts for array in part]
    vmem = pl.BlockSpec(memory_space=pltpu.VMEM)
    hbm = pl.BlockSpec(memory_space=pl.ANY)
    copies = 8 * sum(1 if region[2] else 2 for i in range(3) for region in part_regions(i, 256))
    return call(
        functools.partial(open_experts, base),
        "open_experts",
        (),
        [pl.BlockSpec(memory_space=pltpu.SMEM)] + [vmem] * len(args) + [hbm] * len(begun),
        [hbm] * 2,
        [jax.ShapeDtypeStruct(shape_in, F32), jax.ShapeDtypeStruct(shape_out, F32)],
        1e10,
        1e7,
        scratch_shapes=[
            pltpu.VMEM((24, max(SPLIT), shape_out[2]), F32),
            pltpu.SemaphoreType.DMA((copies,)),
        ],
        input_output_aliases={1 + len(args) + i: i for i in range(len(begun))},
    )(ids, *args, *begun)


def tie(*values):
    return lax.optimization_barrier(values)


def build(mesh):
    n_head, n_batch = mesh.shape["head"], mesh.shape["batch"]
    head_bits = [("head", 1 << i) for i in range(n_head.bit_length() - 1)]
    batch_bits = [("batch", 1 << i) for i in range(n_batch.bit_length() - 1)]
    pair, across = head_bits
    first_batch, second_batch, *last_batch = batch_bits
    orders = [
        (across, first_batch, second_batch),
        (first_batch, second_batch, across),
        (second_batch, across, first_batch),
    ]

    def swap(value, step):
        axis, bit = step
        return lax.ppermute(value, axis, [(i, i ^ bit) for i in range(mesh.shape[axis])])

    def bit_of(step):
        axis, bit = step
        return (lax.axis_index(axis) // bit) % 2

    def number(steps):
        return functools.reduce(lambda value, step: 2 * value + bit_of(step), steps, 0)

    def add(kept, got):
        return (kept.astype(F32) + got.astype(F32)).astype(BF)

    def local(
        inputs,
        attn_gain,
        query_weight,
        key_weight,
        value_weight,
        output_weight,
        ffn_gain,
        controller,
        expert_in,
        expert_out,
        group_ids,
        live_mask,
        cotangent,
    ):
        tokens_here, width = inputs.shape
        sequences = tokens_here // LENGTH
        ids = jnp.stack(
            [bit_of(pair)]
            + [number(order) for order in orders]
            + [number((first_batch, second_batch))]
        ).astype(jnp.int32)
        w0 = run_pack(query_weight, key_weight, value_weight, output_weight)
        w2 = swap(w0, across)
        w1 = swap(w0, pair)
        normed, *saved_a = run_forward_first(inputs, attn_gain[None], [w0, w1])
        w2, normed = tie(w2, normed)
        w3 = swap(w2, pair)
        weights = [w0, w1, w2, w3]
        control = jnp.pad(controller, ((0, 0), (0, WIDTH - controller.shape[1])))
        *saved_b, middle, normed2, logits = run_forward_last(
            normed, inputs, saved_a[-1], ffn_gain[None], control, weights
        )

        blank = jnp.zeros((1, tokens_here), F32)
        tags = jnp.concatenate(
            [blank, blank, group_ids.astype(F32)[None], live_mask.astype(F32)[None]] + [blank] * 4,
            axis=0,
        )
        columns, keep, send = run_gather(ids, logits, normed2, cotangent, tags)
        *parts, home, away = run_experts(ids, keep, swap(send, pair), expert_in, expert_out)
        home_got = swap(away, pair)
        kept, sent = parts[:3], parts[3:]
        got = [swap(part, order[0]) for part, order in zip(sent, orders)]

        def send_half(blocks, step):
            half = blocks.shape[0] // 2
            return blocks[:half], swap(blocks[half:], step)

        layer_out, middle_low, small = run_spread(
            ids,
            middle,
            normed2,
            cotangent,
            columns,
            tags,
            home,
            home_got,
            ffn_gain[None],
            jnp.pad(controller.T, ((0, 8 - controller.shape[1]), (0, 0))),
        )

        half = sequences // 2

        def next_stage(kept, got, low, mark, stage):
            *got, mark = tie(*got, mark)
            blocks = [add(a, b) for a, b in zip(kept, got)]
            if stage < 3:
                kept = [block[: block.shape[0] // 2] for block in blocks]
                sent = [block[block.shape[0] // 2 :] for block in blocks]
            else:
                kept = sent = blocks
            *sent, low = tie(*sent, low)
            steps = [order[stage] if stage < 3 else last_batch[stage - 3] for order in orders]
            return kept, [swap(block, step) for block, step in zip(sent, steps)], low, mark

        low = middle_low
        early, late = range(half), range(half, sequences)
        first_items = [(1, i) for i in early]
        second_items = [(1, i) for i in late] + [(0, i) for i in early]
        third_items = [(0, i) for i in late]
        far_slots = weights[2:]
        flat, sums = run_backward(saved_b, low, far_slots, normed, first_items)
        kept, got, low, sums = next_stage(kept, got, low, sums, 1)
        flat, sums = run_backward(
            saved_b, low, far_slots, normed, second_items, first_items, (flat, sums)
        )
        kept, got, low, sums = next_stage(kept, got, low, sums, 2)
        third_got = swap(sums[1].astype(BF), pair)
        flat, sums = run_backward(
            saved_b, low, far_slots, normed, third_items, first_items + second_items, (flat, sums)
        )
        kept, got, low, sums = next_stage(kept, got, low, sums, 3)
        for stage in range(4, 3 + len(last_batch)):
            kept, got, low, sums = next_stage(kept, got, low, sums, stage)
        second = (sums[0] + third_got.astype(F32)).astype(BF)
        second, low = tie(second, low)
        second_got = swap(second, across)
        one_items, own_items = ([(slot, i) for i in range(sequences)] for slot in (1, 0))
        near = run_backward(saved_a, low, weights[:2], normed, one_items)
        first = near[1][1].astype(BF)
        first, low = tie(first, low)
        first_got = swap(first, pair)
        flat_near, sums_near = run_backward(
            saved_a, low, weights[:2], normed, own_items, one_items, near, 6e9
        )
        *got, second_got, first_got, sums_near, low = tie(
            *got, second_got, first_got, sums_near, low
        )

        def widen(blocks, stage):
            return [swap(block, order[stage]) for block, order in zip(blocks, orders)]

        def join(blocks, got):
            return [jnp.concatenate(both, axis=0) for both in zip(blocks, got)]

        def split(value):
            half = value.shape[0] // 2
            return value[:half], value[half:]

        small_steps = head_bits + batch_bits

        blocks = [add(a, b) for a, b in zip(kept, got)]
        *blocks, low = tie(*blocks, low)
        got = widen(blocks, 2)
        own_kept, own_sent = run_join(ids, sums_near, second_got, first_got)
        own_sent, low = tie(own_sent, low)
        own_got = swap(own_sent, first_batch)
        input_grad, small = run_input(
            inputs, attn_gain[None], low, small, [flat_near, flat], weights
        )
        *got, own_got, small = tie(*got, own_got, small)

        blocks = join(blocks, got)
        got = widen(blocks, 1)
        own_kept, own_sent = split(add(own_kept, own_got))
        own_got = swap(own_sent, second_batch)
        small_got = swap(small, small_steps[0])
        *got, own_got, small_got = tie(*got, own_got, small_got)

        blocks = join(blocks, got)
        far = widen(blocks, 0)
        blocks_other = [swap(block, pair) for block in blocks]
        begun = run_open_experts(
            ids, 0, list(zip(blocks, blocks_other)), expert_in.shape, expert_out.shape
        )
        own = add(own_kept, own_got)
        for step in last_batch[:-1]:
            own = add(own, swap(own, step))
        own_got = swap(own, last_batch[-1])
        small = small + small_got
        small_got = swap(small, small_steps[1])
        own_got, small_got, grad_in, grad_out = tie(own_got, small_got, *begun)
        own = add(own, own_got)
        own_got = swap(own, second_batch)
        small = small + small_got
        small_got = swap(small, small_steps[2])
        *far, own_got, small_got = tie(*far, own_got, small_got)

        far_other = [swap(block, pair) for block in far]
        own = jnp.concatenate([own, own_got], axis=0)
        own_got = swap(own, first_batch)
        small = small + small_got
        small_got = swap(small, small_steps[3])
        *far_other, small, small_got = tie(*far_other, small, small_got)

        small = small + small_got
        for step in small_steps[4:-1]:
            small = small + swap(small, step)
        small_got = swap(small, small_steps[-1])
        expert_grads = run_open_experts(
            ids, 4, list(zip(far, far_other)), expert_in.shape, expert_out.shape, (grad_in, grad_out)
        )
        own_got, small_got, expert_in_grad, expert_out_grad = tie(
            own_got, small_got, *expert_grads
        )
        small = small + small_got
        query_grad, key_grad, value_grad, output_grad = run_open(ids, own, own_got)
        return (
            layer_out,
            input_grad,
            small[3],
            query_grad,
            key_grad,
            value_grad,
            output_grad,
            small[0],
            small[1:3].T,
            expert_in_grad,
            expert_out_grad,
        )

    return local


def solution(mesh):
    in_specs = (
        P(("batch", "head"), None),
        P(),
        P(None, "head"),
        P(None, "head"),
        P(None, "head"),
        P("head", None),
        P(),
        P(),
        P(),
        P(),
        P(("batch", "head")),
        P(("batch", "head")),
        P(("batch", "head"), None),
    )
    out_specs = (
        P(("batch", "head"), None),
        P(("batch", "head"), None),
        P(),
        P(None, "head"),
        P(None, "head"),
        P(None, "head"),
        P("head", None),
        P(),
        P(),
        P(),
        P(),
    )
    return jax.shard_map(
        build(mesh), mesh=mesh, in_specs=in_specs, out_specs=out_specs, check_vma=False
    )
```

```python
import functools

import jax
import jax.numpy as jnp
from jax import lax
from jax.experimental import pallas as pl
from jax.experimental.pallas import tpu as pltpu
from jax.sharding import PartitionSpec as P

HD = 64
LENGTH = 1024
WIDTH = 128
BF = jnp.bfloat16
F32 = jnp.float32
LOG2E = 1.4426950408889634
LN2 = 0.6931471805599453
VMEM = 20 * 2**20
FULL_VMEM = 56 * 2**20

eps = 1e-06
last_dims = (((1,), (1,)), ((), ()))
first_dims = (((0,), (0,)), ((), ()))


def dot(left, right):
    return jnp.dot(left, right, preferred_element_type=F32)


def dot_last(left, right):
    return lax.dot_general(left, right, last_dims, preferred_element_type=F32)


def dot_first(left, right):
    return lax.dot_general(left, right, first_dims, preferred_element_type=F32)


def split3(value):
    high = value.astype(BF)
    rest = value - high.astype(F32)
    mid = rest.astype(BF)
    low = (rest - mid.astype(F32)).astype(BF)
    return high, mid, low


def call(
    body, name, grid, in_specs, out_specs, out_shape, flops, moved, exps=0, vmem=VMEM, **extra
):
    return pl.pallas_call(
        body,
        grid=grid,
        in_specs=in_specs,
        out_specs=out_specs,
        out_shape=out_shape,
        compiler_params=pltpu.CompilerParams(vmem_limit_bytes=vmem),
        cost_estimate=pl.CostEstimate(
            flops=int(flops), bytes_accessed=int(moved), transcendentals=int(exps)
        ),
        name=name,
        **extra,
    )


def row_block(columns):
    return pl.BlockSpec((LENGTH, columns), lambda s: (s, 0))


def whole(*shape):
    return pl.BlockSpec(shape, lambda s: (0,) * len(shape))


def head_lanes(rows, head):
    lane = lax.broadcasted_iota(jnp.int32, (rows, WIDTH), 1)
    mine = (lane < HD) if head == 0 else (lane >= HD)
    return lane, mine, HD if head == 0 else 0


def with_extra(mine, lane, other, values, extra):
    high, mid, low = split3(extra)
    filler = jnp.zeros_like(values)
    for place, part in ((2, low), (1, mid), (0, high)):
        filler = jnp.where(lane == other + place, part, filler)
    return jnp.where(mine, values, filler)


def twice(mine, values):
    return jnp.where(mine, values, jnp.roll(values, HD, axis=1))


def scaled_queries(mine, q):
    long = q.astype(F32) * (HD**-0.5 * LOG2E)
    high = long.astype(BF)
    low = (long - high.astype(F32)).astype(BF)
    return jnp.where(mine, high, jnp.roll(low, HD, axis=1))


def attend(normed, weights, q_ref, k_ref, v_ref, logsum_ref, ctx_ref):
    block = 256
    r = lax.broadcasted_iota(jnp.int32, (WIDTH, WIDTH), 0)
    c = lax.broadcasted_iota(jnp.int32, (WIDTH, WIDTH), 1)
    same_head = jnp.where((r < HD) == (c < HD), 1.0, 0.0).astype(BF)

    def most(values):
        long = values.astype(F32)
        return jnp.max(dot((long * long).astype(BF), same_head), axis=0, keepdims=True)

    bounds = []
    for slot, weight in enumerate(weights):
        qkv = dot(normed, weight)
        q = qkv[:, :WIDTH].astype(BF)
        k = qkv[:, WIDTH : 2 * WIDTH].astype(BF)
        q_ref[slot] = q
        k_ref[slot] = k
        v_ref[slot] = qkv[:, 2 * WIDTH :].astype(BF)
        bounds.append(most(q) * most(k))
    bound = jnp.max(functools.reduce(jnp.maximum, bounds))

    def finish(slot, head, here, out, peak):
        lane_b, mine_b, other = head_lanes(block, head)
        total = out[:, other : other + 1]
        logsum = jnp.log2(total) + peak
        context = (out * (1.0 / total)).astype(BF)
        marks = with_extra(jnp.full_like(mine_b, False), lane_b, head * HD, context, logsum)
        if head == 1:
            context = jnp.where(mine_b, context, ctx_ref[slot, here])
            marks = jnp.where(mine_b, marks, logsum_ref[slot, here])
        ctx_ref[slot, here] = context
        logsum_ref[slot, here] = marks

    def head_keys(slot, head):
        lane, mine, other = head_lanes(LENGTH, head)
        vh = jnp.where(mine, v_ref[slot], (lane == other).astype(F32).astype(BF))
        return twice(mine, k_ref[slot]), vh

    def rows_small(slot, head):
        kh, vh = head_keys(slot, head)
        qh = scaled_queries(head_lanes(LENGTH, head)[1], q_ref[slot])
        for start in range(0, LENGTH, block):
            here = slice(start, start + block)
            queries = qh[here]
            scores = []
            for at in range(0, start + block, block):
                part = dot_last(queries, kh[at : at + block])
                if at == start:
                    r = lax.broadcasted_iota(jnp.int32, (block, block), 0)
                    c = lax.broadcasted_iota(jnp.int32, (block, block), 1)
                    part = jnp.where(c <= r, part, -1e30)
                scores.append(part)
            out = 0.0
            for index, part in enumerate(scores):
                out = out + dot(
                    jnp.exp2(part).astype(BF), vh[index * block : (index + 1) * block]
                )
            finish(slot, head, here, out, 0.0)

    def rows_large(slot, head):
        @pl.loop(0, LENGTH // block)
        def _(index):
            kh, vh = head_keys(slot, head)
            here = pl.ds(pl.multiple_of(index * block, block), block)
            queries = scaled_queries(head_lanes(block, head)[1], q_ref[slot, here])
            scores = dot_last(queries, kh)
            r = lax.broadcasted_iota(jnp.int32, scores.shape, 0) + index * block
            c = lax.broadcasted_iota(jnp.int32, scores.shape, 1)
            scores = jnp.where(c <= r, scores, -1e30)
            peak = jnp.max(scores, axis=1, keepdims=True)
            finish(slot, head, here, dot(jnp.exp2(scores - peak).astype(BF), vh), peak)

    small = bound * (HD**-0.5 * LOG2E) ** 2 * 1.1 < 1e4

    @pl.when(small)
    def _():
        for slot in range(len(weights)):
            for head in range(2):
                rows_small(slot, head)

    @pl.when(jnp.logical_not(small))
    def _():
        for head in range(2):

            @pl.loop(0, len(weights))
            def _(slot):
                rows_large(slot, head)


def norm_rows(rows):
    return rows * lax.rsqrt(jnp.mean(rows * rows, axis=-1, keepdims=True) + eps)


def pack_weights(q_ref, k_ref, v_ref, o_ref, packed_ref):
    for index, ref in enumerate((q_ref, k_ref, v_ref)):
        packed_ref[:, index * WIDTH : (index + 1) * WIDTH] = ref[...]
    packed_ref[:, 3 * WIDTH :] = o_ref[...].T


def run_pack(q, k, v, o):
    width = q.shape[0]
    return call(
        pack_weights,
        "pack_weights",
        (),
        [pl.BlockSpec(memory_space=pltpu.VMEM)] * 4,
        pl.BlockSpec(memory_space=pltpu.VMEM),
        jax.ShapeDtypeStruct((width, 4 * WIDTH), BF),
        1e6,
        2e6,
        vmem=FULL_VMEM,
    )(q, k, v, o)


def forward_first(x_ref, gain_ref, *refs):
    slots = len(refs) - 6
    normed_ref, *saved = refs[slots:]
    normed = (norm_rows(x_ref[...].astype(F32)) * gain_ref[...]).astype(BF)
    normed_ref[...] = normed
    attend(normed, [ref[:, : 3 * WIDTH] for ref in refs[:slots]], *saved)


def forward_last(
    ids_ref, normed_ref, x_ref, ctx_in_ref, ffn_gain_ref, control_ref, cot_ref, group_ref,
    live_ref, *refs
):
    slots = len(refs) - 12
    weights = refs[:slots]
    *saved, middle_ref, normed2_ref = refs[slots : slots + 7]
    *groups, normed2_all, logits_all = refs[slots + 7 :]
    ctx_ref = saved[-1]
    normed = normed_ref[...]
    before = ctx_in_ref.shape[0]
    attend(normed, [ref[:, : 3 * WIDTH] for ref in weights[before:]], *saved)
    sequence = pl.program_id(0)
    here = pl.ds(pl.multiple_of(sequence * LENGTH, LENGTH), LENGTH)
    context = jnp.concatenate(
        [ctx_in_ref[i] for i in range(before)] + [ctx_ref[i] for i in range(slots - before)],
        axis=1,
    )
    flipped = jnp.concatenate([ref[:, -WIDTH:] for ref in weights], axis=1)
    middle = x_ref[...].astype(F32) + dot_last(context, flipped)
    middle_ref[...] = middle
    normed2 = (norm_rows(middle) * ffn_gain_ref[...]).astype(BF)
    normed2_ref[...] = normed2
    normed2_all[here] = normed2
    logits_all[here] = dot_last(normed2, control_ref[...])

    @pl.when(sequence == pl.num_programs(0) - 1)
    def _():
        gather_groups(
            ids_ref, logits_all, normed2_all, cot_ref, group_ref, live_ref, *groups
        )


def slot_outputs(slots, tokens):
    per = pl.BlockSpec((slots, LENGTH, WIDTH), lambda s: (0, s, 0))
    return [per] * 5, [jax.ShapeDtypeStruct((slots, tokens, WIDTH), BF)] * 5


def run_forward_first(x, gain, weights):
    tokens, width = x.shape
    specs, shapes = slot_outputs(len(weights), tokens)
    return call(
        forward_first,
        "attention_forward_first",
        (tokens // LENGTH,),
        [row_block(width), whole(1, width)] + [whole(width, 4 * WIDTH)] * len(weights),
        [row_block(width)] + specs,
        [jax.ShapeDtypeStruct((tokens, width), BF)] + shapes,
        1.5e10,
        1e7,
        1e7,
        vmem=FULL_VMEM,
    )(x, gain, *weights)


def run_forward_last(ids, normed, x, ctx, ffn_gain, control, cot, group, live, weights):
    tokens, width = x.shape
    groups = tokens // 8
    before = ctx.shape[0]
    specs, shapes = slot_outputs(len(weights) - before, tokens)
    sums = jax.ShapeDtypeStruct((2, groups, width), BF)
    return call(
        forward_last,
        "attention_forward_last",
        (tokens // LENGTH,),
        [
            pl.BlockSpec(memory_space=pltpu.SMEM),
            row_block(width),
            row_block(width),
            pl.BlockSpec((before, LENGTH, WIDTH), lambda s: (0, s, 0)),
            whole(1, width),
            whole(2, width),
            whole(tokens, width),
            whole(1, tokens),
            whole(1, tokens),
        ]
        + [pl.BlockSpec((width, WIDTH), lambda s: (0, 3))] * before
        + [whole(width, 4 * WIDTH)] * (len(weights) - before),
        specs
        + [row_block(width), row_block(width), whole(tokens, WIDTH)]
        + [whole(2, groups, width)] * 2,
        shapes
        + [
            jax.ShapeDtypeStruct((tokens, width), F32),
            jax.ShapeDtypeStruct((tokens, width), BF),
            jax.ShapeDtypeStruct((tokens, WIDTH), F32),
            sums,
            sums,
        ],
        1.5e10,
        1e7,
        1e7,
        vmem=40 * 2**20,
        scratch_shapes=[pltpu.VMEM((tokens, width), BF), pltpu.VMEM((tokens, 2), F32)],
    )(ids, normed, x, ctx, ffn_gain, control, cot, group, live, *weights)


def backward_items(
    slots, items_ref, q_ref, k_ref, v_ref, logsum_ref, ctx_ref, ml_ref, normed_ref, *refs
):
    dqkv_ref, dw_ref = refs[-2:]
    item = pl.program_id(0)
    weight = refs[0][...]
    for index in range(1, slots):
        weight = jnp.where(items_ref[0, item] == index, refs[index][...], weight)
    block = 256
    ml = ml_ref[...]
    ctx = ctx_ref[0]
    d_out = dot(ml, weight).astype(BF)
    product = d_out.astype(F32) * ctx.astype(F32)
    q = q_ref[0]
    k = k_ref[0]
    v = v_ref[0]
    logsum = logsum_ref[0]
    k_flip = k.T
    dks, dvs, dqs = [], [], []
    for head in range(2):
        lane, mine, other = head_lanes(LENGTH, head)
        minus = jnp.where((lane >= other) & (lane < other + 3), -1.0, 0.0).astype(BF)
        minus_own = jnp.where((lane >= HD - other) & (lane < HD - other + 3), -1.0, 0.0).astype(BF)
        central = jnp.sum(jnp.where(mine, product, 0.0), axis=1, keepdims=True)
        d_all = with_extra(mine, lane, other, d_out, central)
        v_all = jnp.where(mine, v, minus)
        k_all = jnp.concatenate([twice(mine, k), minus_own], axis=1)
        q_scaled = scaled_queries(mine, q)
        q_all = jnp.concatenate([q_scaled, logsum], axis=1)
        dq = [0.0] * (LENGTH // block)
        dk, dv = [], []
        for at in range(0, LENGTH, block):
            keys = k_all[at : at + block]
            values = v_all[at : at + block]
            flipped = k_flip[head * HD : (head + 1) * HD, at : at + block]
            probs = jnp.exp2(dot_last(keys, q_all[at:]))
            r = lax.broadcasted_iota(jnp.int32, (block, block), 0)
            c = lax.broadcasted_iota(jnp.int32, (block, block), 1)
            corner = jnp.where(r <= c, probs[:, :block], 0.0)
            probs = corner if at + block == LENGTH else jnp.concatenate([corner, probs[:, block:]], axis=1)
            d_scores = (probs * dot_last(values, d_all[at:])).astype(BF)
            dv.append(dot(probs.astype(BF), d_all[at:]))
            dk.append(dot(d_scores, q_scaled[at:]))
            part = dot(flipped, d_scores)
            for start in range(at, LENGTH, block):
                dq[start // block] = dq[start // block] + part[:, start - at : start - at + block]
        dk = jnp.concatenate(dk, axis=0)
        dks.append(dk + jnp.roll(dk, HD, axis=1))
        dvs.append(jnp.concatenate(dv, axis=0))
        dqs.append(jnp.concatenate(dq, axis=1))
    lane, mine, _ = head_lanes(LENGTH, 0)
    dk = (jnp.where(mine, dks[0], dks[1]) * LN2).astype(BF)
    dv = jnp.where(mine, dvs[0], dvs[1]).astype(BF)
    dq_flip = (jnp.concatenate(dqs, axis=0) * HD**-0.5).astype(BF)
    dqkv_ref[0, :, :WIDTH] = dq_flip.T
    dqkv_ref[0, :, WIDTH : 2 * WIDTH] = dk
    dqkv_ref[0, :, 2 * WIDTH :] = dv
    dw = dot(jnp.concatenate([dq_flip, dk.T, dv.T], axis=0), normed_ref[...])
    dwo = dot_first(ctx, ml)
    parts = [dw[:WIDTH], dw[WIDTH : 2 * WIDTH], dw[2 * WIDTH :], dwo]
    adds = items_ref[2, item]
    earlier = refs[slots + 1] if len(refs) > slots + 2 else None

    @pl.when(adds == 0)
    def _():
        for index, part in enumerate(parts):
            dw_ref[0, index] = part

    @pl.when(adds == 1)
    def _():
        for index, part in enumerate(parts):
            dw_ref[0, index] += part

    if earlier is not None:

        @pl.when(adds == 2)
        def _():
            for index, part in enumerate(parts):
                dw_ref[0, index] = earlier[0, index] + part


def run_backward(saved, ml, weights, normed, items, done=(), earlier=None, flops=6e9):
    tokens, width = ml.shape
    slots = len(weights)
    table = [[], [], []]
    for index, (slot, sequence) in enumerate(items):
        seen = [one for one in items[:index] if one[0] == slot]
        before = [one for one in done if one[0] == slot]
        table[0].append(slot)
        table[1].append(sequence)
        table[2].append(1 if seen else 2 if before else 0)
    table = jnp.array(table, jnp.int32)
    per = pl.BlockSpec((1, LENGTH, WIDTH), lambda i, t: (t[0, i], t[1, i], 0))
    rows = pl.BlockSpec((LENGTH, width), lambda i, t: (t[1, i], 0))
    sums = pl.BlockSpec((1, 4, WIDTH, width), lambda i, t: (t[0, i], 0, 0, 0))
    args = [table, *saved, ml, normed, *weights]
    in_specs = [*([per] * 5), rows, rows]
    in_specs += [pl.BlockSpec((width, WIDTH), lambda i, t: (0, 3))] * slots
    aliases = {}
    if earlier is not None:
        aliases = {len(args): 0, len(args) + 1: 1}
        args += list(earlier)
        in_specs += [pl.BlockSpec(memory_space=pl.ANY), sums]
    return pl.pallas_call(
        functools.partial(backward_items, slots),
        grid_spec=pltpu.PrefetchScalarGridSpec(
            num_scalar_prefetch=1,
            grid=(len(items),),
            in_specs=in_specs,
            out_specs=[pl.BlockSpec((1, LENGTH, 3 * WIDTH), lambda i, t: (t[0, i], t[1, i], 0)), sums],
        ),
        out_shape=[
            jax.ShapeDtypeStruct((slots, tokens, 3 * WIDTH), BF),
            jax.ShapeDtypeStruct((slots, 4, WIDTH, width), F32),
        ],
        input_output_aliases=aliases,
        compiler_params=pltpu.CompilerParams(vmem_limit_bytes=VMEM),
        cost_estimate=pl.CostEstimate(
            flops=int(flops * len(items)), bytes_accessed=1, transcendentals=0
        ),
        name="attention_backward",
    )(*args)


def group_marks(group, alive, groups):
    slot = lax.broadcasted_iota(jnp.int32, (groups, group.shape[1]), 0).astype(F32)
    return jnp.where((slot == group) & (alive > 0), 1.0, 0.0).astype(BF)


def token_marks(columns, groups):
    slot = lax.broadcasted_iota(jnp.int32, (columns.shape[0], groups), 1).astype(F32)
    return jnp.where((slot == columns[:, 2:3]) & (columns[:, 3:4] > 0), 1.0, 0.0).astype(BF)


def dot_exact(marks, values):
    return functools.reduce(jnp.add, [dot(marks, part) for part in split3(values)])


def gather_groups(
    ids_ref, logits_ref, normed2_ref, cot_ref, group_ref, live_ref, columns_ref, keep_ref, send_ref
):
    tokens = normed2_ref.shape[0]
    groups = keep_ref.shape[1]
    group = group_ref[...].astype(F32)
    alive = live_ref[...].astype(F32)
    row = lax.broadcasted_iota(jnp.int32, (WIDTH, tokens), 0)
    turned = jnp.where(row == 2, group, jnp.where(row == 3, alive, 0.0)).T
    marks = group_marks(group, alive, groups)
    token_side = token_marks(turned, groups)
    live = turned[:, 3:4]
    lane = lax.broadcasted_iota(jnp.int32, (tokens, WIDTH), 1)
    logits = jnp.concatenate([logits_ref[...], jnp.zeros((tokens, WIDTH - 2), F32)], axis=1)
    expo = jnp.exp(logits) * live
    totals = dot_exact(marks, expo)
    weights = expo / (dot_exact(token_side, totals) + (1.0 - live))
    columns_ref[...] = jnp.where(lane < 2, weights, turned)
    rows = weights.T[:8].astype(BF)
    own = ids_ref[0] == 0
    normed2 = normed2_ref[...]
    cot = cot_ref[...]
    for ref, pick in ((keep_ref, own), (send_ref, jnp.logical_not(own))):
        assign = marks * jnp.where(pick, rows[0:1].astype(F32), rows[1:2].astype(F32)).astype(BF)
        ref[0] = dot(assign, normed2).astype(BF)
        ref[1] = dot(assign, cot).astype(BF)


def gelu_both(x):
    inner = 0.7978845608028654
    cubic = 0.044715
    square = x * x
    bent = jnp.tanh(inner * x * (1.0 + cubic * square))
    half = 0.5 * (1.0 + bent)
    slope = half + 0.5 * x * (1.0 - bent * bent) * (inner * (1.0 + 3.0 * cubic * square))
    return x * half, slope


SPLIT = (176, 176, 160)


def expert_step(
    ids_ref, keep_ref, got_ref, in_ref, out_ref, *refs
):
    kept_refs, sent_refs = refs[:3], refs[3:6]
    home_ref, away_ref, mixed_flip, result, mixed_grad, in_all, out_all, sems = refs[6:]
    step = pl.program_id(0)
    groups = keep_ref.shape[1]
    mixed = jnp.concatenate([keep_ref[0], got_ref[0]], axis=0)
    d_result = jnp.concatenate([keep_ref[1], got_ref[1]], axis=0)
    wide = in_all.shape[2]

    def loads(at):
        span = pl.ds(pl.multiple_of(at * wide, wide), wide)
        return [
            pltpu.make_async_copy(in_ref.at[ids_ref[0], :, span], in_all.at[at], sems.at[0, at]),
            pltpu.make_async_copy(out_ref.at[ids_ref[0], span], out_all.at[at], sems.at[1, at]),
        ]

    @pl.when(step == 0)
    def _():
        for at in range(in_all.shape[0]):
            for load in loads(at):
                load.start()
        mixed_flip[...] = mixed.T
        result[...] = jnp.zeros_like(result)
        mixed_grad[...] = jnp.zeros_like(mixed_grad)

    for load in loads(step):
        load.wait()
    w_in = in_all[step]
    w_out = out_all[step]
    active, slope = gelu_both(dot(mixed, w_in))
    active = active.astype(BF)
    d_before = (dot_last(d_result, w_out) * slope).astype(BF)
    result[...] += dot(active, w_out)
    mixed_grad[...] += dot_last(d_before, w_in)
    d_out = dot_first(active, d_result).astype(BF)
    d_in = dot(mixed_flip[...], d_before).astype(BF)
    half = d_in.shape[0] // 2
    for index in range(2):
        columns = slice(index * half, (index + 1) * half)
        side = d_in[:, columns]
        block = jnp.concatenate(
            [d_out[columns], jnp.concatenate([side[:half], side[half:]], axis=1)], axis=0
        )
        at = 0
        for part, rows in enumerate(SPLIT):
            place = jnp.bitwise_xor(2 * step + index, ids_ref[part + 1])
            piece = block[at : at + rows]
            at += rows

            @pl.when(place < 4)
            def _():
                kept_refs[part][place] = piece

            @pl.when(place >= 4)
            def _():
                sent_refs[part][place - 4] = piece

    @pl.when(step == pl.num_programs(0) - 1)
    def _():
        home_ref[0] = result[:groups].astype(BF)
        home_ref[1] = mixed_grad[:groups].astype(BF)
        away_ref[0] = result[groups:].astype(BF)
        away_ref[1] = mixed_grad[groups:].astype(BF)


def run_experts(ids, keep, got, expert_in, expert_out):
    _, width, hidden = expert_in.shape
    steps = 4
    wide = hidden // steps
    groups = keep.shape[1]
    sums = jax.ShapeDtypeStruct(keep.shape, BF)
    halves = [(4, rows, width) for rows in SPLIT] * 2
    hbm = pl.BlockSpec(memory_space=pltpu.HBM)
    return call(
        expert_step,
        "experts",
        (steps,),
        [pl.BlockSpec(memory_space=pltpu.SMEM), whole(*keep.shape), whole(*keep.shape), hbm, hbm],
        [whole(*shape) for shape in halves + [keep.shape] * 2],
        [jax.ShapeDtypeStruct(shape, BF) for shape in halves] + [sums, sums],
        1e10,
        1.2e7,
        1e6,
        scratch_shapes=[
            pltpu.VMEM((width, 2 * groups), BF),
            pltpu.VMEM((2 * groups, width), F32),
            pltpu.VMEM((2 * groups, width), F32),
            pltpu.VMEM((steps, width, wide), BF),
            pltpu.VMEM((steps, wide, width), BF),
            pltpu.SemaphoreType.DMA((2, steps)),
        ],
    )(ids, keep, got, expert_in, expert_out)


def spread_groups(
    ids_ref, middle_ref, normed2_ref, cot_ref, columns_ref, group_ref, live_ref, home_ref, got_ref,
    gain_ref, control_ref, out_ref, low_ref, small_ref,
    table, mixed_part, weight_grads, group_sums,
):
    phase, index = pl.program_id(0), pl.program_id(1)
    rows, width = middle_ref.shape
    groups = home_ref.shape[1]
    here = pl.ds(pl.multiple_of(index * rows, rows), rows)

    @pl.when((phase == 0) & (index == 0))
    def _():
        group_sums[...] = jnp.zeros_like(group_sums)
        small_ref[...] = jnp.zeros_like(small_ref)
        own = ids_ref[0] == 0
        for kind in range(2):
            home, got = home_ref[kind], got_ref[kind]
            at = 2 * kind * width
            table[:, at : at + width] = jnp.where(own, home, got)
            table[:, at + width : at + 2 * width] = jnp.where(own, got, home)

    @pl.when(phase == 0)
    def _():
        columns = columns_ref[...]
        lane = lax.broadcasted_iota(jnp.int32, columns.shape, 1)
        token_side = token_marks(columns, groups)
        spread = dot(token_side, table[...])
        cot = cot_ref[...]
        normed2 = normed2_ref[...]
        middle = middle_ref[...]
        cot = cot.astype(F32)
        normed2 = normed2.astype(F32)
        low = columns.astype(BF).astype(F32)
        first, second = low[:, 0:1], low[:, 1:2]
        result = [spread[:, i * width : (i + 1) * width] for i in range(4)]
        out_ref[...] = (middle + first * result[0] + second * result[1]).astype(BF)
        mixed_part[here] = first * result[2] + second * result[3]
        grads = [
            jnp.sum(cot * result[i] + normed2 * result[2 + i], axis=1, keepdims=True)
            for i in range(2)
        ]
        grads = jnp.where(lane == 0, grads[0], jnp.where(lane == 1, grads[1], 0.0))
        pulls = jnp.where(lane < 2, columns * grads, 0.0)
        weight_grads[here] = pulls
        group = group_ref[...].astype(F32)
        alive = live_ref[...].astype(F32)
        group_sums[...] += dot_exact(group_marks(group, alive, groups), pulls)

    @pl.when(phase == 1)
    def _():
        columns = columns_ref[...]
        central = dot_exact(token_marks(columns, groups), group_sums[...])
        logit_grads = weight_grads[here] - columns * central
        first, second = logit_grads[:, 0:1], logit_grads[:, 1:2]
        control = control_ref[...].astype(F32)
        cot = cot_ref[...].astype(F32)
        normed2 = normed2_ref[...].astype(F32)
        middle = middle_ref[...]
        grad = mixed_part[here] + first * control[0:1] + second * control[1:2]
        scale = lax.rsqrt(jnp.mean(middle * middle, axis=-1, keepdims=True) + eps)
        unit = middle * scale
        pulled = grad * gain_ref[...]
        pulled = scale * (pulled - unit * jnp.mean(pulled * unit, axis=-1, keepdims=True))
        low_ref[...] = (cot + pulled).astype(BF)
        small_ref[0:1] += jnp.sum(grad * unit, axis=0, keepdims=True)
        small_ref[1:2] += jnp.sum(first * normed2, axis=0, keepdims=True)
        small_ref[2:3] += jnp.sum(second * normed2, axis=0, keepdims=True)


def run_spread(ids, middle, normed2, cot, columns, group, live, home, got, gain, control):
    tokens, width = middle.shape
    groups = home.shape[1]
    rows = 512
    steps = tokens // rows
    by_block = lambda n: pl.BlockSpec((rows, n), lambda p, b: (b, 0))
    fixed = lambda *shape: pl.BlockSpec(shape, lambda p, b: (0,) * len(shape))
    return call(
        spread_groups,
        "spread_groups",
        (2, steps),
        [
            pl.BlockSpec(memory_space=pltpu.SMEM),
            by_block(width),
            by_block(width),
            by_block(width),
            by_block(WIDTH),
            pl.BlockSpec((1, rows), lambda p, b: (0, b)),
            pl.BlockSpec((1, rows), lambda p, b: (0, b)),
            fixed(*home.shape),
            fixed(*home.shape),
            fixed(1, width),
            fixed(2, width),
        ],
        [
            pl.BlockSpec((rows, width), lambda p, b: (b * (1 - p) + (steps - 1) * p, 0)),
            pl.BlockSpec((rows, width), lambda p, b: (b * p, 0)),
            fixed(8, width),
        ],
        [
            jax.ShapeDtypeStruct((tokens, width), BF),
            jax.ShapeDtypeStruct((tokens, width), BF),
            jax.ShapeDtypeStruct((8, width), F32),
        ],
        8e9,
        2e7,
        scratch_shapes=[
            pltpu.VMEM((groups, 4 * width), BF),
            pltpu.VMEM((tokens, width), F32),
            pltpu.VMEM((tokens, WIDTH), F32),
            pltpu.VMEM((groups, WIDTH), F32),
        ],
    )(ids, middle, normed2, cot, columns, group, live, home, got, gain, control)


def input_rows(x_ref, gain_ref, grad_ref, *refs):
    slots = 4
    flats, weights, out_ref = refs[: -slots - 1], refs[-slots - 1 : -1], refs[-1]
    rows = x_ref[...].astype(F32)
    grad = dot_last(
        jnp.concatenate([flat[i] for flat in flats for i in range(flat.shape[0])], axis=1),
        jnp.concatenate([weight[:, : 3 * WIDTH] for weight in weights], axis=1),
    )
    scale = lax.rsqrt(jnp.mean(rows * rows, axis=-1, keepdims=True) + eps)
    unit = rows * scale
    pulled = grad * gain_ref[...]
    pulled = scale * (pulled - unit * jnp.mean(pulled * unit, axis=-1, keepdims=True))
    out_ref[...] = grad_ref[...].astype(F32) + pulled


def run_input(x, gain, grad, flats, weights):
    tokens, width = x.shape
    rows = 512
    by_block = lambda n: pl.BlockSpec((rows, n), lambda s: (s, 0))
    return call(
        input_rows,
        "input_rows",
        (tokens // rows,),
        [by_block(width), whole(1, width), by_block(width)]
        + [
            pl.BlockSpec((flat.shape[0], rows, 3 * WIDTH), lambda s: (0, s, 0)) for flat in flats
        ]
        + [whole(width, 4 * WIDTH)] * len(weights),
        by_block(width),
        jax.ShapeDtypeStruct((tokens, width), F32),
        1,
        1,
        vmem=FULL_VMEM,
    )(x, gain, grad, *flats, *weights)


def join_own(
    ids_ref, own_ref, one_ref, two_ref, weight_ref, gain_ref, rest_ref, kept_ref, sent_ref, small_ref
):
    half = kept_ref.shape[0]
    flipped = weight_ref[:, : 3 * WIDTH].T.astype(F32)
    gain_grad = 0.0
    for place in range(2 * half):
        total = own_ref[0, place] + one_ref[place].astype(F32) + two_ref[place].astype(F32)
        if place < 3:
            part = flipped[place * WIDTH : (place + 1) * WIDTH] * total
            gain_grad = gain_grad + jnp.sum(part, axis=0, keepdims=True)
        index = jnp.bitwise_xor(place, ids_ref[4])
        total = total.astype(BF)

        @pl.when(index < half)
        def _():
            kept_ref[index] = total

        @pl.when(index >= half)
        def _():
            sent_ref[index - half] = total

    small_ref[...] = rest_ref[...]
    small_ref[3:4] = gain_grad / gain_ref[...]


def run_join(ids, own, one, two, weight, gain, rest):
    _, n, rows, width = own.shape
    vmem = pl.BlockSpec(memory_space=pltpu.VMEM)
    return call(
        join_own,
        "join_own",
        (),
        [pl.BlockSpec(memory_space=pltpu.SMEM)] + [vmem] * 6,
        [vmem] * 3,
        [jax.ShapeDtypeStruct((n // 2, rows, width), BF)] * 2
        + [jax.ShapeDtypeStruct(rest.shape, F32)],
        1,
        1,
    )(ids, own, one, two, weight, gain, rest)


def open_own(ids_ref, own_ref, *refs):
    gots, outs = refs[:3], refs[3:]
    for index, out in enumerate(outs):
        place = jnp.bitwise_xor(index, ids_ref[4])
        value = own_ref[0]
        for at, got in enumerate(gots):
            value = jnp.where(place == at + 1, got[0], value)
        value = value.astype(F32)
        out[...] = value if index == 3 else value.T


def run_open(ids, own, gots):
    _, rows, width = own.shape
    vmem = pl.BlockSpec(memory_space=pltpu.VMEM)
    return call(
        open_own,
        "open_own",
        (),
        [pl.BlockSpec(memory_space=pltpu.SMEM)] + [vmem] * 4,
        [vmem] * 4,
        [jax.ShapeDtypeStruct((width, rows), F32)] * 3
        + [jax.ShapeDtypeStruct((rows, width), F32)],
        1e6,
        2e6,
    )(ids, own, *gots)


def part_regions(index, half):
    start = sum(SPLIT[:index])
    regions = []
    for low, high, output in ((0, half, 1), (half, 2 * half, 0)):
        first, last = max(start, low), min(start + SPLIT[index], high)
        if first < last:
            regions.append((first - start, last - first, output, first - low))
    return regions


def open_experts(base, ids_ref, *refs):
    sources, (in_ref, out_ref, stage, sems) = refs[:-4], refs[-4:]
    joined = len(sources) in (4, 6) and sources[3].shape[1] == sum(SPLIT)
    half = stage.shape[2] // 2
    copies = []
    for side in range(2):
        expert = ids_ref[0] if side == 0 else 1 - ids_ref[0]
        for index in range(3):
            rows = SPLIT[index]
            for spot in range(4):
                slot = (side * 3 + index) * 4 + spot
                place = jnp.bitwise_xor(base + spot, ids_ref[index + 1])
                columns = pl.ds(pl.multiple_of(place * half, half), half)
                if side == 1 and joined:
                    at = sum(SPLIT[:index])
                    piece = sources[3][spot, at : at + rows]
                else:
                    piece = sources[3 * side + index][spot]
                stage[slot, :rows] = piece.astype(F32)
                for start, count, output, at in part_regions(index, half):
                    if output == 1:
                        copies.append(
                            pltpu.make_async_copy(
                                stage.at[slot, pl.ds(start, count)],
                                out_ref.at[expert, pl.ds(place * half + at, count)],
                                sems.at[len(copies)],
                            )
                        )
                        copies[-1].start()
                        continue
                    for part in range(2):
                        copies.append(
                            pltpu.make_async_copy(
                                stage.at[slot, pl.ds(start, count), pl.ds(part * half, half)],
                                in_ref.at[expert, pl.ds(part * half + at, count), columns],
                                sems.at[len(copies)],
                            )
                        )
                        copies[-1].start()
    for copy in copies:
        copy.wait()


def run_open_experts(ids, base, args, shape_in, shape_out, begun=()):
    vmem = pl.BlockSpec(memory_space=pltpu.VMEM)
    hbm = pl.BlockSpec(memory_space=pl.ANY)
    copies = 8 * sum(1 if region[2] else 2 for i in range(3) for region in part_regions(i, 256))
    return call(
        functools.partial(open_experts, base),
        "open_experts",
        (),
        [pl.BlockSpec(memory_space=pltpu.SMEM)] + [vmem] * len(args) + [hbm] * len(begun),
        [hbm] * 2,
        [jax.ShapeDtypeStruct(shape_in, F32), jax.ShapeDtypeStruct(shape_out, F32)],
        1e10 if base else 1,
        1e7 if base else 1,
        scratch_shapes=[
            pltpu.VMEM((24, max(SPLIT), shape_out[2]), F32),
            pltpu.SemaphoreType.DMA((copies,)),
        ],
        input_output_aliases={1 + len(args) + i: i for i in range(len(begun))},
    )(ids, *args, *begun)


def tie(*values):
    return lax.optimization_barrier(values)


def tie_groups(*groups):
    values = iter(tie(*[value for group in groups for value in group]))
    return [[next(values) for _ in group] for group in groups]


def build(mesh):
    n_head, n_batch = mesh.shape["head"], mesh.shape["batch"]
    head_bits = [("head", 1 << i) for i in range(n_head.bit_length() - 1)]
    batch_bits = [("batch", 1 << i) for i in range(n_batch.bit_length() - 1)]
    pair, across = head_bits
    first_batch, second_batch, *last_batch = batch_bits
    orders = [
        (across, first_batch, second_batch),
        (first_batch, second_batch, across),
        (second_batch, across, first_batch),
    ]

    def swap(value, step):
        axis, bit = step
        return lax.ppermute(value, axis, [(i, i ^ bit) for i in range(mesh.shape[axis])])

    def bit_of(step):
        axis, bit = step
        return (lax.axis_index(axis) // bit) % 2

    def number(steps):
        return functools.reduce(lambda value, step: 2 * value + bit_of(step), steps, 0)

    def add(kept, got):
        return (kept.astype(F32) + got.astype(F32)).astype(BF)

    def local(
        inputs,
        attn_gain,
        query_weight,
        key_weight,
        value_weight,
        output_weight,
        ffn_gain,
        controller,
        expert_in,
        expert_out,
        group_ids,
        live_mask,
        cotangent,
    ):
        tokens_here, width = inputs.shape
        sequences = tokens_here // LENGTH
        ids = jnp.stack(
            [bit_of(pair)]
            + [number(order) for order in orders]
            + [number((first_batch, second_batch))]
        ).astype(jnp.int32)
        w0 = run_pack(query_weight, key_weight, value_weight, output_weight)
        w2 = swap(w0, across)
        w1 = swap(w0, pair)
        normed, *saved_a = run_forward_first(inputs, attn_gain[None], [w0, w1])
        w2, normed = tie(w2, normed)
        w3 = swap(w2, pair)
        weights = [w0, w1, w2, w3]
        control = controller.T
        group, live = group_ids[None], live_mask[None]
        *saved_b, middle, normed2, columns, keep, send = run_forward_last(
            ids,
            normed,
            inputs,
            saved_a[-1],
            ffn_gain[None],
            control,
            cotangent,
            group,
            live,
            weights,
        )
        *parts, home, away = run_experts(ids, keep, swap(send, pair), expert_in, expert_out)
        home_got = swap(away, pair)
        kept, sent = parts[:3], parts[3:]
        got = [swap(part, order[0]) for part, order in zip(sent, orders)]

        def send_half(blocks, step):
            half = blocks.shape[0] // 2
            return blocks[:half], swap(blocks[half:], step)

        layer_out, middle_low, small = run_spread(
            ids,
            middle,
            normed2,
            cotangent,
            columns,
            group,
            live,
            home,
            home_got,
            ffn_gain[None],
            control,
        )

        half = sequences // 2

        def next_stage(kept, got, low, mark, stage):
            *got, mark = tie(*got, mark)
            blocks = [add(a, b) for a, b in zip(kept, got)]
            if stage < 3:
                kept = [block[: block.shape[0] // 2] for block in blocks]
                sent = [block[block.shape[0] // 2 :] for block in blocks]
            else:
                kept = sent = blocks
            *sent, low = tie(*sent, low)
            steps = [order[stage] if stage < 3 else last_batch[stage - 3] for order in orders]
            return kept, [swap(block, step) for block, step in zip(sent, steps)], low, mark

        low = middle_low
        early, late = range(half), range(half, sequences)
        first_items = [(1, i) for i in early]
        second_items = [(1, i) for i in late] + [(0, i) for i in early]
        third_items = [(0, i) for i in late]
        far_slots = weights[2:]
        flat, sums = run_backward(saved_b, low, far_slots, normed, first_items)
        kept, got, low, sums = next_stage(kept, got, low, sums, 1)
        flat, sums = run_backward(
            saved_b, low, far_slots, normed, second_items, first_items, (flat, sums)
        )
        kept, got, low, sums = next_stage(kept, got, low, sums, 2)
        third_got = swap(sums[1].astype(BF), pair)
        flat, sums = run_backward(
            saved_b, low, far_slots, normed, third_items, first_items + second_items, (flat, sums)
        )
        kept, got, low, sums = next_stage(kept, got, low, sums, 3)
        for stage in range(4, 3 + len(last_batch)):
            kept, got, low, sums = next_stage(kept, got, low, sums, stage)
        second = (sums[0] + third_got.astype(F32)).astype(BF)
        second, low = tie(second, low)
        second_got = swap(second, across)
        near_items = [(slot, i) for slot in (1, 0) for i in range(sequences)]
        flat_near, sums_near = run_backward(saved_a, low, weights[:2], normed, near_items)
        *got, second_got, sums_near, low = tie(*got, second_got, sums_near, low)

        def widen(blocks, stage):
            return [swap(block, order[stage]) for block, order in zip(blocks, orders)]

        def join(blocks, got):
            return [jnp.concatenate(both, axis=0) for both in zip(blocks, got)]

        def split(value):
            half = value.shape[0] // 2
            return value[:half], value[half:]

        def all_of(value, steps):
            (axis, one), (_, two) = steps
            return [swap(value, (axis, bits)) for bits in (one, two, one | two)]

        first_got = swap(sums_near[1].astype(BF), pair)
        blocks = [add(a, b) for a, b in zip(kept, got)]
        *blocks, low = tie(*blocks, low)
        got = widen(blocks, 2)
        own_kept, own_sent, small = run_join(
            ids, sums_near, second_got, first_got, w0, attn_gain[None], small
        )
        own_got = swap(own_sent, first_batch)
        small = small + swap(small, pair)
        small_got = swap(small, across)
        *got, own_got, small_got, low = tie(*got, own_got, small_got, low)

        blocks = join(blocks, got)
        got = widen(blocks, 1)
        own_kept, own_sent = split(add(own_kept, own_got))
        own_got = swap(own_sent, second_batch)
        small = small + small_got
        small_got = swap(small, first_batch)
        input_grad = run_input(inputs, attn_gain[None], low, [flat_near, flat], weights)
        *got, own_got, small_got, input_grad = tie(*got, own_got, small_got, input_grad)

        blocks = join(blocks, got)
        blocks_other = swap(jnp.concatenate(blocks, axis=1), pair)
        far = widen(blocks, 0)
        begun = run_open_experts(
            ids, 0, [*blocks, blocks_other], expert_in.shape, expert_out.shape
        )
        own = add(own_kept, own_got)
        small = small + small_got
        for step in last_batch[:-1]:
            own = add(own, swap(own, step))
            small = small + swap(small, step)
        own_got = swap(own, last_batch[-1])
        small_got = swap(small, second_batch)
        far, (own_got, small_got, *begun) = tie_groups(far, (own_got, small_got, *begun))

        far_other = [swap(block, pair) for block in far]
        own = add(own, own_got)
        own_got = all_of(own, (second_batch, first_batch))
        small = small + small_got
        small_got = swap(small, last_batch[-1])
        expert_grads = run_open_experts(
            ids, 4, [*far, *far_other], expert_in.shape, expert_out.shape, begun
        )
        own_got, (small_got, expert_in_grad, expert_out_grad) = tie_groups(
            own_got, (small_got, *expert_grads)
        )
        small = small + small_got
        query_grad, key_grad, value_grad, output_grad = run_open(ids, own, own_got)
        return (
            layer_out,
            input_grad,
            small[3],
            query_grad,
            key_grad,
            value_grad,
            output_grad,
            small[0],
            small[1:3].T,
            expert_in_grad,
            expert_out_grad,
        )

    return local


def solution(mesh):
    in_specs = (
        P(("batch", "head"), None),
        P(),
        P(None, "head"),
        P(None, "head"),
        P(None, "head"),
        P("head", None),
        P(),
        P(),
        P(),
        P(),
        P(("batch", "head")),
        P(("batch", "head")),
        P(("batch", "head"), None),
    )
    out_specs = (
        P(("batch", "head"), None),
        P(("batch", "head"), None),
        P(),
        P(None, "head"),
        P(None, "head"),
        P(None, "head"),
        P("head", None),
        P(),
        P(),
        P(),
        P(),
    )
    return jax.shard_map(
        build(mesh), mesh=mesh, in_specs=in_specs, out_specs=out_specs, check_vma=False
    )
```

```python
import functools

import jax
import jax.numpy as jnp
from jax import lax
from jax.experimental import pallas as pl
from jax.experimental.pallas import tpu as pltpu
from jax.sharding import PartitionSpec as P

HD = 64
LENGTH = 1024
WIDTH = 128
BF = jnp.bfloat16
F32 = jnp.float32
LOG2E = 1.4426950408889634
LN2 = 0.6931471805599453
VMEM = 20 * 2**20
FULL_VMEM = 56 * 2**20

eps = 1e-06
last_dims = (((1,), (1,)), ((), ()))
first_dims = (((0,), (0,)), ((), ()))


def dot(left, right):
    return jnp.dot(left, right, preferred_element_type=F32)


def dot_last(left, right):
    return lax.dot_general(left, right, last_dims, preferred_element_type=F32)


def dot_first(left, right):
    return lax.dot_general(left, right, first_dims, preferred_element_type=F32)


def split3(value):
    high = value.astype(BF)
    rest = value - high.astype(F32)
    mid = rest.astype(BF)
    low = (rest - mid.astype(F32)).astype(BF)
    return high, mid, low


def call(
    body, name, grid, in_specs, out_specs, out_shape, flops, moved, exps=0, vmem=VMEM, **extra
):
    return pl.pallas_call(
        body,
        grid=grid,
        in_specs=in_specs,
        out_specs=out_specs,
        out_shape=out_shape,
        compiler_params=pltpu.CompilerParams(vmem_limit_bytes=vmem),
        cost_estimate=pl.CostEstimate(
            flops=int(flops), bytes_accessed=int(moved), transcendentals=int(exps)
        ),
        name=name,
        **extra,
    )


def row_block(columns):
    return pl.BlockSpec((LENGTH, columns), lambda s: (s, 0))


def whole(*shape):
    return pl.BlockSpec(shape, lambda s: (0,) * len(shape))


def head_lanes(rows, head):
    lane = lax.broadcasted_iota(jnp.int32, (rows, WIDTH), 1)
    mine = (lane < HD) if head == 0 else (lane >= HD)
    return lane, mine, HD if head == 0 else 0


def with_extra(mine, lane, other, values, extra):
    high, mid, low = split3(extra)
    filler = jnp.zeros_like(values)
    for place, part in ((2, low), (1, mid), (0, high)):
        filler = jnp.where(lane == other + place, part, filler)
    return jnp.where(mine, values, filler)


def twice(mine, values):
    return jnp.where(mine, values, jnp.roll(values, HD, axis=1))


def scaled_queries(mine, q):
    long = q.astype(F32) * (HD**-0.5 * LOG2E)
    high = long.astype(BF)
    low = (long - high.astype(F32)).astype(BF)
    return jnp.where(mine, high, jnp.roll(low, HD, axis=1))


def attend(normed, weights, q_ref, k_ref, v_ref, logsum_ref, ctx_ref):
    block = 256
    r = lax.broadcasted_iota(jnp.int32, (WIDTH, WIDTH), 0)
    c = lax.broadcasted_iota(jnp.int32, (WIDTH, WIDTH), 1)
    same_head = jnp.where((r < HD) == (c < HD), 1.0, 0.0).astype(BF)

    def most(values):
        long = values.astype(F32)
        return jnp.max(dot((long * long).astype(BF), same_head), axis=0, keepdims=True)

    bounds = []
    for slot, weight in enumerate(weights):
        qkv = dot(normed, weight)
        q = qkv[:, :WIDTH].astype(BF)
        k = qkv[:, WIDTH : 2 * WIDTH].astype(BF)
        q_ref[slot] = q
        k_ref[slot] = k
        v_ref[slot] = qkv[:, 2 * WIDTH :].astype(BF)
        bounds.append(most(q) * most(k))
    bound = jnp.max(functools.reduce(jnp.maximum, bounds))

    def finish(slot, head, here, out, peak):
        lane_b, mine_b, other = head_lanes(block, head)
        total = out[:, other : other + 1]
        logsum = jnp.log2(total) + peak
        context = (out * (1.0 / total)).astype(BF)
        marks = with_extra(jnp.full_like(mine_b, False), lane_b, head * HD, context, logsum)
        if head == 1:
            context = jnp.where(mine_b, context, ctx_ref[slot, here])
            marks = jnp.where(mine_b, marks, logsum_ref[slot, here])
        ctx_ref[slot, here] = context
        logsum_ref[slot, here] = marks

    def head_keys(slot, head):
        lane, mine, other = head_lanes(LENGTH, head)
        vh = jnp.where(mine, v_ref[slot], (lane == other).astype(F32).astype(BF))
        return twice(mine, k_ref[slot]), vh

    def rows_small(slot, head):
        kh, vh = head_keys(slot, head)
        qh = scaled_queries(head_lanes(LENGTH, head)[1], q_ref[slot])
        for start in range(0, LENGTH, block):
            here = slice(start, start + block)
            queries = qh[here]
            scores = []
            for at in range(0, start + block, block):
                part = dot_last(queries, kh[at : at + block])
                if at == start:
                    r = lax.broadcasted_iota(jnp.int32, (block, block), 0)
                    c = lax.broadcasted_iota(jnp.int32, (block, block), 1)
                    part = jnp.where(c <= r, part, -1e30)
                scores.append(part)
            out = 0.0
            for index, part in enumerate(scores):
                out = out + dot(
                    jnp.exp2(part).astype(BF), vh[index * block : (index + 1) * block]
                )
            finish(slot, head, here, out, 0.0)

    def rows_large(slot, head):
        @pl.loop(0, LENGTH // block)
        def _(index):
            kh, vh = head_keys(slot, head)
            here = pl.ds(pl.multiple_of(index * block, block), block)
            queries = scaled_queries(head_lanes(block, head)[1], q_ref[slot, here])
            scores = dot_last(queries, kh)
            r = lax.broadcasted_iota(jnp.int32, scores.shape, 0) + index * block
            c = lax.broadcasted_iota(jnp.int32, scores.shape, 1)
            scores = jnp.where(c <= r, scores, -1e30)
            peak = jnp.max(scores, axis=1, keepdims=True)
            finish(slot, head, here, dot(jnp.exp2(scores - peak).astype(BF), vh), peak)

    small = bound * (HD**-0.5 * LOG2E) ** 2 * 1.1 < 1e4

    @pl.when(small)
    def _():
        for slot in range(len(weights)):
            for head in range(2):
                rows_small(slot, head)

    @pl.when(jnp.logical_not(small))
    def _():
        for head in range(2):

            @pl.loop(0, len(weights))
            def _(slot):
                rows_large(slot, head)


def norm_rows(rows):
    return rows * lax.rsqrt(jnp.mean(rows * rows, axis=-1, keepdims=True) + eps)


def pack_weights(q_ref, k_ref, v_ref, o_ref, packed_ref):
    for index, ref in enumerate((q_ref, k_ref, v_ref)):
        packed_ref[:, index * WIDTH : (index + 1) * WIDTH] = ref[...]
    packed_ref[:, 3 * WIDTH :] = o_ref[...].T


def run_pack(q, k, v, o):
    width = q.shape[0]
    return call(
        pack_weights,
        "pack_weights",
        (),
        [pl.BlockSpec(memory_space=pltpu.VMEM)] * 4,
        pl.BlockSpec(memory_space=pltpu.VMEM),
        jax.ShapeDtypeStruct((width, 4 * WIDTH), BF),
        1e6,
        2e6,
        vmem=FULL_VMEM,
    )(q, k, v, o)


def forward_first(x_ref, gain_ref, *refs):
    slots = len(refs) - 6
    normed_ref, *saved = refs[slots:]
    normed = (norm_rows(x_ref[...].astype(F32)) * gain_ref[...]).astype(BF)
    normed_ref[...] = normed
    attend(normed, [ref[:, : 3 * WIDTH] for ref in refs[:slots]], *saved)


def forward_last(
    ids_ref, normed_ref, x_ref, ctx_in_ref, ffn_gain_ref, control_ref, cot_ref, group_ref,
    live_ref, *refs
):
    slots = len(refs) - 12
    weights = refs[:slots]
    *saved, middle_ref, normed2_ref = refs[slots : slots + 7]
    *groups, normed2_all, logits_all = refs[slots + 7 :]
    ctx_ref = saved[-1]
    normed = normed_ref[...]
    before = ctx_in_ref.shape[0]
    attend(normed, [ref[:, : 3 * WIDTH] for ref in weights[before:]], *saved)
    sequence = pl.program_id(0)
    here = pl.ds(pl.multiple_of(sequence * LENGTH, LENGTH), LENGTH)
    context = jnp.concatenate(
        [ctx_in_ref[i] for i in range(before)] + [ctx_ref[i] for i in range(slots - before)],
        axis=1,
    )
    flipped = jnp.concatenate([ref[:, -WIDTH:] for ref in weights], axis=1)
    middle = x_ref[...].astype(F32) + dot_last(context, flipped)
    middle_ref[...] = middle
    normed2 = (norm_rows(middle) * ffn_gain_ref[...]).astype(BF)
    normed2_ref[...] = normed2
    normed2_all[here] = normed2
    logits_all[here] = dot_last(normed2, control_ref[...])

    @pl.when(sequence == pl.num_programs(0) - 1)
    def _():
        gather_groups(
            ids_ref, logits_all, normed2_all, cot_ref, group_ref, live_ref, *groups
        )


def slot_outputs(slots, tokens):
    per = pl.BlockSpec((slots, LENGTH, WIDTH), lambda s: (0, s, 0))
    return [per] * 5, [jax.ShapeDtypeStruct((slots, tokens, WIDTH), BF)] * 5


def run_forward_first(x, gain, weights):
    tokens, width = x.shape
    specs, shapes = slot_outputs(len(weights), tokens)
    return call(
        forward_first,
        "attention_forward_first",
        (tokens // LENGTH,),
        [row_block(width), whole(1, width)] + [whole(width, 4 * WIDTH)] * len(weights),
        [row_block(width)] + specs,
        [jax.ShapeDtypeStruct((tokens, width), BF)] + shapes,
        1.5e10,
        1e7,
        1e7,
        vmem=FULL_VMEM,
    )(x, gain, *weights)


def run_forward_last(ids, normed, x, ctx, ffn_gain, control, cot, group, live, weights):
    tokens, width = x.shape
    groups = tokens // 8
    before = ctx.shape[0]
    specs, shapes = slot_outputs(len(weights) - before, tokens)
    sums = jax.ShapeDtypeStruct((2, groups, width), BF)
    return call(
        forward_last,
        "attention_forward_last",
        (tokens // LENGTH,),
        [
            pl.BlockSpec(memory_space=pltpu.SMEM),
            row_block(width),
            row_block(width),
            pl.BlockSpec((before, LENGTH, WIDTH), lambda s: (0, s, 0)),
            whole(1, width),
            whole(2, width),
            whole(tokens, width),
            whole(1, tokens),
            whole(1, tokens),
        ]
        + [pl.BlockSpec((width, WIDTH), lambda s: (0, 3))] * before
        + [whole(width, 4 * WIDTH)] * (len(weights) - before),
        specs
        + [row_block(width), row_block(width), whole(tokens, WIDTH)]
        + [whole(2, groups, width)] * 2,
        shapes
        + [
            jax.ShapeDtypeStruct((tokens, width), F32),
            jax.ShapeDtypeStruct((tokens, width), BF),
            jax.ShapeDtypeStruct((tokens, WIDTH), F32),
            sums,
            sums,
        ],
        1.5e10,
        1e7,
        1e7,
        vmem=40 * 2**20,
        scratch_shapes=[pltpu.VMEM((tokens, width), BF), pltpu.VMEM((tokens, 2), F32)],
    )(ids, normed, x, ctx, ffn_gain, control, cot, group, live, *weights)


def backward_items(
    slots, items_ref, q_ref, k_ref, v_ref, logsum_ref, ctx_ref, ml_ref, normed_ref, *refs
):
    dqkv_ref, dw_ref = refs[-2:]
    item = pl.program_id(0)
    weight = refs[0][...]
    for index in range(1, slots):
        weight = jnp.where(items_ref[0, item] == index, refs[index][...], weight)
    block = 256
    ml = ml_ref[...]
    ctx = ctx_ref[0]
    d_out = dot(ml, weight).astype(BF)
    product = d_out.astype(F32) * ctx.astype(F32)
    q = q_ref[0]
    k = k_ref[0]
    v = v_ref[0]
    logsum = logsum_ref[0]
    k_flip = k.T
    dks, dvs, dqs = [], [], []
    for head in range(2):
        lane, mine, other = head_lanes(LENGTH, head)
        minus = jnp.where((lane >= other) & (lane < other + 3), -1.0, 0.0).astype(BF)
        minus_own = jnp.where((lane >= HD - other) & (lane < HD - other + 3), -1.0, 0.0).astype(BF)
        central = jnp.sum(jnp.where(mine, product, 0.0), axis=1, keepdims=True)
        d_all = with_extra(mine, lane, other, d_out, central)
        v_all = jnp.where(mine, v, minus)
        k_all = jnp.concatenate([twice(mine, k), minus_own], axis=1)
        q_scaled = scaled_queries(mine, q)
        q_all = jnp.concatenate([q_scaled, logsum], axis=1)
        dq = [0.0] * (LENGTH // block)
        dk, dv = [], []
        for at in range(0, LENGTH, block):
            keys = k_all[at : at + block]
            values = v_all[at : at + block]
            flipped = k_flip[head * HD : (head + 1) * HD, at : at + block]
            probs = jnp.exp2(dot_last(keys, q_all[at:]))
            r = lax.broadcasted_iota(jnp.int32, (block, block), 0)
            c = lax.broadcasted_iota(jnp.int32, (block, block), 1)
            corner = jnp.where(r <= c, probs[:, :block], 0.0)
            probs = corner if at + block == LENGTH else jnp.concatenate([corner, probs[:, block:]], axis=1)
            d_scores = (probs * dot_last(values, d_all[at:])).astype(BF)
            dv.append(dot(probs.astype(BF), d_all[at:]))
            dk.append(dot(d_scores, q_scaled[at:]))
            part = dot(flipped, d_scores)
            for start in range(at, LENGTH, block):
                dq[start // block] = dq[start // block] + part[:, start - at : start - at + block]
        dk = jnp.concatenate(dk, axis=0)
        dks.append(dk + jnp.roll(dk, HD, axis=1))
        dvs.append(jnp.concatenate(dv, axis=0))
        dqs.append(jnp.concatenate(dq, axis=1))
    lane, mine, _ = head_lanes(LENGTH, 0)
    dk = (jnp.where(mine, dks[0], dks[1]) * LN2).astype(BF)
    dv = jnp.where(mine, dvs[0], dvs[1]).astype(BF)
    dq_flip = (jnp.concatenate(dqs, axis=0) * HD**-0.5).astype(BF)
    dqkv_ref[0, :, :WIDTH] = dq_flip.T
    dqkv_ref[0, :, WIDTH : 2 * WIDTH] = dk
    dqkv_ref[0, :, 2 * WIDTH :] = dv
    dw = dot(jnp.concatenate([dq_flip, dk.T, dv.T], axis=0), normed_ref[...])
    dwo = dot_first(ctx, ml)
    parts = [dw[:WIDTH], dw[WIDTH : 2 * WIDTH], dw[2 * WIDTH :], dwo]
    adds = items_ref[2, item]
    earlier = refs[slots + 1] if len(refs) > slots + 2 else None

    @pl.when(adds == 0)
    def _():
        for index, part in enumerate(parts):
            dw_ref[0, index] = part

    @pl.when(adds == 1)
    def _():
        for index, part in enumerate(parts):
            dw_ref[0, index] += part

    if earlier is not None:

        @pl.when(adds == 2)
        def _():
            for index, part in enumerate(parts):
                dw_ref[0, index] = earlier[0, index] + part


def run_backward(saved, ml, weights, normed, items, done=(), earlier=None, flops=6e9):
    tokens, width = ml.shape
    slots = len(weights)
    table = [[], [], []]
    for index, (slot, sequence) in enumerate(items):
        seen = [one for one in items[:index] if one[0] == slot]
        before = [one for one in done if one[0] == slot]
        table[0].append(slot)
        table[1].append(sequence)
        table[2].append(1 if seen else 2 if before else 0)
    table = jnp.array(table, jnp.int32)
    per = pl.BlockSpec((1, LENGTH, WIDTH), lambda i, t: (t[0, i], t[1, i], 0))
    rows = pl.BlockSpec((LENGTH, width), lambda i, t: (t[1, i], 0))
    sums = pl.BlockSpec((1, 4, WIDTH, width), lambda i, t: (t[0, i], 0, 0, 0))
    args = [table, *saved, ml, normed, *weights]
    in_specs = [*([per] * 5), rows, rows]
    in_specs += [pl.BlockSpec((width, WIDTH), lambda i, t: (0, 3))] * slots
    aliases = {}
    if earlier is not None:
        aliases = {len(args): 0, len(args) + 1: 1}
        args += list(earlier)
        in_specs += [pl.BlockSpec(memory_space=pl.ANY), sums]
    return pl.pallas_call(
        functools.partial(backward_items, slots),
        grid_spec=pltpu.PrefetchScalarGridSpec(
            num_scalar_prefetch=1,
            grid=(len(items),),
            in_specs=in_specs,
            out_specs=[pl.BlockSpec((1, LENGTH, 3 * WIDTH), lambda i, t: (t[0, i], t[1, i], 0)), sums],
        ),
        out_shape=[
            jax.ShapeDtypeStruct((slots, tokens, 3 * WIDTH), BF),
            jax.ShapeDtypeStruct((slots, 4, WIDTH, width), F32),
        ],
        input_output_aliases=aliases,
        compiler_params=pltpu.CompilerParams(vmem_limit_bytes=VMEM),
        cost_estimate=pl.CostEstimate(
            flops=int(flops * len(items)), bytes_accessed=1, transcendentals=0
        ),
        name="attention_backward",
    )(*args)


def group_marks(group, alive, groups):
    slot = lax.broadcasted_iota(jnp.int32, (groups, group.shape[1]), 0).astype(F32)
    return jnp.where((slot == group) & (alive > 0), 1.0, 0.0).astype(BF)


def token_marks(columns, groups):
    slot = lax.broadcasted_iota(jnp.int32, (columns.shape[0], groups), 1).astype(F32)
    return jnp.where((slot == columns[:, 2:3]) & (columns[:, 3:4] > 0), 1.0, 0.0).astype(BF)


def dot_exact(marks, values):
    return functools.reduce(jnp.add, [dot(marks, part) for part in split3(values)])


def gather_groups(
    ids_ref, logits_ref, normed2_ref, cot_ref, group_ref, live_ref, columns_ref, keep_ref, send_ref
):
    tokens = normed2_ref.shape[0]
    groups = keep_ref.shape[1]
    group = group_ref[...].astype(F32)
    alive = live_ref[...].astype(F32)
    row = lax.broadcasted_iota(jnp.int32, (WIDTH, tokens), 0)
    turned = jnp.where(row == 2, group, jnp.where(row == 3, alive, 0.0)).T
    marks = group_marks(group, alive, groups)
    token_side = token_marks(turned, groups)
    live = turned[:, 3:4]
    lane = lax.broadcasted_iota(jnp.int32, (tokens, WIDTH), 1)
    logits = jnp.concatenate([logits_ref[...], jnp.zeros((tokens, WIDTH - 2), F32)], axis=1)
    expo = jnp.exp(logits) * live
    totals = dot_exact(marks, expo)
    weights = expo / (dot_exact(token_side, totals) + (1.0 - live))
    columns_ref[...] = jnp.where(lane < 2, weights, turned)
    rows = weights.T[:8].astype(BF)
    own = ids_ref[0] == 0
    normed2 = normed2_ref[...]
    cot = cot_ref[...]
    for ref, pick in ((keep_ref, own), (send_ref, jnp.logical_not(own))):
        assign = marks * jnp.where(pick, rows[0:1].astype(F32), rows[1:2].astype(F32)).astype(BF)
        ref[0] = dot(assign, normed2).astype(BF)
        ref[1] = dot(assign, cot).astype(BF)


def gelu_both(x):
    inner = 0.7978845608028654
    cubic = 0.044715
    square = x * x
    bent = jnp.tanh(inner * x * (1.0 + cubic * square))
    half = 0.5 * (1.0 + bent)
    slope = half + 0.5 * x * (1.0 - bent * bent) * (inner * (1.0 + 3.0 * cubic * square))
    return x * half, slope


SPLIT = (176, 176, 160)


def expert_step(
    ids_ref, keep_ref, got_ref, in_ref, out_ref, *refs
):
    kept_refs, sent_refs = refs[:3], refs[3:6]
    home_ref, away_ref, mixed_flip, result, mixed_grad, in_all, out_all, sems = refs[6:]
    step = pl.program_id(0)
    groups = keep_ref.shape[1]
    mixed = jnp.concatenate([keep_ref[0], got_ref[0]], axis=0)
    d_result = jnp.concatenate([keep_ref[1], got_ref[1]], axis=0)
    wide = in_all.shape[2]

    def loads(at):
        span = pl.ds(pl.multiple_of(at * wide, wide), wide)
        return [
            pltpu.make_async_copy(in_ref.at[ids_ref[0], :, span], in_all.at[at], sems.at[0, at]),
            pltpu.make_async_copy(out_ref.at[ids_ref[0], span], out_all.at[at], sems.at[1, at]),
        ]

    @pl.when(step == 0)
    def _():
        for at in range(in_all.shape[0]):
            for load in loads(at):
                load.start()
        mixed_flip[...] = mixed.T
        result[...] = jnp.zeros_like(result)
        mixed_grad[...] = jnp.zeros_like(mixed_grad)

    for load in loads(step):
        load.wait()
    w_in = in_all[step]
    w_out = out_all[step]
    active, slope = gelu_both(dot(mixed, w_in))
    active = active.astype(BF)
    d_before = (dot_last(d_result, w_out) * slope).astype(BF)
    result[...] += dot(active, w_out)
    mixed_grad[...] += dot_last(d_before, w_in)
    d_out = dot_first(active, d_result).astype(BF)
    d_in = dot(mixed_flip[...], d_before).astype(BF)
    half = d_in.shape[0] // 2
    for index in range(2):
        columns = slice(index * half, (index + 1) * half)
        side = d_in[:, columns]
        block = jnp.concatenate(
            [d_out[columns], jnp.concatenate([side[:half], side[half:]], axis=1)], axis=0
        )
        at = 0
        for part, rows in enumerate(SPLIT):
            place = jnp.bitwise_xor(2 * step + index, ids_ref[part + 1])
            piece = block[at : at + rows]
            at += rows

            @pl.when(place < 4)
            def _():
                kept_refs[part][place] = piece

            @pl.when(place >= 4)
            def _():
                sent_refs[part][place - 4] = piece

    @pl.when(step == pl.num_programs(0) - 1)
    def _():
        home_ref[0] = result[:groups].astype(BF)
        home_ref[1] = mixed_grad[:groups].astype(BF)
        away_ref[0] = result[groups:].astype(BF)
        away_ref[1] = mixed_grad[groups:].astype(BF)


def run_experts(ids, keep, got, expert_in, expert_out):
    _, width, hidden = expert_in.shape
    steps = 4
    wide = hidden // steps
    groups = keep.shape[1]
    sums = jax.ShapeDtypeStruct(keep.shape, BF)
    halves = [(4, rows, width) for rows in SPLIT] * 2
    hbm = pl.BlockSpec(memory_space=pltpu.HBM)
    return call(
        expert_step,
        "experts",
        (steps,),
        [pl.BlockSpec(memory_space=pltpu.SMEM), whole(*keep.shape), whole(*keep.shape), hbm, hbm],
        [whole(*shape) for shape in halves + [keep.shape] * 2],
        [jax.ShapeDtypeStruct(shape, BF) for shape in halves] + [sums, sums],
        1e10,
        1.2e7,
        1e6,
        scratch_shapes=[
            pltpu.VMEM((width, 2 * groups), BF),
            pltpu.VMEM((2 * groups, width), F32),
            pltpu.VMEM((2 * groups, width), F32),
            pltpu.VMEM((steps, width, wide), BF),
            pltpu.VMEM((steps, wide, width), BF),
            pltpu.SemaphoreType.DMA((2, steps)),
        ],
    )(ids, keep, got, expert_in, expert_out)


def spread_groups(
    ids_ref, middle_ref, normed2_ref, cot_ref, columns_ref, group_ref, live_ref, home_ref, got_ref,
    gain_ref, control_ref, out_ref, low_ref, small_ref,
    table, mixed_part, weight_grads, group_sums,
):
    phase, index = pl.program_id(0), pl.program_id(1)
    rows, width = middle_ref.shape
    groups = home_ref.shape[1]
    here = pl.ds(pl.multiple_of(index * rows, rows), rows)

    @pl.when((phase == 0) & (index == 0))
    def _():
        group_sums[...] = jnp.zeros_like(group_sums)
        small_ref[...] = jnp.zeros_like(small_ref)
        own = ids_ref[0] == 0
        for kind in range(2):
            home, got = home_ref[kind], got_ref[kind]
            at = 2 * kind * width
            table[:, at : at + width] = jnp.where(own, home, got)
            table[:, at + width : at + 2 * width] = jnp.where(own, got, home)

    @pl.when(phase == 0)
    def _():
        columns = columns_ref[...]
        lane = lax.broadcasted_iota(jnp.int32, columns.shape, 1)
        token_side = token_marks(columns, groups)
        spread = dot(token_side, table[...])
        cot = cot_ref[...]
        normed2 = normed2_ref[...]
        middle = middle_ref[...]
        cot = cot.astype(F32)
        normed2 = normed2.astype(F32)
        low = columns.astype(BF).astype(F32)
        first, second = low[:, 0:1], low[:, 1:2]
        result = [spread[:, i * width : (i + 1) * width] for i in range(4)]
        out_ref[...] = (middle + first * result[0] + second * result[1]).astype(BF)
        mixed_part[here] = first * result[2] + second * result[3]
        grads = [
            jnp.sum(cot * result[i] + normed2 * result[2 + i], axis=1, keepdims=True)
            for i in range(2)
        ]
        grads = jnp.where(lane == 0, grads[0], jnp.where(lane == 1, grads[1], 0.0))
        pulls = jnp.where(lane < 2, columns * grads, 0.0)
        weight_grads[here] = pulls
        group = group_ref[...].astype(F32)
        alive = live_ref[...].astype(F32)
        group_sums[...] += dot_exact(group_marks(group, alive, groups), pulls)

    @pl.when(phase == 1)
    def _():
        columns = columns_ref[...]
        central = dot_exact(token_marks(columns, groups), group_sums[...])
        logit_grads = weight_grads[here] - columns * central
        first, second = logit_grads[:, 0:1], logit_grads[:, 1:2]
        control = control_ref[...].astype(F32)
        cot = cot_ref[...].astype(F32)
        normed2 = normed2_ref[...].astype(F32)
        middle = middle_ref[...]
        grad = mixed_part[here] + first * control[0:1] + second * control[1:2]
        scale = lax.rsqrt(jnp.mean(middle * middle, axis=-1, keepdims=True) + eps)
        unit = middle * scale
        pulled = grad * gain_ref[...]
        pulled = scale * (pulled - unit * jnp.mean(pulled * unit, axis=-1, keepdims=True))
        low_ref[...] = (cot + pulled).astype(BF)
        small_ref[0:1] += jnp.sum(grad * unit, axis=0, keepdims=True)
        small_ref[1:2] += jnp.sum(first * normed2, axis=0, keepdims=True)
        small_ref[2:3] += jnp.sum(second * normed2, axis=0, keepdims=True)


def run_spread(ids, middle, normed2, cot, columns, group, live, home, got, gain, control):
    tokens, width = middle.shape
    groups = home.shape[1]
    rows = 512
    steps = tokens // rows
    by_block = lambda n: pl.BlockSpec((rows, n), lambda p, b: (b, 0))
    fixed = lambda *shape: pl.BlockSpec(shape, lambda p, b: (0,) * len(shape))
    return call(
        spread_groups,
        "spread_groups",
        (2, steps),
        [
            pl.BlockSpec(memory_space=pltpu.SMEM),
            by_block(width),
            by_block(width),
            by_block(width),
            by_block(WIDTH),
            pl.BlockSpec((1, rows), lambda p, b: (0, b)),
            pl.BlockSpec((1, rows), lambda p, b: (0, b)),
            fixed(*home.shape),
            fixed(*home.shape),
            fixed(1, width),
            fixed(2, width),
        ],
        [
            pl.BlockSpec((rows, width), lambda p, b: (b * (1 - p) + (steps - 1) * p, 0)),
            pl.BlockSpec((rows, width), lambda p, b: (b * p, 0)),
            fixed(8, width),
        ],
        [
            jax.ShapeDtypeStruct((tokens, width), BF),
            jax.ShapeDtypeStruct((tokens, width), BF),
            jax.ShapeDtypeStruct((8, width), F32),
        ],
        8e9,
        2e7,
        scratch_shapes=[
            pltpu.VMEM((groups, 4 * width), BF),
            pltpu.VMEM((tokens, width), F32),
            pltpu.VMEM((tokens, WIDTH), F32),
            pltpu.VMEM((groups, WIDTH), F32),
        ],
    )(ids, middle, normed2, cot, columns, group, live, home, got, gain, control)


def input_rows(x_ref, gain_ref, grad_ref, *refs):
    slots = 4
    flats, weights, out_ref = refs[: -slots - 1], refs[-slots - 1 : -1], refs[-1]
    rows = x_ref[...].astype(F32)
    grad = dot_last(
        jnp.concatenate([flat[i] for flat in flats for i in range(flat.shape[0])], axis=1),
        jnp.concatenate([weight[:, : 3 * WIDTH] for weight in weights], axis=1),
    )
    scale = lax.rsqrt(jnp.mean(rows * rows, axis=-1, keepdims=True) + eps)
    unit = rows * scale
    pulled = grad * gain_ref[...]
    pulled = scale * (pulled - unit * jnp.mean(pulled * unit, axis=-1, keepdims=True))
    out_ref[...] = grad_ref[...].astype(F32) + pulled


def run_input(x, gain, grad, flats, weights):
    tokens, width = x.shape
    rows = 512
    by_block = lambda n: pl.BlockSpec((rows, n), lambda s: (s, 0))
    return call(
        input_rows,
        "input_rows",
        (tokens // rows,),
        [by_block(width), whole(1, width), by_block(width)]
        + [
            pl.BlockSpec((flat.shape[0], rows, 3 * WIDTH), lambda s: (0, s, 0)) for flat in flats
        ]
        + [whole(width, 4 * WIDTH)] * len(weights),
        by_block(width),
        jax.ShapeDtypeStruct((tokens, width), F32),
        1,
        1,
        vmem=FULL_VMEM,
    )(x, gain, grad, *flats, *weights)


def join_own(
    ids_ref, own_ref, one_ref, two_ref, weight_ref, gain_ref, rest_ref, kept_ref, sent_ref, small_ref
):
    half = kept_ref.shape[0]
    flipped = weight_ref[:, : 3 * WIDTH].T.astype(F32)
    gain_grad = 0.0
    for place in range(2 * half):
        total = own_ref[0, place] + one_ref[place].astype(F32) + two_ref[place].astype(F32)
        if place < 3:
            part = flipped[place * WIDTH : (place + 1) * WIDTH] * total
            gain_grad = gain_grad + jnp.sum(part, axis=0, keepdims=True)
        index = jnp.bitwise_xor(place, ids_ref[4])
        total = total.astype(BF)

        @pl.when(index < half)
        def _():
            kept_ref[index] = total

        @pl.when(index >= half)
        def _():
            sent_ref[index - half] = total

    small_ref[...] = rest_ref[...]
    small_ref[3:4] = gain_grad / gain_ref[...]


def run_join(ids, own, one, two, weight, gain, rest):
    _, n, rows, width = own.shape
    vmem = pl.BlockSpec(memory_space=pltpu.VMEM)
    return call(
        join_own,
        "join_own",
        (),
        [pl.BlockSpec(memory_space=pltpu.SMEM)] + [vmem] * 6,
        [vmem] * 3,
        [jax.ShapeDtypeStruct((n // 2, rows, width), BF)] * 2
        + [jax.ShapeDtypeStruct(rest.shape, F32)],
        1,
        1,
    )(ids, own, one, two, weight, gain, rest)


def open_own(ids_ref, small_ref, small_got_ref, own_ref, *refs):
    gots, outs, (attn_ref, ffn_ref, control_ref) = refs[:3], refs[3:7], refs[7:]
    small = small_ref[...] + small_got_ref[...]
    ffn_ref[...] = small[0:1]
    control_ref[...] = small[1:3]
    attn_ref[...] = small[3:4]
    for index, out in enumerate(outs):
        place = jnp.bitwise_xor(index, ids_ref[4])
        value = own_ref[0]
        for at, got in enumerate(gots):
            value = jnp.where(place == at + 1, got[0], value)
        value = value.astype(F32)
        out[...] = value if index == 3 else value.T


def run_open(ids, small, small_got, own, gots):
    _, rows, width = own.shape
    vmem = pl.BlockSpec(memory_space=pltpu.VMEM)
    return call(
        open_own,
        "open_own",
        (),
        [pl.BlockSpec(memory_space=pltpu.SMEM)] + [vmem] * 6,
        [vmem] * 7,
        [jax.ShapeDtypeStruct((width, rows), F32)] * 3
        + [jax.ShapeDtypeStruct((rows, width), F32)]
        + [jax.ShapeDtypeStruct((n, width), F32) for n in (1, 1, 2)],
        1e6,
        2e6,
    )(ids, small, small_got, own, *gots)


def part_regions(index, half):
    start = sum(SPLIT[:index])
    regions = []
    for low, high, output in ((0, half, 1), (half, 2 * half, 0)):
        first, last = max(start, low), min(start + SPLIT[index], high)
        if first < last:
            regions.append((first - start, last - first, output, first - low))
    return regions


def open_experts(base, ids_ref, *refs):
    sources, (in_ref, out_ref, stage, sems) = refs[:-4], refs[-4:]
    joined = len(sources) in (4, 6) and sources[3].shape[1] == sum(SPLIT)
    half = stage.shape[2] // 2
    copies = []
    for side in range(2):
        expert = ids_ref[0] if side == 0 else 1 - ids_ref[0]
        for index in range(3):
            rows = SPLIT[index]
            for spot in range(4):
                slot = (side * 3 + index) * 4 + spot
                place = jnp.bitwise_xor(base + spot, ids_ref[index + 1])
                columns = pl.ds(pl.multiple_of(place * half, half), half)
                if side == 1 and joined:
                    at = sum(SPLIT[:index])
                    piece = sources[3][spot, at : at + rows]
                else:
                    piece = sources[3 * side + index][spot]
                stage[slot, :rows] = piece.astype(F32)
                for start, count, output, at in part_regions(index, half):
                    if output == 1:
                        copies.append(
                            pltpu.make_async_copy(
                                stage.at[slot, pl.ds(start, count)],
                                out_ref.at[expert, pl.ds(place * half + at, count)],
                                sems.at[len(copies)],
                            )
                        )
                        copies[-1].start()
                        continue
                    for part in range(2):
                        copies.append(
                            pltpu.make_async_copy(
                                stage.at[slot, pl.ds(start, count), pl.ds(part * half, half)],
                                in_ref.at[expert, pl.ds(part * half + at, count), columns],
                                sems.at[len(copies)],
                            )
                        )
                        copies[-1].start()
    for copy in copies:
        copy.wait()


def run_open_experts(ids, base, args, shape_in, shape_out, begun=()):
    vmem = pl.BlockSpec(memory_space=pltpu.VMEM)
    hbm = pl.BlockSpec(memory_space=pl.ANY)
    copies = 8 * sum(1 if region[2] else 2 for i in range(3) for region in part_regions(i, 256))
    return call(
        functools.partial(open_experts, base),
        "open_experts",
        (),
        [pl.BlockSpec(memory_space=pltpu.SMEM)] + [vmem] * len(args) + [hbm] * len(begun),
        [hbm] * 2,
        [jax.ShapeDtypeStruct(shape_in, F32), jax.ShapeDtypeStruct(shape_out, F32)],
        1e10 if base else 1,
        1e7 if base else 1,
        scratch_shapes=[
            pltpu.VMEM((24, max(SPLIT), shape_out[2]), F32),
            pltpu.SemaphoreType.DMA((copies,)),
        ],
        input_output_aliases={1 + len(args) + i: i for i in range(len(begun))},
    )(ids, *args, *begun)


def tie(*values):
    return lax.optimization_barrier(values)


def tie_groups(*groups):
    values = iter(tie(*[value for group in groups for value in group]))
    return [[next(values) for _ in group] for group in groups]


def build(mesh):
    n_head, n_batch = mesh.shape["head"], mesh.shape["batch"]
    head_bits = [("head", 1 << i) for i in range(n_head.bit_length() - 1)]
    batch_bits = [("batch", 1 << i) for i in range(n_batch.bit_length() - 1)]
    pair, across = head_bits
    first_batch, second_batch, *last_batch = batch_bits
    orders = [
        (across, first_batch, second_batch),
        (first_batch, second_batch, across),
        (second_batch, across, first_batch),
    ]

    def swap(value, step):
        axis, bit = step
        return lax.ppermute(value, axis, [(i, i ^ bit) for i in range(mesh.shape[axis])])

    def bit_of(step):
        axis, bit = step
        return (lax.axis_index(axis) // bit) % 2

    def number(steps):
        return functools.reduce(lambda value, step: 2 * value + bit_of(step), steps, 0)

    def add(kept, got):
        return (kept.astype(F32) + got.astype(F32)).astype(BF)

    def local(
        inputs,
        attn_gain,
        query_weight,
        key_weight,
        value_weight,
        output_weight,
        ffn_gain,
        controller,
        expert_in,
        expert_out,
        group_ids,
        live_mask,
        cotangent,
    ):
        tokens_here, width = inputs.shape
        sequences = tokens_here // LENGTH
        ids = jnp.stack(
            [bit_of(pair)]
            + [number(order) for order in orders]
            + [number((first_batch, second_batch))]
        ).astype(jnp.int32)
        w0 = run_pack(query_weight, key_weight, value_weight, output_weight)
        w2 = swap(w0, across)
        w1 = swap(w0, pair)
        normed, *saved_a = run_forward_first(inputs, attn_gain[None], [w0, w1])
        w2, normed = tie(w2, normed)
        w3 = swap(w2, pair)
        weights = [w0, w1, w2, w3]
        control = controller.T
        group, live = group_ids[None], live_mask[None]
        *saved_b, middle, normed2, columns, keep, send = run_forward_last(
            ids,
            normed,
            inputs,
            saved_a[-1],
            ffn_gain[None],
            control,
            cotangent,
            group,
            live,
            weights,
        )
        *parts, home, away = run_experts(ids, keep, swap(send, pair), expert_in, expert_out)
        home_got = swap(away, pair)
        kept, sent = parts[:3], parts[3:]
        got = [swap(part, order[0]) for part, order in zip(sent, orders)]

        def send_half(blocks, step):
            half = blocks.shape[0] // 2
            return blocks[:half], swap(blocks[half:], step)

        layer_out, middle_low, small = run_spread(
            ids,
            middle,
            normed2,
            cotangent,
            columns,
            group,
            live,
            home,
            home_got,
            ffn_gain[None],
            control,
        )

        half = sequences // 2

        def next_stage(kept, got, low, mark, stage):
            *got, mark = tie(*got, mark)
            blocks = [add(a, b) for a, b in zip(kept, got)]
            if stage < 3:
                kept = [block[: block.shape[0] // 2] for block in blocks]
                sent = [block[block.shape[0] // 2 :] for block in blocks]
            else:
                kept = sent = blocks
            *sent, low = tie(*sent, low)
            steps = [order[stage] if stage < 3 else last_batch[stage - 3] for order in orders]
            return kept, [swap(block, step) for block, step in zip(sent, steps)], low, mark

        low = middle_low
        early, late = range(half), range(half, sequences)
        first_items = [(1, i) for i in early]
        second_items = [(1, i) for i in late] + [(0, i) for i in early]
        third_items = [(0, i) for i in late]
        far_slots = weights[2:]
        flat, sums = run_backward(saved_b, low, far_slots, normed, first_items)
        kept, got, low, sums = next_stage(kept, got, low, sums, 1)
        flat, sums = run_backward(
            saved_b, low, far_slots, normed, second_items, first_items, (flat, sums)
        )
        kept, got, low, sums = next_stage(kept, got, low, sums, 2)
        third_got = swap(sums[1].astype(BF), pair)
        flat, sums = run_backward(
            saved_b, low, far_slots, normed, third_items, first_items + second_items, (flat, sums)
        )
        kept, got, low, sums = next_stage(kept, got, low, sums, 3)
        for stage in range(4, 3 + len(last_batch)):
            kept, got, low, sums = next_stage(kept, got, low, sums, stage)
        second = (sums[0] + third_got.astype(F32)).astype(BF)
        second, low = tie(second, low)
        second_got = swap(second, across)
        near_items = [(slot, i) for slot in (1, 0) for i in range(sequences)]
        flat_near, sums_near = run_backward(saved_a, low, weights[:2], normed, near_items)
        *got, second_got, sums_near, low = tie(*got, second_got, sums_near, low)

        def widen(blocks, stage):
            return [swap(block, order[stage]) for block, order in zip(blocks, orders)]

        def join(blocks, got):
            return [jnp.concatenate(both, axis=0) for both in zip(blocks, got)]

        def split(value):
            half = value.shape[0] // 2
            return value[:half], value[half:]

        def all_of(value, steps):
            (axis, one), (_, two) = steps
            return [swap(value, (axis, bits)) for bits in (one, two, one | two)]

        first_got = swap(sums_near[1].astype(BF), pair)
        blocks = [add(a, b) for a, b in zip(kept, got)]
        *blocks, low = tie(*blocks, low)
        got = widen(blocks, 2)
        own_kept, own_sent, small = run_join(
            ids, sums_near, second_got, first_got, w0, attn_gain[None], small
        )
        small, own_sent = tie(small + swap(small, pair), own_sent)
        own_got = swap(own_sent, first_batch)
        small_got = swap(small, across)
        *got, small_got, low = tie(*got, small_got, low)

        blocks = join(blocks, got)
        got = widen(blocks, 1)
        own_kept, own_sent = split(add(own_kept, own_got))
        own_got = swap(own_sent, second_batch)
        small = small + small_got
        small_got = swap(small, second_batch)
        *got, own_got, small_got, low = tie(*got, own_got, small_got, low)

        blocks = join(blocks, got)
        blocks_other = swap(jnp.concatenate(blocks, axis=1), pair)
        far = widen(blocks, 0)
        begun = run_open_experts(
            ids, 0, [*blocks, blocks_other], expert_in.shape, expert_out.shape
        )
        own = add(own_kept, own_got)
        small = small + small_got
        for step in last_batch[:-1]:
            own = add(own, swap(own, step))
            small = small + swap(small, step)
        own_got = swap(own, last_batch[-1])
        small_got = swap(small, first_batch)
        input_grad = run_input(inputs, attn_gain[None], low, [flat_near, flat], weights)
        far, (own_got, small_got, input_grad, *begun) = tie_groups(
            far, (own_got, small_got, input_grad, *begun)
        )

        far_other = [swap(block, pair) for block in far]
        own = add(own, own_got)
        own_got = all_of(own, (second_batch, first_batch))
        small = small + small_got
        small_got = swap(small, last_batch[-1])
        expert_grads = run_open_experts(
            ids, 4, [*far, *far_other], expert_in.shape, expert_out.shape, begun
        )
        own_got, (small_got, expert_in_grad, expert_out_grad) = tie_groups(
            own_got, (small_got, *expert_grads)
        )
        query_grad, key_grad, value_grad, output_grad, attn_grad, ffn_grad, control_grad = run_open(
            ids, small, small_got, own, own_got
        )
        return (
            layer_out,
            input_grad,
            attn_grad[0],
            query_grad,
            key_grad,
            value_grad,
            output_grad,
            ffn_grad[0],
            control_grad.T,
            expert_in_grad,
            expert_out_grad,
        )

    return local


def solution(mesh):
    in_specs = (
        P(("batch", "head"), None),
        P(),
        P(None, "head"),
        P(None, "head"),
        P(None, "head"),
        P("head", None),
        P(),
        P(),
        P(),
        P(),
        P(("batch", "head")),
        P(("batch", "head")),
        P(("batch", "head"), None),
    )
    out_specs = (
        P(("batch", "head"), None),
        P(("batch", "head"), None),
        P(),
        P(None, "head"),
        P(None, "head"),
        P(None, "head"),
        P("head", None),
        P(),
        P(),
        P(),
        P(),
    )
    return jax.shard_map(
        build(mesh), mesh=mesh, in_specs=in_specs, out_specs=out_specs, check_vma=False
    )
```

```python
import functools

import jax
import jax.numpy as jnp
from jax import lax
from jax.experimental import pallas as pl
from jax.experimental.pallas import tpu as pltpu
from jax.sharding import PartitionSpec as P

HD = 64
LENGTH = 1024
WIDTH = 128
BF = jnp.bfloat16
F32 = jnp.float32
LOG2E = 1.4426950408889634
LN2 = 0.6931471805599453
VMEM = 20 * 2**20
FULL_VMEM = 56 * 2**20

eps = 1e-06
last_dims = (((1,), (1,)), ((), ()))
first_dims = (((0,), (0,)), ((), ()))


def dot(left, right):
    return jnp.dot(left, right, preferred_element_type=F32)


def dot_last(left, right):
    return lax.dot_general(left, right, last_dims, preferred_element_type=F32)


def dot_first(left, right):
    return lax.dot_general(left, right, first_dims, preferred_element_type=F32)


def split3(value):
    high = value.astype(BF)
    rest = value - high.astype(F32)
    mid = rest.astype(BF)
    low = (rest - mid.astype(F32)).astype(BF)
    return high, mid, low


def call(
    body, name, grid, in_specs, out_specs, out_shape, flops, moved, exps=0, vmem=VMEM, **extra
):
    return pl.pallas_call(
        body,
        grid=grid,
        in_specs=in_specs,
        out_specs=out_specs,
        out_shape=out_shape,
        compiler_params=pltpu.CompilerParams(vmem_limit_bytes=vmem),
        cost_estimate=pl.CostEstimate(
            flops=int(flops), bytes_accessed=int(moved), transcendentals=int(exps)
        ),
        name=name,
        **extra,
    )


def row_block(columns):
    return pl.BlockSpec((LENGTH, columns), lambda s: (s, 0))


def whole(*shape):
    return pl.BlockSpec(shape, lambda s: (0,) * len(shape))


def head_lanes(rows, head):
    lane = lax.broadcasted_iota(jnp.int32, (rows, WIDTH), 1)
    mine = (lane < HD) if head == 0 else (lane >= HD)
    return lane, mine, HD if head == 0 else 0


def with_extra(mine, lane, other, values, extra):
    high, mid, low = split3(extra)
    filler = jnp.zeros_like(values)
    for place, part in ((2, low), (1, mid), (0, high)):
        filler = jnp.where(lane == other + place, part, filler)
    return jnp.where(mine, values, filler)


def twice(mine, values):
    return jnp.where(mine, values, jnp.roll(values, HD, axis=1))


def scaled_queries(mine, q):
    long = q.astype(F32) * (HD**-0.5 * LOG2E)
    high = long.astype(BF)
    low = (long - high.astype(F32)).astype(BF)
    return jnp.where(mine, high, jnp.roll(low, HD, axis=1))


def attend(normed, weights, q_ref, k_ref, v_ref, logsum_ref, ctx_ref):
    block = 256
    r = lax.broadcasted_iota(jnp.int32, (WIDTH, WIDTH), 0)
    c = lax.broadcasted_iota(jnp.int32, (WIDTH, WIDTH), 1)
    same_head = jnp.where((r < HD) == (c < HD), 1.0, 0.0).astype(BF)

    def most(values):
        long = values.astype(F32)
        return jnp.max(dot((long * long).astype(BF), same_head), axis=0, keepdims=True)

    bounds = []
    for slot, weight in enumerate(weights):
        qkv = dot(normed, weight)
        q = qkv[:, :WIDTH].astype(BF)
        k = qkv[:, WIDTH : 2 * WIDTH].astype(BF)
        q_ref[slot] = q
        k_ref[slot] = k
        v_ref[slot] = qkv[:, 2 * WIDTH :].astype(BF)
        bounds.append(most(q) * most(k))
    bound = jnp.max(functools.reduce(jnp.maximum, bounds))

    def finish(slot, head, here, out, peak):
        lane_b, mine_b, other = head_lanes(block, head)
        total = out[:, other : other + 1]
        logsum = jnp.log2(total) + peak
        context = (out * (1.0 / total)).astype(BF)
        marks = with_extra(jnp.full_like(mine_b, False), lane_b, head * HD, context, logsum)
        if head == 1:
            context = jnp.where(mine_b, context, ctx_ref[slot, here])
            marks = jnp.where(mine_b, marks, logsum_ref[slot, here])
        ctx_ref[slot, here] = context
        logsum_ref[slot, here] = marks

    def head_keys(slot, head):
        lane, mine, other = head_lanes(LENGTH, head)
        vh = jnp.where(mine, v_ref[slot], (lane == other).astype(F32).astype(BF))
        return twice(mine, k_ref[slot]), vh

    def rows_small(slot, head):
        kh, vh = head_keys(slot, head)
        qh = scaled_queries(head_lanes(LENGTH, head)[1], q_ref[slot])
        for start in range(0, LENGTH, block):
            here = slice(start, start + block)
            queries = qh[here]
            scores = []
            for at in range(0, start + block, block):
                part = dot_last(queries, kh[at : at + block])
                if at == start:
                    r = lax.broadcasted_iota(jnp.int32, (block, block), 0)
                    c = lax.broadcasted_iota(jnp.int32, (block, block), 1)
                    part = jnp.where(c <= r, part, -1e30)
                scores.append(part)
            out = 0.0
            for index, part in enumerate(scores):
                out = out + dot(
                    jnp.exp2(part).astype(BF), vh[index * block : (index + 1) * block]
                )
            finish(slot, head, here, out, 0.0)

    def rows_large(slot, head):
        @pl.loop(0, LENGTH // block)
        def _(index):
            kh, vh = head_keys(slot, head)
            here = pl.ds(pl.multiple_of(index * block, block), block)
            queries = scaled_queries(head_lanes(block, head)[1], q_ref[slot, here])
            scores = dot_last(queries, kh)
            r = lax.broadcasted_iota(jnp.int32, scores.shape, 0) + index * block
            c = lax.broadcasted_iota(jnp.int32, scores.shape, 1)
            scores = jnp.where(c <= r, scores, -1e30)
            peak = jnp.max(scores, axis=1, keepdims=True)
            finish(slot, head, here, dot(jnp.exp2(scores - peak).astype(BF), vh), peak)

    small = bound * (HD**-0.5 * LOG2E) ** 2 * 1.1 < 1e4

    @pl.when(small)
    def _():
        for slot in range(len(weights)):
            for head in range(2):
                rows_small(slot, head)

    @pl.when(jnp.logical_not(small))
    def _():
        for head in range(2):

            @pl.loop(0, len(weights))
            def _(slot):
                rows_large(slot, head)


def norm_rows(rows):
    return rows * lax.rsqrt(jnp.mean(rows * rows, axis=-1, keepdims=True) + eps)


def pack_weights(q_ref, k_ref, v_ref, o_ref, packed_ref):
    for index, ref in enumerate((q_ref, k_ref, v_ref)):
        packed_ref[:, index * WIDTH : (index + 1) * WIDTH] = ref[...]
    packed_ref[:, 3 * WIDTH :] = o_ref[...].T


def run_pack(q, k, v, o):
    width = q.shape[0]
    return call(
        pack_weights,
        "pack_weights",
        (),
        [pl.BlockSpec(memory_space=pltpu.VMEM)] * 4,
        pl.BlockSpec(memory_space=pltpu.VMEM),
        jax.ShapeDtypeStruct((width, 4 * WIDTH), BF),
        1e6,
        2e6,
        vmem=FULL_VMEM,
    )(q, k, v, o)


def forward_first(x_ref, gain_ref, *refs):
    slots = len(refs) - 6
    normed_ref, *saved = refs[slots:]
    normed = (norm_rows(x_ref[...].astype(F32)) * gain_ref[...]).astype(BF)
    normed_ref[...] = normed
    attend(normed, [ref[:, : 3 * WIDTH] for ref in refs[:slots]], *saved)


def forward_last(
    ids_ref, normed_ref, x_ref, ctx_in_ref, ffn_gain_ref, control_ref, cot_ref, group_ref,
    live_ref, *refs
):
    slots = len(refs) - 12
    weights = refs[:slots]
    *saved, middle_ref, normed2_ref = refs[slots : slots + 7]
    *groups, normed2_all, logits_all = refs[slots + 7 :]
    ctx_ref = saved[-1]
    normed = normed_ref[...]
    before = ctx_in_ref.shape[0]
    attend(normed, [ref[:, : 3 * WIDTH] for ref in weights[before:]], *saved)
    sequence = pl.program_id(0)
    here = pl.ds(pl.multiple_of(sequence * LENGTH, LENGTH), LENGTH)
    context = jnp.concatenate(
        [ctx_in_ref[i] for i in range(before)] + [ctx_ref[i] for i in range(slots - before)],
        axis=1,
    )
    flipped = jnp.concatenate([ref[:, -WIDTH:] for ref in weights], axis=1)
    middle = x_ref[...].astype(F32) + dot_last(context, flipped)
    middle_ref[...] = middle
    normed2 = (norm_rows(middle) * ffn_gain_ref[...]).astype(BF)
    normed2_ref[...] = normed2
    normed2_all[here] = normed2
    logits_all[here] = dot_last(normed2, control_ref[...])

    @pl.when(sequence == pl.num_programs(0) - 1)
    def _():
        gather_groups(
            ids_ref, logits_all, normed2_all, cot_ref, group_ref, live_ref, *groups
        )


def slot_outputs(slots, tokens):
    per = pl.BlockSpec((slots, LENGTH, WIDTH), lambda s: (0, s, 0))
    return [per] * 5, [jax.ShapeDtypeStruct((slots, tokens, WIDTH), BF)] * 5


def run_forward_first(x, gain, weights):
    tokens, width = x.shape
    specs, shapes = slot_outputs(len(weights), tokens)
    return call(
        forward_first,
        "attention_forward_first",
        (tokens // LENGTH,),
        [row_block(width), whole(1, width)] + [whole(width, 4 * WIDTH)] * len(weights),
        [row_block(width)] + specs,
        [jax.ShapeDtypeStruct((tokens, width), BF)] + shapes,
        1.5e10,
        1e7,
        1e7,
        vmem=FULL_VMEM,
    )(x, gain, *weights)


def run_forward_last(ids, normed, x, ctx, ffn_gain, control, cot, group, live, weights):
    tokens, width = x.shape
    groups = tokens // 8
    before = ctx.shape[0]
    specs, shapes = slot_outputs(len(weights) - before, tokens)
    sums = jax.ShapeDtypeStruct((2, groups, width), BF)
    return call(
        forward_last,
        "attention_forward_last",
        (tokens // LENGTH,),
        [
            pl.BlockSpec(memory_space=pltpu.SMEM),
            row_block(width),
            row_block(width),
            pl.BlockSpec((before, LENGTH, WIDTH), lambda s: (0, s, 0)),
            whole(1, width),
            whole(2, width),
            whole(tokens, width),
            whole(1, tokens),
            whole(1, tokens),
        ]
        + [pl.BlockSpec((width, WIDTH), lambda s: (0, 3))] * before
        + [whole(width, 4 * WIDTH)] * (len(weights) - before),
        specs
        + [row_block(width), row_block(width), whole(tokens, WIDTH)]
        + [whole(2, groups, width)] * 2,
        shapes
        + [
            jax.ShapeDtypeStruct((tokens, width), F32),
            jax.ShapeDtypeStruct((tokens, width), BF),
            jax.ShapeDtypeStruct((tokens, WIDTH), F32),
            sums,
            sums,
        ],
        1.5e10,
        1e7,
        1e7,
        vmem=40 * 2**20,
        scratch_shapes=[pltpu.VMEM((tokens, width), BF), pltpu.VMEM((tokens, 2), F32)],
    )(ids, normed, x, ctx, ffn_gain, control, cot, group, live, *weights)


def backward_items(
    slots, items_ref, q_ref, k_ref, v_ref, logsum_ref, ctx_ref, ml_ref, normed_ref, *refs
):
    dqkv_ref, dw_ref = refs[-2:]
    item = pl.program_id(0)
    weight = refs[0][...]
    for index in range(1, slots):
        weight = jnp.where(items_ref[0, item] == index, refs[index][...], weight)
    block = 256
    ml = ml_ref[...]
    ctx = ctx_ref[0]
    d_out = dot(ml, weight).astype(BF)
    product = d_out.astype(F32) * ctx.astype(F32)
    q = q_ref[0]
    k = k_ref[0]
    v = v_ref[0]
    logsum = logsum_ref[0]
    k_flip = k.T
    dks, dvs, dqs = [], [], []
    for head in range(2):
        lane, mine, other = head_lanes(LENGTH, head)
        minus = jnp.where((lane >= other) & (lane < other + 3), -1.0, 0.0).astype(BF)
        minus_own = jnp.where((lane >= HD - other) & (lane < HD - other + 3), -1.0, 0.0).astype(BF)
        central = jnp.sum(jnp.where(mine, product, 0.0), axis=1, keepdims=True)
        d_all = with_extra(mine, lane, other, d_out, central)
        v_all = jnp.where(mine, v, minus)
        k_all = jnp.concatenate([twice(mine, k), minus_own], axis=1)
        q_scaled = scaled_queries(mine, q)
        q_all = jnp.concatenate([q_scaled, logsum], axis=1)
        dq = [0.0] * (LENGTH // block)
        dk, dv = [], []
        for at in range(0, LENGTH, block):
            keys = k_all[at : at + block]
            values = v_all[at : at + block]
            flipped = k_flip[head * HD : (head + 1) * HD, at : at + block]
            probs = jnp.exp2(dot_last(keys, q_all[at:]))
            r = lax.broadcasted_iota(jnp.int32, (block, block), 0)
            c = lax.broadcasted_iota(jnp.int32, (block, block), 1)
            corner = jnp.where(r <= c, probs[:, :block], 0.0)
            probs = corner if at + block == LENGTH else jnp.concatenate([corner, probs[:, block:]], axis=1)
            d_scores = (probs * dot_last(values, d_all[at:])).astype(BF)
            dv.append(dot(probs.astype(BF), d_all[at:]))
            dk.append(dot(d_scores, q_scaled[at:]))
            part = dot(flipped, d_scores)
            for start in range(at, LENGTH, block):
                dq[start // block] = dq[start // block] + part[:, start - at : start - at + block]
        dk = jnp.concatenate(dk, axis=0)
        dks.append(dk + jnp.roll(dk, HD, axis=1))
        dvs.append(jnp.concatenate(dv, axis=0))
        dqs.append(jnp.concatenate(dq, axis=1))
    lane, mine, _ = head_lanes(LENGTH, 0)
    dk = (jnp.where(mine, dks[0], dks[1]) * LN2).astype(BF)
    dv = jnp.where(mine, dvs[0], dvs[1]).astype(BF)
    dq_flip = (jnp.concatenate(dqs, axis=0) * HD**-0.5).astype(BF)
    dqkv_ref[0, :, :WIDTH] = dq_flip.T
    dqkv_ref[0, :, WIDTH : 2 * WIDTH] = dk
    dqkv_ref[0, :, 2 * WIDTH :] = dv
    dw = dot(jnp.concatenate([dq_flip, dk.T, dv.T], axis=0), normed_ref[...])
    dwo = dot_first(ctx, ml)
    parts = [dw[:WIDTH], dw[WIDTH : 2 * WIDTH], dw[2 * WIDTH :], dwo]
    adds = items_ref[2, item]
    earlier = refs[slots + 1] if len(refs) > slots + 2 else None

    @pl.when(adds == 0)
    def _():
        for index, part in enumerate(parts):
            dw_ref[0, index] = part

    @pl.when(adds == 1)
    def _():
        for index, part in enumerate(parts):
            dw_ref[0, index] += part

    if earlier is not None:

        @pl.when(adds == 2)
        def _():
            for index, part in enumerate(parts):
                dw_ref[0, index] = earlier[0, index] + part


def run_backward(saved, ml, weights, normed, items, done=(), earlier=None, flops=6e9):
    tokens, width = ml.shape
    slots = len(weights)
    table = [[], [], []]
    for index, (slot, sequence) in enumerate(items):
        seen = [one for one in items[:index] if one[0] == slot]
        before = [one for one in done if one[0] == slot]
        table[0].append(slot)
        table[1].append(sequence)
        table[2].append(1 if seen else 2 if before else 0)
    table = jnp.array(table, jnp.int32)
    per = pl.BlockSpec((1, LENGTH, WIDTH), lambda i, t: (t[0, i], t[1, i], 0))
    rows = pl.BlockSpec((LENGTH, width), lambda i, t: (t[1, i], 0))
    sums = pl.BlockSpec((1, 4, WIDTH, width), lambda i, t: (t[0, i], 0, 0, 0))
    args = [table, *saved, ml, normed, *weights]
    in_specs = [*([per] * 5), rows, rows]
    in_specs += [pl.BlockSpec((width, WIDTH), lambda i, t: (0, 3))] * slots
    aliases = {}
    if earlier is not None:
        aliases = {len(args): 0, len(args) + 1: 1}
        args += list(earlier)
        in_specs += [pl.BlockSpec(memory_space=pl.ANY), sums]
    return pl.pallas_call(
        functools.partial(backward_items, slots),
        grid_spec=pltpu.PrefetchScalarGridSpec(
            num_scalar_prefetch=1,
            grid=(len(items),),
            in_specs=in_specs,
            out_specs=[pl.BlockSpec((1, LENGTH, 3 * WIDTH), lambda i, t: (t[0, i], t[1, i], 0)), sums],
        ),
        out_shape=[
            jax.ShapeDtypeStruct((slots, tokens, 3 * WIDTH), BF),
            jax.ShapeDtypeStruct((slots, 4, WIDTH, width), F32),
        ],
        input_output_aliases=aliases,
        compiler_params=pltpu.CompilerParams(vmem_limit_bytes=28 * 2**20),
        cost_estimate=pl.CostEstimate(
            flops=int(flops * len(items)), bytes_accessed=1, transcendentals=0
        ),
        name="attention_backward",
    )(*args)


def group_marks(group, alive, groups):
    slot = lax.broadcasted_iota(jnp.int32, (groups, group.shape[1]), 0).astype(F32)
    return jnp.where((slot == group) & (alive > 0), 1.0, 0.0).astype(BF)


def token_marks(columns, groups):
    slot = lax.broadcasted_iota(jnp.int32, (columns.shape[0], groups), 1).astype(F32)
    return jnp.where((slot == columns[:, 2:3]) & (columns[:, 3:4] > 0), 1.0, 0.0).astype(BF)


def dot_exact(marks, values):
    return functools.reduce(jnp.add, [dot(marks, part) for part in split3(values)])


def gather_groups(
    ids_ref, logits_ref, normed2_ref, cot_ref, group_ref, live_ref, columns_ref, keep_ref, send_ref
):
    tokens = normed2_ref.shape[0]
    groups = keep_ref.shape[1]
    group = group_ref[...].astype(F32)
    alive = live_ref[...].astype(F32)
    row = lax.broadcasted_iota(jnp.int32, (WIDTH, tokens), 0)
    turned = jnp.where(row == 2, group, jnp.where(row == 3, alive, 0.0)).T
    marks = group_marks(group, alive, groups)
    token_side = token_marks(turned, groups)
    live = turned[:, 3:4]
    lane = lax.broadcasted_iota(jnp.int32, (tokens, WIDTH), 1)
    logits = jnp.concatenate([logits_ref[...], jnp.zeros((tokens, WIDTH - 2), F32)], axis=1)
    expo = jnp.exp(logits) * live
    totals = dot_exact(marks, expo)
    weights = expo / (dot_exact(token_side, totals) + (1.0 - live))
    columns_ref[...] = jnp.where(lane < 2, weights, turned)
    rows = weights.T[:8].astype(BF)
    own = ids_ref[0] == 0
    normed2 = normed2_ref[...]
    cot = cot_ref[...]
    for ref, pick in ((keep_ref, own), (send_ref, jnp.logical_not(own))):
        assign = marks * jnp.where(pick, rows[0:1].astype(F32), rows[1:2].astype(F32)).astype(BF)
        ref[0] = dot(assign, normed2).astype(BF)
        ref[1] = dot(assign, cot).astype(BF)


def gelu_both(x):
    inner = 0.7978845608028654
    cubic = 0.044715
    square = x * x
    bent = jnp.tanh(inner * x * (1.0 + cubic * square))
    half = 0.5 * (1.0 + bent)
    slope = half + 0.5 * x * (1.0 - bent * bent) * (inner * (1.0 + 3.0 * cubic * square))
    return x * half, slope


SPLIT = (176, 176, 160)


def expert_step(
    ids_ref, keep_ref, got_ref, in_ref, out_ref, *refs
):
    kept_refs, sent_refs = refs[:3], refs[3:6]
    home_ref, away_ref, mixed_flip, result, mixed_grad, in_all, out_all, sems = refs[6:]
    step = pl.program_id(0)
    groups = keep_ref.shape[1]
    mixed = jnp.concatenate([keep_ref[0], got_ref[0]], axis=0)
    d_result = jnp.concatenate([keep_ref[1], got_ref[1]], axis=0)
    wide = in_all.shape[2]

    def loads(at):
        span = pl.ds(pl.multiple_of(at * wide, wide), wide)
        return [
            pltpu.make_async_copy(in_ref.at[ids_ref[0], :, span], in_all.at[at], sems.at[0, at]),
            pltpu.make_async_copy(out_ref.at[ids_ref[0], span], out_all.at[at], sems.at[1, at]),
        ]

    @pl.when(step == 0)
    def _():
        for at in range(in_all.shape[0]):
            for load in loads(at):
                load.start()
        mixed_flip[...] = mixed.T
        result[...] = jnp.zeros_like(result)
        mixed_grad[...] = jnp.zeros_like(mixed_grad)

    for load in loads(step):
        load.wait()
    w_in = in_all[step]
    w_out = out_all[step]
    active, slope = gelu_both(dot(mixed, w_in))
    active = active.astype(BF)
    d_before = (dot_last(d_result, w_out) * slope).astype(BF)
    result[...] += dot(active, w_out)
    mixed_grad[...] += dot_last(d_before, w_in)
    d_out = dot_first(active, d_result).astype(BF)
    d_in = dot(mixed_flip[...], d_before).astype(BF)
    half = d_in.shape[0] // 2
    for index in range(2):
        columns = slice(index * half, (index + 1) * half)
        side = d_in[:, columns]
        block = jnp.concatenate(
            [d_out[columns], jnp.concatenate([side[:half], side[half:]], axis=1)], axis=0
        )
        at = 0
        for part, rows in enumerate(SPLIT):
            place = jnp.bitwise_xor(2 * step + index, ids_ref[part + 1])
            piece = block[at : at + rows]
            at += rows

            @pl.when(place < 4)
            def _():
                kept_refs[part][place] = piece

            @pl.when(place >= 4)
            def _():
                sent_refs[part][place - 4] = piece

    @pl.when(step == pl.num_programs(0) - 1)
    def _():
        home_ref[0] = result[:groups].astype(BF)
        home_ref[1] = mixed_grad[:groups].astype(BF)
        away_ref[0] = result[groups:].astype(BF)
        away_ref[1] = mixed_grad[groups:].astype(BF)


def run_experts(ids, keep, got, expert_in, expert_out):
    _, width, hidden = expert_in.shape
    steps = 4
    wide = hidden // steps
    groups = keep.shape[1]
    sums = jax.ShapeDtypeStruct(keep.shape, BF)
    halves = [(4, rows, width) for rows in SPLIT] * 2
    hbm = pl.BlockSpec(memory_space=pltpu.HBM)
    return call(
        expert_step,
        "experts",
        (steps,),
        [pl.BlockSpec(memory_space=pltpu.SMEM), whole(*keep.shape), whole(*keep.shape), hbm, hbm],
        [whole(*shape) for shape in halves + [keep.shape] * 2],
        [jax.ShapeDtypeStruct(shape, BF) for shape in halves] + [sums, sums],
        1e10,
        1.2e7,
        1e6,
        scratch_shapes=[
            pltpu.VMEM((width, 2 * groups), BF),
            pltpu.VMEM((2 * groups, width), F32),
            pltpu.VMEM((2 * groups, width), F32),
            pltpu.VMEM((steps, width, wide), BF),
            pltpu.VMEM((steps, wide, width), BF),
            pltpu.SemaphoreType.DMA((2, steps)),
        ],
    )(ids, keep, got, expert_in, expert_out)


def spread_groups(
    ids_ref, middle_ref, normed2_ref, cot_ref, columns_ref, group_ref, live_ref, home_ref, got_ref,
    gain_ref, control_ref, out_ref, low_ref, small_ref,
    table, mixed_part, weight_grads, group_sums,
):
    phase, index = pl.program_id(0), pl.program_id(1)
    rows, width = middle_ref.shape
    groups = home_ref.shape[1]
    here = pl.ds(pl.multiple_of(index * rows, rows), rows)

    @pl.when((phase == 0) & (index == 0))
    def _():
        group_sums[...] = jnp.zeros_like(group_sums)
        small_ref[...] = jnp.zeros_like(small_ref)
        own = ids_ref[0] == 0
        for kind in range(2):
            home, got = home_ref[kind], got_ref[kind]
            at = 2 * kind * width
            table[:, at : at + width] = jnp.where(own, home, got)
            table[:, at + width : at + 2 * width] = jnp.where(own, got, home)

    @pl.when(phase == 0)
    def _():
        columns = columns_ref[...]
        lane = lax.broadcasted_iota(jnp.int32, columns.shape, 1)
        token_side = token_marks(columns, groups)
        spread = dot(token_side, table[...])
        cot = cot_ref[...]
        normed2 = normed2_ref[...]
        middle = middle_ref[...]
        cot = cot.astype(F32)
        normed2 = normed2.astype(F32)
        low = columns.astype(BF).astype(F32)
        first, second = low[:, 0:1], low[:, 1:2]
        result = [spread[:, i * width : (i + 1) * width] for i in range(4)]
        out_ref[...] = (middle + first * result[0] + second * result[1]).astype(BF)
        mixed_part[here] = first * result[2] + second * result[3]
        grads = [
            jnp.sum(cot * result[i] + normed2 * result[2 + i], axis=1, keepdims=True)
            for i in range(2)
        ]
        grads = jnp.where(lane == 0, grads[0], jnp.where(lane == 1, grads[1], 0.0))
        pulls = jnp.where(lane < 2, columns * grads, 0.0)
        weight_grads[here] = pulls
        group = group_ref[...].astype(F32)
        alive = live_ref[...].astype(F32)
        group_sums[...] += dot_exact(group_marks(group, alive, groups), pulls)

    @pl.when(phase == 1)
    def _():
        columns = columns_ref[...]
        central = dot_exact(token_marks(columns, groups), group_sums[...])
        logit_grads = weight_grads[here] - columns * central
        first, second = logit_grads[:, 0:1], logit_grads[:, 1:2]
        control = control_ref[...].astype(F32)
        cot = cot_ref[...].astype(F32)
        normed2 = normed2_ref[...].astype(F32)
        middle = middle_ref[...]
        grad = mixed_part[here] + first * control[0:1] + second * control[1:2]
        scale = lax.rsqrt(jnp.mean(middle * middle, axis=-1, keepdims=True) + eps)
        unit = middle * scale
        pulled = grad * gain_ref[...]
        pulled = scale * (pulled - unit * jnp.mean(pulled * unit, axis=-1, keepdims=True))
        low_ref[...] = (cot + pulled).astype(BF)
        small_ref[0:1] += jnp.sum(grad * unit, axis=0, keepdims=True)
        small_ref[1:2] += jnp.sum(first * normed2, axis=0, keepdims=True)
        small_ref[2:3] += jnp.sum(second * normed2, axis=0, keepdims=True)


def run_spread(ids, middle, normed2, cot, columns, group, live, home, got, gain, control):
    tokens, width = middle.shape
    groups = home.shape[1]
    rows = 512
    steps = tokens // rows
    by_block = lambda n: pl.BlockSpec((rows, n), lambda p, b: (b, 0))
    fixed = lambda *shape: pl.BlockSpec(shape, lambda p, b: (0,) * len(shape))
    return call(
        spread_groups,
        "spread_groups",
        (2, steps),
        [
            pl.BlockSpec(memory_space=pltpu.SMEM),
            by_block(width),
            by_block(width),
            by_block(width),
            by_block(WIDTH),
            pl.BlockSpec((1, rows), lambda p, b: (0, b)),
            pl.BlockSpec((1, rows), lambda p, b: (0, b)),
            fixed(*home.shape),
            fixed(*home.shape),
            fixed(1, width),
            fixed(2, width),
        ],
        [
            pl.BlockSpec((rows, width), lambda p, b: (b * (1 - p) + (steps - 1) * p, 0)),
            pl.BlockSpec((rows, width), lambda p, b: (b * p, 0)),
            fixed(8, width),
        ],
        [
            jax.ShapeDtypeStruct((tokens, width), BF),
            jax.ShapeDtypeStruct((tokens, width), BF),
            jax.ShapeDtypeStruct((8, width), F32),
        ],
        8e9,
        2e7,
        scratch_shapes=[
            pltpu.VMEM((groups, 4 * width), BF),
            pltpu.VMEM((tokens, width), F32),
            pltpu.VMEM((tokens, WIDTH), F32),
            pltpu.VMEM((groups, WIDTH), F32),
        ],
    )(ids, middle, normed2, cot, columns, group, live, home, got, gain, control)


def input_rows(x_ref, gain_ref, grad_ref, *refs):
    slots = 4
    flats, weights, out_ref = refs[: -slots - 1], refs[-slots - 1 : -1], refs[-1]
    rows = x_ref[...].astype(F32)
    grad = dot_last(
        jnp.concatenate([flat[i] for flat in flats for i in range(flat.shape[0])], axis=1),
        jnp.concatenate([weight[:, : 3 * WIDTH] for weight in weights], axis=1),
    )
    scale = lax.rsqrt(jnp.mean(rows * rows, axis=-1, keepdims=True) + eps)
    unit = rows * scale
    pulled = grad * gain_ref[...]
    pulled = scale * (pulled - unit * jnp.mean(pulled * unit, axis=-1, keepdims=True))
    out_ref[...] = grad_ref[...].astype(F32) + pulled


def run_input(x, gain, grad, flats, weights):
    tokens, width = x.shape
    rows = 512
    by_block = lambda n: pl.BlockSpec((rows, n), lambda s: (s, 0))
    return call(
        input_rows,
        "input_rows",
        (tokens // rows,),
        [by_block(width), whole(1, width), by_block(width)]
        + [
            pl.BlockSpec((flat.shape[0], rows, 3 * WIDTH), lambda s: (0, s, 0)) for flat in flats
        ]
        + [whole(width, 4 * WIDTH)] * len(weights),
        by_block(width),
        jax.ShapeDtypeStruct((tokens, width), F32),
        1,
        1,
        vmem=FULL_VMEM,
    )(x, gain, grad, *flats, *weights)


def join_own(
    ids_ref, own_ref, one_ref, two_ref, weight_ref, gain_ref, rest_ref, kept_ref, sent_ref, small_ref
):
    half = kept_ref.shape[0]
    flipped = weight_ref[:, : 3 * WIDTH].T.astype(F32)
    gain_grad = 0.0
    for place in range(2 * half):
        total = own_ref[0, place] + one_ref[place].astype(F32) + two_ref[place].astype(F32)
        if place < 3:
            part = flipped[place * WIDTH : (place + 1) * WIDTH] * total
            gain_grad = gain_grad + jnp.sum(part, axis=0, keepdims=True)
        index = jnp.bitwise_xor(place, ids_ref[4])
        total = total.astype(BF)

        @pl.when(index < half)
        def _():
            kept_ref[index] = total

        @pl.when(index >= half)
        def _():
            sent_ref[index - half] = total

    small_ref[...] = rest_ref[...]
    small_ref[3:4] = gain_grad / gain_ref[...]


def run_join(ids, own, one, two, weight, gain, rest):
    _, n, rows, width = own.shape
    vmem = pl.BlockSpec(memory_space=pltpu.VMEM)
    return call(
        join_own,
        "join_own",
        (),
        [pl.BlockSpec(memory_space=pltpu.SMEM)] + [vmem] * 6,
        [vmem] * 3,
        [jax.ShapeDtypeStruct((n // 2, rows, width), BF)] * 2
        + [jax.ShapeDtypeStruct(rest.shape, F32)],
        1,
        1,
    )(ids, own, one, two, weight, gain, rest)


def open_own(ids_ref, small_ref, small_got_ref, own_ref, *refs):
    gots, outs, (attn_ref, ffn_ref, control_ref) = refs[:3], refs[3:7], refs[7:]
    small = small_ref[...] + small_got_ref[...]
    ffn_ref[...] = small[0:1]
    control_ref[...] = small[1:3]
    attn_ref[...] = small[3:4]
    for index, out in enumerate(outs):
        place = jnp.bitwise_xor(index, ids_ref[4])
        value = own_ref[0]
        for at, got in enumerate(gots):
            value = jnp.where(place == at + 1, got[0], value)
        value = value.astype(F32)
        out[...] = value if index == 3 else value.T


def run_open(ids, small, small_got, own, gots):
    _, rows, width = own.shape
    vmem = pl.BlockSpec(memory_space=pltpu.VMEM)
    return call(
        open_own,
        "open_own",
        (),
        [pl.BlockSpec(memory_space=pltpu.SMEM)] + [vmem] * 6,
        [vmem] * 7,
        [jax.ShapeDtypeStruct((width, rows), F32)] * 3
        + [jax.ShapeDtypeStruct((rows, width), F32)]
        + [jax.ShapeDtypeStruct((n, width), F32) for n in (1, 1, 2)],
        1e6,
        2e6,
    )(ids, small, small_got, own, *gots)


def part_regions(index, half):
    start = sum(SPLIT[:index])
    regions = []
    for low, high, output in ((0, half, 1), (half, 2 * half, 0)):
        first, last = max(start, low), min(start + SPLIT[index], high)
        if first < last:
            regions.append((first - start, last - first, output, first - low))
    return regions


def open_experts(base, ids_ref, *refs):
    sources, (in_ref, out_ref, stage, sems) = refs[:-4], refs[-4:]
    joined = len(sources) in (4, 6) and sources[3].shape[1] == sum(SPLIT)
    half = stage.shape[2] // 2
    copies = []
    for side in range(2):
        expert = ids_ref[0] if side == 0 else 1 - ids_ref[0]
        for index in range(3):
            rows = SPLIT[index]
            for spot in range(4):
                slot = (side * 3 + index) * 4 + spot
                place = jnp.bitwise_xor(base + spot, ids_ref[index + 1])
                columns = pl.ds(pl.multiple_of(place * half, half), half)
                if side == 1 and joined:
                    at = sum(SPLIT[:index])
                    piece = sources[3][spot, at : at + rows]
                else:
                    piece = sources[3 * side + index][spot]
                stage[slot, :rows] = piece.astype(F32)
                for start, count, output, at in part_regions(index, half):
                    if output == 1:
                        copies.append(
                            pltpu.make_async_copy(
                                stage.at[slot, pl.ds(start, count)],
                                out_ref.at[expert, pl.ds(place * half + at, count)],
                                sems.at[len(copies)],
                            )
                        )
                        copies[-1].start()
                        continue
                    for part in range(2):
                        copies.append(
                            pltpu.make_async_copy(
                                stage.at[slot, pl.ds(start, count), pl.ds(part * half, half)],
                                in_ref.at[expert, pl.ds(part * half + at, count), columns],
                                sems.at[len(copies)],
                            )
                        )
                        copies[-1].start()
    for copy in copies:
        copy.wait()


def run_open_experts(ids, base, args, shape_in, shape_out, begun=()):
    vmem = pl.BlockSpec(memory_space=pltpu.VMEM)
    hbm = pl.BlockSpec(memory_space=pl.ANY)
    copies = 8 * sum(1 if region[2] else 2 for i in range(3) for region in part_regions(i, 256))
    return call(
        functools.partial(open_experts, base),
        "open_experts",
        (),
        [pl.BlockSpec(memory_space=pltpu.SMEM)] + [vmem] * len(args) + [hbm] * len(begun),
        [hbm] * 2,
        [jax.ShapeDtypeStruct(shape_in, F32), jax.ShapeDtypeStruct(shape_out, F32)],
        1e10 if base else 1,
        1e7 if base else 1,
        scratch_shapes=[
            pltpu.VMEM((24, max(SPLIT), shape_out[2]), F32),
            pltpu.SemaphoreType.DMA((copies,)),
        ],
        input_output_aliases={1 + len(args) + i: i for i in range(len(begun))},
    )(ids, *args, *begun)


def tie(*values):
    return lax.optimization_barrier(values)


def tie_groups(*groups):
    values = iter(tie(*[value for group in groups for value in group]))
    return [[next(values) for _ in group] for group in groups]


def build(mesh):
    n_head, n_batch = mesh.shape["head"], mesh.shape["batch"]
    head_bits = [("head", 1 << i) for i in range(n_head.bit_length() - 1)]
    batch_bits = [("batch", 1 << i) for i in range(n_batch.bit_length() - 1)]
    pair, across = head_bits
    first_batch, second_batch, *last_batch = batch_bits
    orders = [
        (across, first_batch, second_batch),
        (first_batch, second_batch, across),
        (second_batch, across, first_batch),
    ]

    def swap(value, step):
        axis, bit = step
        return lax.ppermute(value, axis, [(i, i ^ bit) for i in range(mesh.shape[axis])])

    def bit_of(step):
        axis, bit = step
        return (lax.axis_index(axis) // bit) % 2

    def number(steps):
        return functools.reduce(lambda value, step: 2 * value + bit_of(step), steps, 0)

    def add(kept, got):
        return (kept.astype(F32) + got.astype(F32)).astype(BF)

    def local(
        inputs,
        attn_gain,
        query_weight,
        key_weight,
        value_weight,
        output_weight,
        ffn_gain,
        controller,
        expert_in,
        expert_out,
        group_ids,
        live_mask,
        cotangent,
    ):
        tokens_here, width = inputs.shape
        sequences = tokens_here // LENGTH
        ids = jnp.stack(
            [bit_of(pair)]
            + [number(order) for order in orders]
            + [number((first_batch, second_batch))]
        ).astype(jnp.int32)
        w0 = run_pack(query_weight, key_weight, value_weight, output_weight)
        w2 = swap(w0, across)
        w1 = swap(w0, pair)
        normed, *saved_a = run_forward_first(inputs, attn_gain[None], [w0, w1])
        w2, normed = tie(w2, normed)
        w3 = swap(w2, pair)
        weights = [w0, w1, w2, w3]
        control = controller.T
        group, live = group_ids[None], live_mask[None]
        *saved_b, middle, normed2, columns, keep, send = run_forward_last(
            ids,
            normed,
            inputs,
            saved_a[-1],
            ffn_gain[None],
            control,
            cotangent,
            group,
            live,
            weights,
        )
        *parts, home, away = run_experts(ids, keep, swap(send, pair), expert_in, expert_out)
        home_got = swap(away, pair)
        kept, sent = parts[:3], parts[3:]
        got = [swap(part, order[0]) for part, order in zip(sent, orders)]

        def send_half(blocks, step):
            half = blocks.shape[0] // 2
            return blocks[:half], swap(blocks[half:], step)

        layer_out, middle_low, small = run_spread(
            ids,
            middle,
            normed2,
            cotangent,
            columns,
            group,
            live,
            home,
            home_got,
            ffn_gain[None],
            control,
        )

        half = sequences // 2

        def next_stage(kept, got, low, mark, stage):
            *got, mark = tie(*got, mark)
            blocks = [add(a, b) for a, b in zip(kept, got)]
            if stage < 3:
                kept = [block[: block.shape[0] // 2] for block in blocks]
                sent = [block[block.shape[0] // 2 :] for block in blocks]
            else:
                kept = sent = blocks
            *sent, low = tie(*sent, low)
            steps = [order[stage] if stage < 3 else last_batch[stage - 3] for order in orders]
            return kept, [swap(block, step) for block, step in zip(sent, steps)], low, mark

        low = middle_low
        early, late = range(half), range(half, sequences)
        first_items = [(1, i) for i in early]
        second_items = [(1, i) for i in late] + [(0, i) for i in early]
        third_items = [(0, i) for i in late]
        far_slots = weights[2:]
        flat, sums = run_backward(saved_b, low, far_slots, normed, first_items)
        kept, got, low, sums = next_stage(kept, got, low, sums, 1)
        flat, sums = run_backward(
            saved_b, low, far_slots, normed, second_items, first_items, (flat, sums)
        )
        kept, got, low, sums = next_stage(kept, got, low, sums, 2)
        third_got = swap(sums[1].astype(BF), pair)
        flat, sums = run_backward(
            saved_b, low, far_slots, normed, third_items, first_items + second_items, (flat, sums)
        )
        kept, got, low, sums = next_stage(kept, got, low, sums, 3)
        for stage in range(4, 3 + len(last_batch)):
            kept, got, low, sums = next_stage(kept, got, low, sums, stage)
        second = (sums[0] + third_got.astype(F32)).astype(BF)
        second, low = tie(second, low)
        second_got = swap(second, across)
        near_items = [(slot, i) for slot in (1, 0) for i in range(sequences)]
        flat_near, sums_near = run_backward(saved_a, low, weights[:2], normed, near_items)
        *got, second_got, sums_near, low = tie(*got, second_got, sums_near, low)

        def widen(blocks, stage):
            return [swap(block, order[stage]) for block, order in zip(blocks, orders)]

        def join(blocks, got):
            return [jnp.concatenate(both, axis=0) for both in zip(blocks, got)]

        def split(value):
            half = value.shape[0] // 2
            return value[:half], value[half:]

        def all_of(value, steps):
            (axis, one), (_, two) = steps
            return [swap(value, (axis, bits)) for bits in (one, two, one | two)]

        first_got = swap(sums_near[1].astype(BF), pair)
        blocks = [add(a, b) for a, b in zip(kept, got)]
        *blocks, low = tie(*blocks, low)
        got = widen(blocks, 2)
        own_kept, own_sent, small = run_join(
            ids, sums_near, second_got, first_got, w0, attn_gain[None], small
        )
        small, own_sent = tie(small + swap(small, pair), own_sent)
        own_got = swap(own_sent, first_batch)
        small_got = swap(small, across)
        *got, small_got, low = tie(*got, small_got, low)

        blocks = join(blocks, got)
        got = widen(blocks, 1)
        own_kept, own_sent = split(add(own_kept, own_got))
        own_got = swap(own_sent, second_batch)
        small = small + small_got
        small_got = swap(small, second_batch)
        *got, own_got, small_got, low = tie(*got, own_got, small_got, low)

        blocks = join(blocks, got)
        blocks_other = swap(jnp.concatenate(blocks, axis=1), pair)
        far = widen(blocks, 0)
        begun = run_open_experts(
            ids, 0, [*blocks, blocks_other], expert_in.shape, expert_out.shape
        )
        own = add(own_kept, own_got)
        small = small + small_got
        for step in last_batch[:-1]:
            own = add(own, swap(own, step))
            small = small + swap(small, step)
        own_got = swap(own, last_batch[-1])
        small_got = swap(small, first_batch)
        input_grad = run_input(inputs, attn_gain[None], low, [flat_near, flat], weights)
        far, (own_got, small_got, input_grad, *begun) = tie_groups(
            far, (own_got, small_got, input_grad, *begun)
        )

        far_other = [swap(block, pair) for block in far]
        own = add(own, own_got)
        own_got = all_of(own, (second_batch, first_batch))
        small = small + small_got
        small_got = swap(small, last_batch[-1])
        expert_grads = run_open_experts(
            ids, 4, [*far, *far_other], expert_in.shape, expert_out.shape, begun
        )
        own_got, (small_got, expert_in_grad, expert_out_grad) = tie_groups(
            own_got, (small_got, *expert_grads)
        )
        query_grad, key_grad, value_grad, output_grad, attn_grad, ffn_grad, control_grad = run_open(
            ids, small, small_got, own, own_got
        )
        return (
            layer_out,
            input_grad,
            attn_grad[0],
            query_grad,
            key_grad,
            value_grad,
            output_grad,
            ffn_grad[0],
            control_grad.T,
            expert_in_grad,
            expert_out_grad,
        )

    return local


def solution(mesh):
    in_specs = (
        P(("batch", "head"), None),
        P(),
        P(None, "head"),
        P(None, "head"),
        P(None, "head"),
        P("head", None),
        P(),
        P(),
        P(),
        P(),
        P(("batch", "head")),
        P(("batch", "head")),
        P(("batch", "head"), None),
    )
    out_specs = (
        P(("batch", "head"), None),
        P(("batch", "head"), None),
        P(),
        P(None, "head"),
        P(None, "head"),
        P(None, "head"),
        P("head", None),
        P(),
        P(),
        P(),
        P(),
    )
    return jax.shard_map(
        build(mesh), mesh=mesh, in_specs=in_specs, out_specs=out_specs, check_vma=False
    )
```

```python
import functools

import jax
import jax.numpy as jnp
from jax import lax
from jax.experimental import pallas as pl
from jax.experimental.pallas import tpu as pltpu
from jax.sharding import PartitionSpec as P

HD = 64
LENGTH = 1024
WIDTH = 128
BF = jnp.bfloat16
F32 = jnp.float32
LOG2E = 1.4426950408889634
LN2 = 0.6931471805599453
VMEM = 20 * 2**20
FULL_VMEM = 56 * 2**20

eps = 1e-06
last_dims = (((1,), (1,)), ((), ()))
first_dims = (((0,), (0,)), ((), ()))


def dot(left, right):
    return jnp.dot(left, right, preferred_element_type=F32)


def dot_last(left, right):
    return lax.dot_general(left, right, last_dims, preferred_element_type=F32)


def dot_first(left, right):
    return lax.dot_general(left, right, first_dims, preferred_element_type=F32)


def split3(value):
    high = value.astype(BF)
    rest = value - high.astype(F32)
    mid = rest.astype(BF)
    low = (rest - mid.astype(F32)).astype(BF)
    return high, mid, low


def call(
    body, name, grid, in_specs, out_specs, out_shape, flops, moved, exps=0, vmem=VMEM, **extra
):
    return pl.pallas_call(
        body,
        grid=grid,
        in_specs=in_specs,
        out_specs=out_specs,
        out_shape=out_shape,
        compiler_params=pltpu.CompilerParams(vmem_limit_bytes=vmem),
        cost_estimate=pl.CostEstimate(
            flops=int(flops), bytes_accessed=int(moved), transcendentals=int(exps)
        ),
        name=name,
        **extra,
    )


def row_block(columns):
    return pl.BlockSpec((LENGTH, columns), lambda s: (s, 0))


def whole(*shape):
    return pl.BlockSpec(shape, lambda s: (0,) * len(shape))


def head_lanes(rows, head):
    lane = lax.broadcasted_iota(jnp.int32, (rows, WIDTH), 1)
    mine = (lane < HD) if head == 0 else (lane >= HD)
    return lane, mine, HD if head == 0 else 0


def with_extra(mine, lane, other, values, extra):
    high, mid, low = split3(extra)
    filler = jnp.zeros_like(values)
    for place, part in ((2, low), (1, mid), (0, high)):
        filler = jnp.where(lane == other + place, part, filler)
    return jnp.where(mine, values, filler)


def twice(mine, values):
    return jnp.where(mine, values, jnp.roll(values, HD, axis=1))


def scaled_queries(mine, q):
    long = q.astype(F32) * (HD**-0.5 * LOG2E)
    high = long.astype(BF)
    low = (long - high.astype(F32)).astype(BF)
    return jnp.where(mine, high, jnp.roll(low, HD, axis=1))


def attend(normed, weights, q_ref, k_ref, v_ref, logsum_ref, ctx_ref):
    block = 256
    r = lax.broadcasted_iota(jnp.int32, (WIDTH, WIDTH), 0)
    c = lax.broadcasted_iota(jnp.int32, (WIDTH, WIDTH), 1)
    same_head = jnp.where((r < HD) == (c < HD), 1.0, 0.0).astype(BF)

    def most(values):
        long = values.astype(F32)
        return jnp.max(dot((long * long).astype(BF), same_head), axis=0, keepdims=True)

    bounds = []
    for slot, weight in enumerate(weights):
        qkv = dot(normed, weight)
        q = qkv[:, :WIDTH].astype(BF)
        k = qkv[:, WIDTH : 2 * WIDTH].astype(BF)
        q_ref[slot] = q
        k_ref[slot] = k
        v_ref[slot] = qkv[:, 2 * WIDTH :].astype(BF)
        bounds.append(most(q) * most(k))
    bound = jnp.max(functools.reduce(jnp.maximum, bounds))

    def finish(slot, head, here, out, peak):
        lane_b, mine_b, other = head_lanes(block, head)
        total = out[:, other : other + 1]
        logsum = jnp.log2(total) + peak
        context = (out * (1.0 / total)).astype(BF)
        marks = with_extra(jnp.full_like(mine_b, False), lane_b, head * HD, context, logsum)
        if head == 1:
            context = jnp.where(mine_b, context, ctx_ref[slot, here])
            marks = jnp.where(mine_b, marks, logsum_ref[slot, here])
        ctx_ref[slot, here] = context
        logsum_ref[slot, here] = marks

    def head_keys(slot, head):
        lane, mine, other = head_lanes(LENGTH, head)
        vh = jnp.where(mine, v_ref[slot], (lane == other).astype(F32).astype(BF))
        return twice(mine, k_ref[slot]), vh

    def rows_small(slot, head):
        kh, vh = head_keys(slot, head)
        qh = scaled_queries(head_lanes(LENGTH, head)[1], q_ref[slot])
        for start in range(0, LENGTH, block):
            here = slice(start, start + block)
            queries = qh[here]
            scores = []
            for at in range(0, start + block, block):
                part = dot_last(queries, kh[at : at + block])
                if at == start:
                    r = lax.broadcasted_iota(jnp.int32, (block, block), 0)
                    c = lax.broadcasted_iota(jnp.int32, (block, block), 1)
                    part = jnp.where(c <= r, part, -1e30)
                scores.append(part)
            out = 0.0
            for index, part in enumerate(scores):
                out = out + dot(
                    jnp.exp2(part).astype(BF), vh[index * block : (index + 1) * block]
                )
            finish(slot, head, here, out, 0.0)

    def rows_large(slot, head):
        @pl.loop(0, LENGTH // block)
        def _(index):
            kh, vh = head_keys(slot, head)
            here = pl.ds(pl.multiple_of(index * block, block), block)
            queries = scaled_queries(head_lanes(block, head)[1], q_ref[slot, here])
            scores = dot_last(queries, kh)
            r = lax.broadcasted_iota(jnp.int32, scores.shape, 0) + index * block
            c = lax.broadcasted_iota(jnp.int32, scores.shape, 1)
            scores = jnp.where(c <= r, scores, -1e30)
            peak = jnp.max(scores, axis=1, keepdims=True)
            finish(slot, head, here, dot(jnp.exp2(scores - peak).astype(BF), vh), peak)

    small = bound * (HD**-0.5 * LOG2E) ** 2 * 1.1 < 1e4

    @pl.when(small)
    def _():
        for slot in range(len(weights)):
            for head in range(2):
                rows_small(slot, head)

    @pl.when(jnp.logical_not(small))
    def _():
        for head in range(2):

            @pl.loop(0, len(weights))
            def _(slot):
                rows_large(slot, head)


def norm_rows(rows):
    return rows * lax.rsqrt(jnp.mean(rows * rows, axis=-1, keepdims=True) + eps)


def pack_weights(q_ref, k_ref, v_ref, o_ref, packed_ref):
    for index, ref in enumerate((q_ref, k_ref, v_ref)):
        packed_ref[:, index * WIDTH : (index + 1) * WIDTH] = ref[...]
    packed_ref[:, 3 * WIDTH :] = o_ref[...].T


def run_pack(q, k, v, o):
    width = q.shape[0]
    return call(
        pack_weights,
        "pack_weights",
        (),
        [pl.BlockSpec(memory_space=pltpu.VMEM)] * 4,
        pl.BlockSpec(memory_space=pltpu.VMEM),
        jax.ShapeDtypeStruct((width, 4 * WIDTH), BF),
        1e6,
        2e6,
        vmem=FULL_VMEM,
    )(q, k, v, o)


def forward_first(x_ref, gain_ref, *refs):
    slots = len(refs) - 6
    normed_ref, *saved = refs[slots:]
    normed = (norm_rows(x_ref[...].astype(F32)) * gain_ref[...]).astype(BF)
    normed_ref[...] = normed
    attend(normed, [ref[:, : 3 * WIDTH] for ref in refs[:slots]], *saved)


def forward_last(
    ids_ref, normed_ref, x_ref, ctx_in_ref, ffn_gain_ref, control_ref, cot_ref, group_ref,
    live_ref, *refs
):
    slots = len(refs) - 12
    weights = refs[:slots]
    *saved, middle_ref, normed2_ref = refs[slots : slots + 7]
    *groups, normed2_all, logits_all = refs[slots + 7 :]
    ctx_ref = saved[-1]
    normed = normed_ref[...]
    before = ctx_in_ref.shape[0]
    attend(normed, [ref[:, : 3 * WIDTH] for ref in weights[before:]], *saved)
    sequence = pl.program_id(0)
    here = pl.ds(pl.multiple_of(sequence * LENGTH, LENGTH), LENGTH)
    context = jnp.concatenate(
        [ctx_in_ref[i] for i in range(before)] + [ctx_ref[i] for i in range(slots - before)],
        axis=1,
    )
    flipped = jnp.concatenate([ref[:, -WIDTH:] for ref in weights], axis=1)
    middle = x_ref[...].astype(F32) + dot_last(context, flipped)
    middle_ref[...] = middle
    normed2 = (norm_rows(middle) * ffn_gain_ref[...]).astype(BF)
    normed2_ref[...] = normed2
    normed2_all[here] = normed2
    logits_all[here] = dot_last(normed2, control_ref[...])

    @pl.when(sequence == pl.num_programs(0) - 1)
    def _():
        gather_groups(
            ids_ref, logits_all, normed2_all, cot_ref, group_ref, live_ref, *groups
        )


def slot_outputs(slots, tokens):
    per = pl.BlockSpec((slots, LENGTH, WIDTH), lambda s: (0, s, 0))
    return [per] * 5, [jax.ShapeDtypeStruct((slots, tokens, WIDTH), BF)] * 5


def run_forward_first(x, gain, weights):
    tokens, width = x.shape
    specs, shapes = slot_outputs(len(weights), tokens)
    return call(
        forward_first,
        "attention_forward_first",
        (tokens // LENGTH,),
        [row_block(width), whole(1, width)] + [whole(width, 4 * WIDTH)] * len(weights),
        [row_block(width)] + specs,
        [jax.ShapeDtypeStruct((tokens, width), BF)] + shapes,
        1.5e10,
        1e7,
        1e7,
        vmem=FULL_VMEM,
    )(x, gain, *weights)


def run_forward_last(ids, normed, x, ctx, ffn_gain, control, cot, group, live, weights):
    tokens, width = x.shape
    groups = tokens // 8
    before = ctx.shape[0]
    specs, shapes = slot_outputs(len(weights) - before, tokens)
    sums = jax.ShapeDtypeStruct((2, groups, width), BF)
    return call(
        forward_last,
        "attention_forward_last",
        (tokens // LENGTH,),
        [
            pl.BlockSpec(memory_space=pltpu.SMEM),
            row_block(width),
            row_block(width),
            pl.BlockSpec((before, LENGTH, WIDTH), lambda s: (0, s, 0)),
            whole(1, width),
            whole(2, width),
            whole(tokens, width),
            whole(1, tokens),
            whole(1, tokens),
        ]
        + [pl.BlockSpec((width, WIDTH), lambda s: (0, 3))] * before
        + [whole(width, 4 * WIDTH)] * (len(weights) - before),
        specs
        + [row_block(width), row_block(width), whole(tokens, WIDTH)]
        + [whole(2, groups, width)] * 2,
        shapes
        + [
            jax.ShapeDtypeStruct((tokens, width), F32),
            jax.ShapeDtypeStruct((tokens, width), BF),
            jax.ShapeDtypeStruct((tokens, WIDTH), F32),
            sums,
            sums,
        ],
        1.5e10,
        1e7,
        1e7,
        vmem=40 * 2**20,
        scratch_shapes=[pltpu.VMEM((tokens, width), BF), pltpu.VMEM((tokens, 2), F32)],
    )(ids, normed, x, ctx, ffn_gain, control, cot, group, live, *weights)


def backward_items(
    slots, items_ref, q_ref, k_ref, v_ref, logsum_ref, ctx_ref, ml_ref, normed_ref, *refs
):
    dqkv_ref, dw_ref = refs[-2:]
    item = pl.program_id(0)
    weight = refs[0][...]
    for index in range(1, slots):
        weight = jnp.where(items_ref[0, item] == index, refs[index][...], weight)
    block = 256
    ml = ml_ref[...]
    ctx = ctx_ref[0]
    d_out = dot(ml, weight).astype(BF)
    product = d_out.astype(F32) * ctx.astype(F32)
    q = q_ref[0]
    k = k_ref[0]
    v = v_ref[0]
    logsum = logsum_ref[0]
    k_flip = k.T
    dks, dvs, dqs = [], [], []
    for head in range(2):
        lane, mine, other = head_lanes(LENGTH, head)
        minus = jnp.where((lane >= other) & (lane < other + 3), -1.0, 0.0).astype(BF)
        minus_own = jnp.where((lane >= HD - other) & (lane < HD - other + 3), -1.0, 0.0).astype(BF)
        central = jnp.sum(jnp.where(mine, product, 0.0), axis=1, keepdims=True)
        d_all = with_extra(mine, lane, other, d_out, central)
        v_all = jnp.where(mine, v, minus)
        k_all = jnp.concatenate([twice(mine, k), minus_own], axis=1)
        q_scaled = scaled_queries(mine, q)
        q_all = jnp.concatenate([q_scaled, logsum], axis=1)
        dq = [0.0] * (LENGTH // block)
        dk, dv = [], []
        for at in range(0, LENGTH, block):
            keys = k_all[at : at + block]
            values = v_all[at : at + block]
            flipped = k_flip[head * HD : (head + 1) * HD, at : at + block]
            probs = jnp.exp2(dot_last(keys, q_all[at:]))
            r = lax.broadcasted_iota(jnp.int32, (block, block), 0)
            c = lax.broadcasted_iota(jnp.int32, (block, block), 1)
            corner = jnp.where(r <= c, probs[:, :block], 0.0)
            probs = corner if at + block == LENGTH else jnp.concatenate([corner, probs[:, block:]], axis=1)
            d_scores = (probs * dot_last(values, d_all[at:])).astype(BF)
            dv.append(dot(probs.astype(BF), d_all[at:]))
            dk.append(dot(d_scores, q_scaled[at:]))
            part = dot(flipped, d_scores)
            for start in range(at, LENGTH, block):
                dq[start // block] = dq[start // block] + part[:, start - at : start - at + block]
        dk = jnp.concatenate(dk, axis=0)
        dks.append(dk + jnp.roll(dk, HD, axis=1))
        dvs.append(jnp.concatenate(dv, axis=0))
        dqs.append(jnp.concatenate(dq, axis=1))
    lane, mine, _ = head_lanes(LENGTH, 0)
    dk = (jnp.where(mine, dks[0], dks[1]) * LN2).astype(BF)
    dv = jnp.where(mine, dvs[0], dvs[1]).astype(BF)
    dq_flip = (jnp.concatenate(dqs, axis=0) * HD**-0.5).astype(BF)
    dqkv_ref[0, :, :WIDTH] = dq_flip.T
    dqkv_ref[0, :, WIDTH : 2 * WIDTH] = dk
    dqkv_ref[0, :, 2 * WIDTH :] = dv
    dw = dot(jnp.concatenate([dq_flip, dk.T, dv.T], axis=0), normed_ref[...])
    dwo = dot_first(ctx, ml)
    parts = [dw[:WIDTH], dw[WIDTH : 2 * WIDTH], dw[2 * WIDTH :], dwo]
    adds = items_ref[2, item]
    earlier = refs[slots + 1] if len(refs) > slots + 2 else None

    @pl.when(adds == 0)
    def _():
        for index, part in enumerate(parts):
            dw_ref[0, index] = part

    @pl.when(adds == 1)
    def _():
        for index, part in enumerate(parts):
            dw_ref[0, index] += part

    if earlier is not None:

        @pl.when(adds == 2)
        def _():
            for index, part in enumerate(parts):
                dw_ref[0, index] = earlier[0, index] + part


def run_backward(saved, ml, weights, normed, items, done=(), earlier=None, flops=6e9):
    tokens, width = ml.shape
    slots = len(weights)
    table = [[], [], []]
    for index, (slot, sequence) in enumerate(items):
        seen = [one for one in items[:index] if one[0] == slot]
        before = [one for one in done if one[0] == slot]
        table[0].append(slot)
        table[1].append(sequence)
        table[2].append(1 if seen else 2 if before else 0)
    table = jnp.array(table, jnp.int32)
    per = pl.BlockSpec((1, LENGTH, WIDTH), lambda i, t: (t[0, i], t[1, i], 0))
    rows = pl.BlockSpec((LENGTH, width), lambda i, t: (t[1, i], 0))
    sums = pl.BlockSpec((1, 4, WIDTH, width), lambda i, t: (t[0, i], 0, 0, 0))
    args = [table, *saved, ml, normed, *weights]
    in_specs = [*([per] * 5), rows, rows]
    in_specs += [pl.BlockSpec((width, WIDTH), lambda i, t: (0, 3))] * slots
    aliases = {}
    if earlier is not None:
        aliases = {len(args): 0, len(args) + 1: 1}
        args += list(earlier)
        in_specs += [pl.BlockSpec(memory_space=pl.ANY), sums]
    return pl.pallas_call(
        functools.partial(backward_items, slots),
        grid_spec=pltpu.PrefetchScalarGridSpec(
            num_scalar_prefetch=1,
            grid=(len(items),),
            in_specs=in_specs,
            out_specs=[pl.BlockSpec((1, LENGTH, 3 * WIDTH), lambda i, t: (t[0, i], t[1, i], 0)), sums],
        ),
        out_shape=[
            jax.ShapeDtypeStruct((slots, tokens, 3 * WIDTH), BF),
            jax.ShapeDtypeStruct((slots, 4, WIDTH, width), F32),
        ],
        input_output_aliases=aliases,
        compiler_params=pltpu.CompilerParams(vmem_limit_bytes=28 * 2**20),
        cost_estimate=pl.CostEstimate(
            flops=int(flops * len(items)), bytes_accessed=1, transcendentals=0
        ),
        name="attention_backward",
    )(*args)


def group_marks(group, alive, groups):
    slot = lax.broadcasted_iota(jnp.int32, (groups, group.shape[1]), 0).astype(F32)
    return jnp.where((slot == group) & (alive > 0), 1.0, 0.0).astype(BF)


def token_marks(columns, groups):
    slot = lax.broadcasted_iota(jnp.int32, (columns.shape[0], groups), 1).astype(F32)
    return jnp.where((slot == columns[:, 2:3]) & (columns[:, 3:4] > 0), 1.0, 0.0).astype(BF)


def dot_exact(marks, values):
    return functools.reduce(jnp.add, [dot(marks, part) for part in split3(values)])


def gather_groups(
    ids_ref, logits_ref, normed2_ref, cot_ref, group_ref, live_ref, columns_ref, keep_ref, send_ref
):
    tokens = normed2_ref.shape[0]
    groups = keep_ref.shape[1]
    group = group_ref[...].astype(F32)
    alive = live_ref[...].astype(F32)
    row = lax.broadcasted_iota(jnp.int32, (WIDTH, tokens), 0)
    turned = jnp.where(row == 2, group, jnp.where(row == 3, alive, 0.0)).T
    marks = group_marks(group, alive, groups)
    token_side = token_marks(turned, groups)
    live = turned[:, 3:4]
    lane = lax.broadcasted_iota(jnp.int32, (tokens, WIDTH), 1)
    logits = jnp.concatenate([logits_ref[...], jnp.zeros((tokens, WIDTH - 2), F32)], axis=1)
    expo = jnp.exp(logits) * live
    totals = dot_exact(marks, expo)
    weights = expo / (dot_exact(token_side, totals) + (1.0 - live))
    columns_ref[...] = jnp.where(lane < 2, weights, turned)
    rows = weights.T[:8].astype(BF)
    own = ids_ref[0] == 0
    normed2 = normed2_ref[...]
    cot = cot_ref[...]
    for ref, pick in ((keep_ref, own), (send_ref, jnp.logical_not(own))):
        assign = marks * jnp.where(pick, rows[0:1].astype(F32), rows[1:2].astype(F32)).astype(BF)
        ref[0] = dot(assign, normed2).astype(BF)
        ref[1] = dot(assign, cot).astype(BF)


def gelu_both(x):
    inner = 0.7978845608028654
    cubic = 0.044715
    square = x * x
    bent = jnp.tanh(inner * x * (1.0 + cubic * square))
    half = 0.5 * (1.0 + bent)
    slope = half + 0.5 * x * (1.0 - bent * bent) * (inner * (1.0 + 3.0 * cubic * square))
    return x * half, slope


SPLIT = (176, 176, 160)


def expert_step(
    ids_ref, keep_ref, got_ref, in_ref, out_ref, *refs
):
    kept_refs, sent_refs = refs[:3], refs[3:6]
    home_ref, away_ref, mixed_flip, result, mixed_grad, in_all, out_all, sems = refs[6:]
    step = pl.program_id(0)
    groups = keep_ref.shape[1]
    mixed = jnp.concatenate([keep_ref[0], got_ref[0]], axis=0)
    d_result = jnp.concatenate([keep_ref[1], got_ref[1]], axis=0)
    wide = in_all.shape[2]

    def loads(at):
        span = pl.ds(pl.multiple_of(at * wide, wide), wide)
        return [
            pltpu.make_async_copy(in_ref.at[ids_ref[0], :, span], in_all.at[at], sems.at[0, at]),
            pltpu.make_async_copy(out_ref.at[ids_ref[0], span], out_all.at[at], sems.at[1, at]),
        ]

    @pl.when(step == 0)
    def _():
        for at in range(in_all.shape[0]):
            for load in loads(at):
                load.start()
        mixed_flip[...] = mixed.T
        result[...] = jnp.zeros_like(result)
        mixed_grad[...] = jnp.zeros_like(mixed_grad)

    for load in loads(step):
        load.wait()
    w_in = in_all[step]
    w_out = out_all[step]
    active, slope = gelu_both(dot(mixed, w_in))
    active = active.astype(BF)
    d_before = (dot_last(d_result, w_out) * slope).astype(BF)
    result[...] += dot(active, w_out)
    mixed_grad[...] += dot_last(d_before, w_in)
    d_out = dot_first(active, d_result).astype(BF)
    d_in = dot(mixed_flip[...], d_before).astype(BF)
    half = d_in.shape[0] // 2
    for index in range(2):
        columns = slice(index * half, (index + 1) * half)
        side = d_in[:, columns]
        block = jnp.concatenate(
            [d_out[columns], jnp.concatenate([side[:half], side[half:]], axis=1)], axis=0
        )
        at = 0
        for part, rows in enumerate(SPLIT):
            place = jnp.bitwise_xor(2 * step + index, ids_ref[part + 1])
            piece = block[at : at + rows]
            at += rows

            @pl.when(place < 4)
            def _():
                kept_refs[part][place] = piece

            @pl.when(place >= 4)
            def _():
                sent_refs[part][place - 4] = piece

    @pl.when(step == pl.num_programs(0) - 1)
    def _():
        home_ref[0] = result[:groups].astype(BF)
        home_ref[1] = mixed_grad[:groups].astype(BF)
        away_ref[0] = result[groups:].astype(BF)
        away_ref[1] = mixed_grad[groups:].astype(BF)


def run_experts(ids, keep, got, expert_in, expert_out):
    _, width, hidden = expert_in.shape
    steps = 4
    wide = hidden // steps
    groups = keep.shape[1]
    sums = jax.ShapeDtypeStruct(keep.shape, BF)
    halves = [(4, rows, width) for rows in SPLIT] * 2
    hbm = pl.BlockSpec(memory_space=pltpu.HBM)
    return call(
        expert_step,
        "experts",
        (steps,),
        [pl.BlockSpec(memory_space=pltpu.SMEM), whole(*keep.shape), whole(*keep.shape), hbm, hbm],
        [whole(*shape) for shape in halves + [keep.shape] * 2],
        [jax.ShapeDtypeStruct(shape, BF) for shape in halves] + [sums, sums],
        1e10,
        1.2e7,
        1e6,
        scratch_shapes=[
            pltpu.VMEM((width, 2 * groups), BF),
            pltpu.VMEM((2 * groups, width), F32),
            pltpu.VMEM((2 * groups, width), F32),
            pltpu.VMEM((steps, width, wide), BF),
            pltpu.VMEM((steps, wide, width), BF),
            pltpu.SemaphoreType.DMA((2, steps)),
        ],
    )(ids, keep, got, expert_in, expert_out)


def spread_groups(
    ids_ref, middle_ref, normed2_ref, cot_ref, columns_ref, group_ref, live_ref, home_ref, got_ref,
    gain_ref, control_ref, out_ref, low_ref, small_ref,
    table, mixed_part, weight_grads, group_sums,
):
    phase, index = pl.program_id(0), pl.program_id(1)
    rows, width = middle_ref.shape
    groups = home_ref.shape[1]
    here = pl.ds(pl.multiple_of(index * rows, rows), rows)

    @pl.when((phase == 0) & (index == 0))
    def _():
        group_sums[...] = jnp.zeros_like(group_sums)
        small_ref[...] = jnp.zeros_like(small_ref)
        own = ids_ref[0] == 0
        for kind in range(2):
            home, got = home_ref[kind], got_ref[kind]
            at = 2 * kind * width
            table[:, at : at + width] = jnp.where(own, home, got)
            table[:, at + width : at + 2 * width] = jnp.where(own, got, home)

    @pl.when(phase == 0)
    def _():
        columns = columns_ref[...]
        lane = lax.broadcasted_iota(jnp.int32, columns.shape, 1)
        token_side = token_marks(columns, groups)
        spread = dot(token_side, table[...])
        cot = cot_ref[...]
        normed2 = normed2_ref[...]
        middle = middle_ref[...]
        cot = cot.astype(F32)
        normed2 = normed2.astype(F32)
        low = columns.astype(BF).astype(F32)
        first, second = low[:, 0:1], low[:, 1:2]
        result = [spread[:, i * width : (i + 1) * width] for i in range(4)]
        out_ref[...] = (middle + first * result[0] + second * result[1]).astype(BF)
        mixed_part[here] = first * result[2] + second * result[3]
        grads = [
            jnp.sum(cot * result[i] + normed2 * result[2 + i], axis=1, keepdims=True)
            for i in range(2)
        ]
        grads = jnp.where(lane == 0, grads[0], jnp.where(lane == 1, grads[1], 0.0))
        pulls = jnp.where(lane < 2, columns * grads, 0.0)
        weight_grads[here] = pulls
        group = group_ref[...].astype(F32)
        alive = live_ref[...].astype(F32)
        group_sums[...] += dot_exact(group_marks(group, alive, groups), pulls)

    @pl.when(phase == 1)
    def _():
        columns = columns_ref[...]
        central = dot_exact(token_marks(columns, groups), group_sums[...])
        logit_grads = weight_grads[here] - columns * central
        first, second = logit_grads[:, 0:1], logit_grads[:, 1:2]
        control = control_ref[...].astype(F32)
        cot = cot_ref[...].astype(F32)
        normed2 = normed2_ref[...].astype(F32)
        middle = middle_ref[...]
        grad = mixed_part[here] + first * control[0:1] + second * control[1:2]
        scale = lax.rsqrt(jnp.mean(middle * middle, axis=-1, keepdims=True) + eps)
        unit = middle * scale
        pulled = grad * gain_ref[...]
        pulled = scale * (pulled - unit * jnp.mean(pulled * unit, axis=-1, keepdims=True))
        low_ref[...] = (cot + pulled).astype(BF)
        small_ref[0:1] += jnp.sum(grad * unit, axis=0, keepdims=True)
        small_ref[1:2] += jnp.sum(first * normed2, axis=0, keepdims=True)
        small_ref[2:3] += jnp.sum(second * normed2, axis=0, keepdims=True)


def run_spread(ids, middle, normed2, cot, columns, group, live, home, got, gain, control):
    tokens, width = middle.shape
    groups = home.shape[1]
    rows = 512
    steps = tokens // rows
    by_block = lambda n: pl.BlockSpec((rows, n), lambda p, b: (b, 0))
    fixed = lambda *shape: pl.BlockSpec(shape, lambda p, b: (0,) * len(shape))
    return call(
        spread_groups,
        "spread_groups",
        (2, steps),
        [
            pl.BlockSpec(memory_space=pltpu.SMEM),
            by_block(width),
            by_block(width),
            by_block(width),
            by_block(WIDTH),
            pl.BlockSpec((1, rows), lambda p, b: (0, b)),
            pl.BlockSpec((1, rows), lambda p, b: (0, b)),
            fixed(*home.shape),
            fixed(*home.shape),
            fixed(1, width),
            fixed(2, width),
        ],
        [
            pl.BlockSpec((rows, width), lambda p, b: (b * (1 - p) + (steps - 1) * p, 0)),
            pl.BlockSpec((rows, width), lambda p, b: (b * p, 0)),
            fixed(8, width),
        ],
        [
            jax.ShapeDtypeStruct((tokens, width), BF),
            jax.ShapeDtypeStruct((tokens, width), BF),
            jax.ShapeDtypeStruct((8, width), F32),
        ],
        8e9,
        2e7,
        scratch_shapes=[
            pltpu.VMEM((groups, 4 * width), BF),
            pltpu.VMEM((tokens, width), F32),
            pltpu.VMEM((tokens, WIDTH), F32),
            pltpu.VMEM((groups, WIDTH), F32),
        ],
    )(ids, middle, normed2, cot, columns, group, live, home, got, gain, control)


def input_rows(x_ref, gain_ref, grad_ref, *refs):
    slots = 4
    flats, weights, out_ref = refs[: -slots - 1], refs[-slots - 1 : -1], refs[-1]
    rows = x_ref[...].astype(F32)
    grad = dot_last(
        jnp.concatenate([flat[i] for flat in flats for i in range(flat.shape[0])], axis=1),
        jnp.concatenate([weight[:, : 3 * WIDTH] for weight in weights], axis=1),
    )
    scale = lax.rsqrt(jnp.mean(rows * rows, axis=-1, keepdims=True) + eps)
    unit = rows * scale
    pulled = grad * gain_ref[...]
    pulled = scale * (pulled - unit * jnp.mean(pulled * unit, axis=-1, keepdims=True))
    out_ref[...] = grad_ref[...].astype(F32) + pulled


def run_input(x, gain, grad, flats, weights):
    tokens, width = x.shape
    rows = 512
    by_block = lambda n: pl.BlockSpec((rows, n), lambda s: (s, 0))
    return call(
        input_rows,
        "input_rows",
        (tokens // rows,),
        [by_block(width), whole(1, width), by_block(width)]
        + [
            pl.BlockSpec((flat.shape[0], rows, 3 * WIDTH), lambda s: (0, s, 0)) for flat in flats
        ]
        + [whole(width, 4 * WIDTH)] * len(weights),
        by_block(width),
        jax.ShapeDtypeStruct((tokens, width), F32),
        1,
        1,
        vmem=FULL_VMEM,
    )(x, gain, grad, *flats, *weights)


def join_own(
    ids_ref, own_ref, one_ref, two_ref, weight_ref, gain_ref, rest_ref, kept_ref, sent_ref, small_ref
):
    half = kept_ref.shape[0]
    flipped = weight_ref[:, : 3 * WIDTH].T.astype(F32)
    gain_grad = 0.0
    for place in range(2 * half):
        total = own_ref[0, place] + one_ref[place].astype(F32) + two_ref[place].astype(F32)
        if place < 3:
            part = flipped[place * WIDTH : (place + 1) * WIDTH] * total
            gain_grad = gain_grad + jnp.sum(part, axis=0, keepdims=True)
        index = jnp.bitwise_xor(place, ids_ref[4])
        total = total.astype(BF)

        @pl.when(index < half)
        def _():
            kept_ref[index] = total

        @pl.when(index >= half)
        def _():
            sent_ref[index - half] = total

    small_ref[...] = rest_ref[...]
    small_ref[3:4] = gain_grad / gain_ref[...]


def run_join(ids, own, one, two, weight, gain, rest):
    _, n, rows, width = own.shape
    vmem = pl.BlockSpec(memory_space=pltpu.VMEM)
    return call(
        join_own,
        "join_own",
        (),
        [pl.BlockSpec(memory_space=pltpu.SMEM)] + [vmem] * 6,
        [vmem] * 3,
        [jax.ShapeDtypeStruct((n // 2, rows, width), BF)] * 2
        + [jax.ShapeDtypeStruct(rest.shape, F32)],
        1,
        1,
    )(ids, own, one, two, weight, gain, rest)


def open_own(ids_ref, small_ref, small_got_ref, own_ref, *refs):
    gots, outs, (attn_ref, ffn_ref, control_ref) = refs[:3], refs[3:7], refs[7:]
    small = small_ref[...] + small_got_ref[...]
    ffn_ref[...] = small[0:1]
    control_ref[...] = small[1:3]
    attn_ref[...] = small[3:4]
    for index, out in enumerate(outs):
        place = jnp.bitwise_xor(index, ids_ref[4])
        value = own_ref[0]
        for at, got in enumerate(gots):
            value = jnp.where(place == at + 1, got[0], value)
        value = value.astype(F32)
        out[...] = value if index == 3 else value.T


def run_open(ids, small, small_got, own, gots):
    _, rows, width = own.shape
    vmem = pl.BlockSpec(memory_space=pltpu.VMEM)
    return call(
        open_own,
        "open_own",
        (),
        [pl.BlockSpec(memory_space=pltpu.SMEM)] + [vmem] * 6,
        [vmem] * 7,
        [jax.ShapeDtypeStruct((width, rows), F32)] * 3
        + [jax.ShapeDtypeStruct((rows, width), F32)]
        + [jax.ShapeDtypeStruct((n, width), F32) for n in (1, 1, 2)],
        1e6,
        2e6,
    )(ids, small, small_got, own, *gots)


def part_regions(index, half):
    start = sum(SPLIT[:index])
    regions = []
    for low, high, output in ((0, half, 1), (half, 2 * half, 0)):
        first, last = max(start, low), min(start + SPLIT[index], high)
        if first < last:
            regions.append((first - start, last - first, output, first - low))
    return regions


def open_experts(base, ids_ref, *refs):
    sources, (in_ref, out_ref, stage, sems) = refs[:-4], refs[-4:]
    joined = len(sources) in (4, 6) and sources[3].shape[1] == sum(SPLIT)
    half = stage.shape[2] // 2
    copies = []
    for side in range(2):
        expert = ids_ref[0] if side == 0 else 1 - ids_ref[0]
        for index in range(3):
            rows = SPLIT[index]
            for spot in range(4):
                slot = (side * 3 + index) * 4 + spot
                place = jnp.bitwise_xor(base + spot, ids_ref[index + 1])
                columns = pl.ds(pl.multiple_of(place * half, half), half)
                if side == 1 and joined:
                    at = sum(SPLIT[:index])
                    piece = sources[3][spot, at : at + rows]
                else:
                    piece = sources[3 * side + index][spot]
                stage[slot, :rows] = piece.astype(F32)
                for start, count, output, at in part_regions(index, half):
                    if output == 1:
                        copies.append(
                            pltpu.make_async_copy(
                                stage.at[slot, pl.ds(start, count)],
                                out_ref.at[expert, pl.ds(place * half + at, count)],
                                sems.at[len(copies)],
                            )
                        )
                        copies[-1].start()
                        continue
                    for part in range(2):
                        copies.append(
                            pltpu.make_async_copy(
                                stage.at[slot, pl.ds(start, count), pl.ds(part * half, half)],
                                in_ref.at[expert, pl.ds(part * half + at, count), columns],
                                sems.at[len(copies)],
                            )
                        )
                        copies[-1].start()
    for copy in copies:
        copy.wait()


def run_open_experts(ids, base, args, shape_in, shape_out, begun=()):
    vmem = pl.BlockSpec(memory_space=pltpu.VMEM)
    hbm = pl.BlockSpec(memory_space=pl.ANY)
    copies = 8 * sum(1 if region[2] else 2 for i in range(3) for region in part_regions(i, 256))
    return call(
        functools.partial(open_experts, base),
        "open_experts",
        (),
        [pl.BlockSpec(memory_space=pltpu.SMEM)] + [vmem] * len(args) + [hbm] * len(begun),
        [hbm] * 2,
        [jax.ShapeDtypeStruct(shape_in, F32), jax.ShapeDtypeStruct(shape_out, F32)],
        1e10 if base else 1,
        1e7 if base else 1,
        scratch_shapes=[
            pltpu.VMEM((24, max(SPLIT), shape_out[2]), F32),
            pltpu.SemaphoreType.DMA((copies,)),
        ],
        input_output_aliases={1 + len(args) + i: i for i in range(len(begun))},
    )(ids, *args, *begun)


def tie(*values):
    return lax.optimization_barrier(values)


def tie_groups(*groups):
    values = iter(tie(*[value for group in groups for value in group]))
    return [[next(values) for _ in group] for group in groups]


def build(mesh):
    n_head, n_batch = mesh.shape["head"], mesh.shape["batch"]
    head_bits = [("head", 1 << i) for i in range(n_head.bit_length() - 1)]
    batch_bits = [("batch", 1 << i) for i in range(n_batch.bit_length() - 1)]
    pair, across = head_bits
    first_batch, second_batch, *last_batch = batch_bits
    orders = [
        (across, first_batch, second_batch),
        (first_batch, second_batch, across),
        (second_batch, across, first_batch),
    ]

    def swap(value, step):
        axis, bit = step
        return lax.ppermute(value, axis, [(i, i ^ bit) for i in range(mesh.shape[axis])])

    def bit_of(step):
        axis, bit = step
        return (lax.axis_index(axis) // bit) % 2

    def number(steps):
        return functools.reduce(lambda value, step: 2 * value + bit_of(step), steps, 0)

    def add(kept, got):
        return (kept.astype(F32) + got.astype(F32)).astype(BF)

    def local(
        inputs,
        attn_gain,
        query_weight,
        key_weight,
        value_weight,
        output_weight,
        ffn_gain,
        controller,
        expert_in,
        expert_out,
        group_ids,
        live_mask,
        cotangent,
    ):
        tokens_here, width = inputs.shape
        sequences = tokens_here // LENGTH
        ids = jnp.stack(
            [bit_of(pair)]
            + [number(order) for order in orders]
            + [number((first_batch, second_batch))]
        ).astype(jnp.int32)
        w0 = run_pack(query_weight, key_weight, value_weight, output_weight)
        w2 = swap(w0, across)
        w1 = swap(w0, pair)
        normed, *saved_a = run_forward_first(inputs, attn_gain[None], [w0, w1])
        w2, normed = tie(w2, normed)
        w3 = swap(w2, pair)
        weights = [w0, w1, w2, w3]
        control = controller.T
        group, live = group_ids[None], live_mask[None]
        *saved_b, middle, normed2, columns, keep, send = run_forward_last(
            ids,
            normed,
            inputs,
            saved_a[-1],
            ffn_gain[None],
            control,
            cotangent,
            group,
            live,
            weights,
        )
        *parts, home, away = run_experts(ids, keep, swap(send, pair), expert_in, expert_out)
        home_got = swap(away, pair)
        kept, sent = parts[:3], parts[3:]
        got = [swap(part, order[0]) for part, order in zip(sent, orders)]

        def send_half(blocks, step):
            half = blocks.shape[0] // 2
            return blocks[:half], swap(blocks[half:], step)

        layer_out, middle_low, small = run_spread(
            ids,
            middle,
            normed2,
            cotangent,
            columns,
            group,
            live,
            home,
            home_got,
            ffn_gain[None],
            control,
        )

        half = sequences // 2

        def next_stage(kept, got, low, mark, stage):
            *got, mark = tie(*got, mark)
            blocks = [add(a, b) for a, b in zip(kept, got)]
            if stage < 3:
                kept = [block[: block.shape[0] // 2] for block in blocks]
                sent = [block[block.shape[0] // 2 :] for block in blocks]
            else:
                kept = sent = blocks
            *sent, low = tie(*sent, low)
            steps = [order[stage] if stage < 3 else last_batch[stage - 3] for order in orders]
            return kept, [swap(block, step) for block, step in zip(sent, steps)], low, mark

        low = middle_low
        early, late = range(half), range(half, sequences)
        first_items = [(1, i) for i in early]
        second_items = [(1, i) for i in late] + [(0, i) for i in early]
        third_items = [(0, i) for i in late]
        far_slots = weights[2:]
        flat, sums = run_backward(saved_b, low, far_slots, normed, first_items)
        kept, got, low, sums = next_stage(kept, got, low, sums, 1)
        flat, sums = run_backward(
            saved_b, low, far_slots, normed, second_items, first_items, (flat, sums)
        )
        kept, got, low, sums = next_stage(kept, got, low, sums, 2)
        third_got = swap(sums[1].astype(BF), pair)
        flat, sums = run_backward(
            saved_b, low, far_slots, normed, third_items, first_items + second_items, (flat, sums)
        )
        kept, got, low, sums = next_stage(kept, got, low, sums, 3)
        for stage in range(4, 3 + len(last_batch)):
            kept, got, low, sums = next_stage(kept, got, low, sums, stage)
        second = (sums[0] + third_got.astype(F32)).astype(BF)
        second, low = tie(second, low)
        second_got = swap(second, across)
        near_items = [(slot, i) for slot in (1, 0) for i in range(sequences)]
        flat_near, sums_near = run_backward(saved_a, low, weights[:2], normed, near_items)
        *got, second_got, sums_near, low = tie(*got, second_got, sums_near, low)

        def widen(blocks, stage):
            return [swap(block, order[stage]) for block, order in zip(blocks, orders)]

        def join(blocks, got):
            return [jnp.concatenate(both, axis=0) for both in zip(blocks, got)]

        def split(value):
            half = value.shape[0] // 2
            return value[:half], value[half:]

        def all_of(value, steps):
            (axis, one), (_, two) = steps
            return [swap(value, (axis, bits)) for bits in (one, two, one | two)]

        first_got = swap(sums_near[1].astype(BF), pair)
        blocks = [add(a, b) for a, b in zip(kept, got)]
        *blocks, low = tie(*blocks, low)
        got = widen(blocks, 2)
        own_kept, own_sent, small = run_join(
            ids, sums_near, second_got, first_got, w0, attn_gain[None], small
        )
        small, own_sent = tie(small + swap(small, pair), own_sent)
        own_got = swap(own_sent, first_batch)
        small_got = swap(small, across)
        *got, small_got, low = tie(*got, small_got, low)

        blocks = join(blocks, got)
        got = widen(blocks, 1)
        own_kept, own_sent = split(add(own_kept, own_got))
        small, own_sent = tie(small + small_got, own_sent)
        own_got = swap(own_sent, second_batch)
        small_got = swap(small, second_batch)
        *got, own_got, small_got, low = tie(*got, own_got, small_got, low)

        blocks = join(blocks, got)
        blocks_other = swap(jnp.concatenate(blocks, axis=1), pair)
        far = widen(blocks, 0)
        begun = run_open_experts(
            ids, 0, [*blocks, blocks_other], expert_in.shape, expert_out.shape
        )
        own = add(own_kept, own_got)
        small = small + small_got
        for step in last_batch[:-1]:
            own = add(own, swap(own, step))
            small = small + swap(small, step)
        own_got = swap(own, last_batch[-1])
        small_got = swap(small, first_batch)
        input_grad = run_input(inputs, attn_gain[None], low, [flat_near, flat], weights)
        far, (own_got, small_got, input_grad, *begun) = tie_groups(
            far, (own_got, small_got, input_grad, *begun)
        )

        far_other = [swap(block, pair) for block in far]
        own = add(own, own_got)
        own_got = all_of(own, (second_batch, first_batch))
        small = small + small_got
        small_got = swap(small, last_batch[-1])
        expert_grads = run_open_experts(
            ids, 4, [*far, *far_other], expert_in.shape, expert_out.shape, begun
        )
        own_got, (small_got, expert_in_grad, expert_out_grad) = tie_groups(
            own_got, (small_got, *expert_grads)
        )
        query_grad, key_grad, value_grad, output_grad, attn_grad, ffn_grad, control_grad = run_open(
            ids, small, small_got, own, own_got
        )
        return (
            layer_out,
            input_grad,
            attn_grad[0],
            query_grad,
            key_grad,
            value_grad,
            output_grad,
            ffn_grad[0],
            control_grad.T,
            expert_in_grad,
            expert_out_grad,
        )

    return local


def solution(mesh):
    in_specs = (
        P(("batch", "head"), None),
        P(),
        P(None, "head"),
        P(None, "head"),
        P(None, "head"),
        P("head", None),
        P(),
        P(),
        P(),
        P(),
        P(("batch", "head")),
        P(("batch", "head")),
        P(("batch", "head"), None),
    )
    out_specs = (
        P(("batch", "head"), None),
        P(("batch", "head"), None),
        P(),
        P(None, "head"),
        P(None, "head"),
        P(None, "head"),
        P("head", None),
        P(),
        P(),
        P(),
        P(),
    )
    return jax.shard_map(
        build(mesh), mesh=mesh, in_specs=in_specs, out_specs=out_specs, check_vma=False
    )
```
